32 devices in a mesh: dp: 4 (over y, x), fsdp: 8 (over z, core).
Axes of the slice: x: 2, y: 2, z: 4, core: 2. Of those that a mesh axis runs over, the one named last changes fastest.
Arguments:
- tokens: bfloat16 [96, 608, 768], P(('dp', 'fsdp')), may hold values from -6 to 6
- cotangent: bfloat16 [96, 608, 768], P(('dp', 'fsdp')), may hold values from -6 to 6
- group: int32 [96], P(('dp', 'fsdp')), may hold values from 0 to 1
- text_len: int32 [96], P(('dp', 'fsdp')), may hold values from 1 to 32
- qkv_w: bfloat16 [1769472], P(('dp', 'fsdp')), may hold values from -2 to 2
- out_w: bfloat16 [589824], P(('dp', 'fsdp')), may hold values from -0.21875 to 0.21875
- mlp_in: bfloat16 [2359296], P(('dp', 'fsdp')), may hold values from -0.21875 to 0.21875
- mlp_out: bfloat16 [2359296], P(('dp', 'fsdp')), may hold values from -0.21875 to 0.21875
- gains: bfloat16 [1536], P(('dp', 'fsdp')), may hold values from 0.5 to 1.5
- biases: bfloat16 [7680], P(('dp', 'fsdp')), may hold values from -0.59765625 to 0.59765625
Outputs:
- block_out: bfloat16 [96, 608, 768], P(('dp', 'fsdp'))
- input_grad: bfloat16 [96, 608, 768], P(('dp', 'fsdp'))
- qkv_grad: float32 [1769472], P(('dp', 'fsdp'))
- out_grad: float32 [589824], P(('dp', 'fsdp'))
- mlp_in_grad: float32 [2359296], P(('dp', 'fsdp'))
- mlp_out_grad: float32 [2359296], P(('dp', 'fsdp'))
- gains_grad: float32 [1536], P(('dp', 'fsdp'))
- biases_grad: float32 [7680], P(('dp', 'fsdp'))
The draws below stay inside these ranges and needn't reach their ends.
All inputs are finite; a program needn't handle non-finite values.
Results may differ from the reference program's by a relative error of at most 0.014.
Values may be sent and summed in bfloat16 or wider, within the bound.
No kernel may reach another device: no remote copies, remote signals or barrier semaphores. Data moves between devices by JAX's collectives and lax.ppermute only.
A program may use at most 256 MiB of HBM per device.

```python
import math
import jax
import jax.numpy as jnp
from jax import lax

D = 768
HEADS = 12
FF = 3072
PATCH_SMALL = 196
PATCH_LARGE = 576
TEXT = 32
SEQ = 608
ITEMS = 96


def draw_qkv_w(key, part):
    key = jax.random.fold_in(key, 11)
    entries = jax.random.normal(key, (3 * D * D,), jnp.float32) * D ** (-0.5)
    column = jnp.arange(3 * D * D, dtype=jnp.int32) % (3 * D)
    widened = jnp.where(column >= 2 * D, entries * 8.0, entries)
    return jnp.clip(widened, -2.0, 2.0).astype(jnp.bfloat16)


def set_ends(values, stream_key, smallest, high):
    longest = values.shape.index(max(values.shape))
    spots = []
    for shift in (0, 1):
        where = [jax.random.randint(jax.random.fold_in(stream_key, axis), (), 0, length) for axis, length in enumerate(values.shape)]
        where[longest] = (where[longest] + shift) % values.shape[longest]
        spots.append(tuple(where))
    return values.at[spots[0]].set(smallest).at[spots[1]].set(high)


def level_of(rng, shape, cuts, least, largest):
    factor_of = 1.0
    for dim, parts in cuts:
        draws = jax.random.uniform(jax.random.fold_in(jax.random.fold_in(rng, 6), dim), (parts,), jnp.float32, least / len(cuts), largest / len(cuts))
        factor_of = factor_of * jnp.repeat(jnp.exp(draws), shape[dim] // parts).reshape((-1,) + (1,) * (len(shape) - 1 - dim))
    return factor_of


def gaussian(key, shape, scale, most, cuts=(), kind=jnp.bfloat16):
    level = level_of(key, shape, cuts, -0.22, 0.18) if cuts else 1.0
    array = jax.random.normal(key, shape, jnp.float32) * scale * level
    return jnp.minimum(jnp.maximum(array, -most), most).astype(kind)


def setup_inputs(seed: int = 0) -> dict:
    key_list = jax.random.split(jax.random.key(seed), 11)
    return {
        "tokens": gaussian(key_list[0], (ITEMS, SEQ, D), 1.0, 6.0, ((0, 32),)),
        "cotangent": gaussian(key_list[1], (ITEMS, SEQ, D), 1.0, 6.0, ((0, 32),)),
        "group": set_ends(jax.random.randint(key_list[2], (ITEMS,), 0, 2), jax.random.fold_in(key_list[2], 1), 0, 1).astype(jnp.int32),
        "text_len": set_ends(jax.random.randint(key_list[3], (ITEMS,), 1, TEXT + 1), jax.random.fold_in(key_list[3], 1), 1, TEXT).astype(jnp.int32),
        "qkv_w": draw_qkv_w(jax.random.fold_in(key_list[10], 71), 0),
        "out_w": gaussian(key_list[5], (D * D,), D ** -0.5, 0.21875, ((0, 32),)),
        "mlp_in": gaussian(key_list[6], (D * FF,), D ** -0.5, 0.21875, ((0, 32),)),
        "mlp_out": gaussian(key_list[7], (FF * D,), (FF // 4) ** -0.5, 0.21875, ((0, 32),)),
        "gains": jnp.clip(1.0 + 0.1 * jax.random.normal(key_list[8], (2 * D,), jnp.float32), 0.5, 1.5).astype(jnp.bfloat16),
        "biases": gaussian(key_list[9], (6 * D + FF,), 0.1, 0.59765625, ((0, 32),)),
    }


@jax.custom_vjp
def low(v):
    return lax.optimization_barrier(v.astype(jnp.bfloat16)).astype(jnp.float32)

@jax.custom_vjp
def low_back(v):
    return v

def low_keep(v):
    return (low(v), None)

def low_pass(kept, grad):
    return (grad,)

def back_keep(v):
    return (v, None)

def back_low(kept, grad):
    return (low(grad),)
low.defvjp(low_keep, low_pass)
low_back.defvjp(back_keep, back_low)
highest = lax.Precision.HIGHEST

def layer_norm(values, gain, shift):
    center = values - lax.optimization_barrier(jnp.mean(values, -1, keepdims=True))
    spread = lax.optimization_barrier(jnp.mean(center * center, -1, keepdims=True))
    return center * lax.rsqrt(spread + 1e-05) * gain + shift

def split_small(gains, biases):
    width = gains.shape[0] // 2
    return (gains[:width], gains[width:], biases[:width], biases[width:2 * width], biases[2 * width:3 * width], biases[3 * width:4 * width], biases[4 * width:5 * width], biases[5 * width:6 * width], biases[6 * width:])

def item_forward(params, tokens, row_keep):
    w_qkv, w_out, w_up, w_down, gains, biases = params
    gain_one, gain_two, bias_query, bias_value, bias_output, shift_one, shift_two, bias_down, bias_up = split_small(gains, biases)
    seq_len, width = tokens.shape
    head_size = width // HEADS
    scaling = 1.0 / math.sqrt(head_size)
    normed = low(layer_norm(tokens, gain_one, shift_one))
    joined = jnp.dot(normed, w_qkv, precision=highest) + jnp.concatenate([bias_query, jnp.zeros_like(bias_query), bias_value])
    joined = low_back(low(joined))
    query = joined[:, :width].reshape(seq_len, HEADS, head_size)
    key_part = joined[:, width:2 * width].reshape(seq_len, HEADS, head_size)
    value_part = joined[:, 2 * width:].reshape(seq_len, HEADS, head_size)
    scores = jnp.einsum('qhe,khe->hqk', query, key_part, precision=highest) * scaling
    scores = low_back(scores)
    scores = jnp.where(row_keep[None, None, :] > 0, scores, -1e+30)
    weights = low(jax.nn.softmax(scores, axis=-1))
    mixture = jnp.einsum('hqk,khe->qhe', weights, value_part, precision=highest).reshape(seq_len, width)
    mixture = low_back(low(mixture))
    branch = low_back(jnp.dot(mixture, w_out, precision=highest) + bias_output)
    middle = tokens + branch
    normed_two = low(layer_norm(middle, gain_two, shift_two))
    hidden = low_back(jnp.dot(normed_two, w_up, precision=highest) + bias_up)
    active = low(jax.nn.gelu(hidden, approximate=False))
    result = low_back(jnp.dot(active, w_down, precision=highest) + bias_down)
    return (middle + result) * row_keep[:, None]

def reference(tokens, cotangent, group, text_len, qkv_w, out_w, mlp_in, mlp_out, gains, biases):
    item_count, seq_len, width = tokens.shape
    valid_len = PATCH_SMALL + (PATCH_LARGE - PATCH_SMALL) * group + text_len
    row_keep = (jnp.arange(seq_len, dtype=jnp.int32)[None, :] < valid_len[:, None]).astype(jnp.float32)
    params = (qkv_w.astype(jnp.float32).reshape(width, 3 * width), out_w.astype(jnp.float32).reshape(width, width), mlp_in.astype(jnp.float32).reshape(width, FF), mlp_out.astype(jnp.float32).reshape(FF, width), gains.astype(jnp.float32), biases.astype(jnp.float32))
    stepper = jax.checkpoint(item_forward)

    def summed(weights, inputs):
        return lax.map(lambda item_pair: stepper(weights, item_pair[0], item_pair[1]), (inputs, row_keep))
    outputs, pull_back = jax.vjp(summed, params, tokens.astype(jnp.float32))
    gradients, input_grad = pull_back(cotangent.astype(jnp.float32))
    return (outputs.astype(jnp.bfloat16), input_grad.astype(jnp.bfloat16), gradients[0].reshape(-1), gradients[1].reshape(-1), gradients[2].reshape(-1), gradients[3].reshape(-1), gradients[4], gradients[5])
```

```python
import functools
import math

import jax
import jax.numpy as jnp
from jax import lax
from jax.experimental import pallas as pl
from jax.experimental.pallas import tpu as pltpu
from jax.sharding import PartitionSpec as P

HEADS = 12
PATCH_SMALL = 196
PATCH_LARGE = 576
AXES = ("dp", "fsdp")
bf16 = jnp.bfloat16
f32 = jnp.float32
NN = (((1,), (0,)), ((), ()))
NT = (((1,), (1,)), ((), ()))
TN = (((0,), (0,)), ((), ()))
VMEM_LIMIT = 60 * 2**20
LOG2E = 1.4426950408889634


def dot(a, b, dims):
    return lax.dot_general(a, b, dims, preferred_element_type=f32)


def params(n):
    return pltpu.CompilerParams(
        vmem_limit_bytes=VMEM_LIMIT, dimension_semantics=("arbitrary",) * n
    )


def cost(*_):
    return pl.CostEstimate(flops=1, bytes_accessed=1, transcendentals=0)


def once(shape):
    return pl.BlockSpec(
        shape, lambda *_: (0,) * len(shape), pipeline_mode=pl.Buffered(buffer_count=1)
    )


def shape_of(shape, dtype):
    return jax.ShapeDtypeStruct(shape, dtype)


class Flights:
    def __init__(self):
        self.waiting = []
        self.flying = []

    def add(self, steps, lengths):
        job = {"steps": steps, "lengths": list(lengths), "result": None}
        self.advance(job, None)
        return job

    def advance(self, job, came):
        try:
            sends = job["steps"].send(came) if came is not None else next(job["steps"])
        except StopIteration as stop:
            job["result"] = stop.value
            return
        length = job["lengths"].pop(0) if job["lengths"] else 1
        self.waiting.append((job, sends, length))

    def depart(self):
        for job, sends, length in self.waiting:
            came = [lax.ppermute(array, AXES, pairs) for array, pairs in sends]
            self.flying.append([job, came, length])
        self.waiting = []

    def run(self, kernel, operand, *others):
        arrays = [array for _, sends, _ in self.waiting for array, _ in sends]
        if arrays:
            operand, arrays = lax.optimization_barrier((operand, arrays))
            left = iter(arrays)
            self.waiting = [
                (job, [(next(left), pairs) for _, pairs in sends], length)
                for job, sends, length in self.waiting
            ]
        self.depart()
        out = kernel(operand, *others)
        for flight in self.flying:
            flight[2] -= 1
        landed = [flight for flight in self.flying if flight[2] <= 0]
        self.flying = [flight for flight in self.flying if flight[2] > 0]
        if landed:
            out, came = lax.optimization_barrier((out, [flight[1] for flight in landed]))
            for flight, got in zip(landed, came):
                self.advance(flight[0], got)
        return out

    def behind(self, value):
        value, _ = lax.optimization_barrier((value, [array for _, sends, _ in self.waiting for array, _ in sends]))
        return value

    def finish(self, turns=1 << 30):
        while (self.waiting or self.flying) and turns > 0:
            turns -= 1
            self.depart()
            landed, self.flying = self.flying, []
            cames = lax.optimization_barrier([flight[1] for flight in landed])
            for flight, came in zip(landed, cames):
                self.advance(flight[0], came)


def bit_groups(mesh):
    inner = int(math.log2(mesh.shape["fsdp"]))
    outer = int(math.log2(mesh.shape["dp"]))
    rest = [list(range(b, min(b + 2, inner))) for b in range(1, inner, 2)]
    return [0], list(range(inner, inner + outer)), rest


def position(me, bits):
    spot = 0
    for place, bit in enumerate(bits):
        spot = spot + ((me >> bit) & 1) * (1 << place)
    return spot


def partners(count, bits):
    swaps = []
    for step in range(1, 1 << len(bits)):
        mask = 0
        for place, bit in enumerate(bits):
            if (step >> place) & 1:
                mask |= 1 << bit
        swaps.append((step, [(i, i ^ mask) for i in range(count)]))
    return swaps


def gather_steps(shard, mesh):
    count = mesh.size
    core, outer, rest = bit_groups(mesh)
    me = lax.axis_index(AXES)
    rows, columns = shard.shape
    held = shard
    rest_size = 1
    for bits in rest:
        size = 1 << len(bits)
        spot = position(me, bits)
        swaps = partners(count, bits)
        block = held.reshape(1, rest_size, rows, columns)
        came = yield [(block, pairs) for _, pairs in swaps]
        whole = jnp.zeros((size, rest_size, rows, columns), shard.dtype)
        for (step, _), got in zip([(0, None)] + swaps, [block] + came):
            whole = lax.dynamic_update_slice(whole, got, (spot ^ step, 0, 0, 0))
        rest_size *= size
        held = whole
    size = 1 << len(outer)
    spot = position(me, outer)
    swaps = partners(count, outer)
    block = held.reshape(1, rest_size, 1, rows, columns)
    came = yield [(block, pairs) for _, pairs in swaps]
    held = jnp.zeros((size, rest_size, 1, rows, columns), shard.dtype)
    for (step, _), got in zip([(0, None)] + swaps, [block] + came):
        held = lax.dynamic_update_slice(held, got, (spot ^ step, 0, 0, 0, 0))
    spot = position(me, core)
    (got,) = yield [(held, partners(count, core)[0][1])]
    whole = jnp.zeros((size, rest_size, 2, rows, columns), shard.dtype)
    whole = lax.dynamic_update_slice(whole, held, (0, 0, spot, 0, 0))
    whole = lax.dynamic_update_slice(whole, got, (0, 0, spot ^ 1, 0, 0))
    return whole.reshape(count * rows, columns)


def pick(array, axis, index):
    return lax.dynamic_slice_in_dim(array, index, 1, axis)


def total(terms, axis, index, kind):
    return sum(pick(term, axis, index).astype(f32) for term in terms).astype(kind)


def sum_steps(parts, mesh, kind):
    count = mesh.size
    core, outer, rest = bit_groups(mesh)
    me = lax.axis_index(AXES)
    rows, columns = parts.shape[0] // count, parts.shape[1]
    rest_size = mesh.shape["fsdp"] // 2
    held = parts.reshape(mesh.shape["dp"], rest_size, 2, rows, columns)
    spot = position(me, core)
    (got,) = yield [(pick(held, 2, spot ^ 1).astype(kind), partners(count, core)[0][1])]
    terms = [pick(held, 2, spot), got]
    split = 2 if len(outer) == 2 and columns % 256 == 0 else 1
    width = columns // split
    shape = (2,) * len(outer) + (rest_size, 1, rows, width)
    pieces = []
    for piece in range(split):
        own = [term[..., piece * width : (piece + 1) * width].reshape(shape) for term in terms]
        order = list(range(len(outer)))
        pieces.append((own, order if piece == 0 else order[::-1]))
    for turn in range(len(outer)):
        sends = []
        for own, order in pieces:
            axis = order[turn]
            bit = outer[len(outer) - 1 - axis]
            mine = position(me, [bit])
            sends.append((total(own, axis, mine ^ 1, kind), partners(count, [bit])[0][1]))
        came = yield sends
        pieces = [
            ([pick(term, order[turn], position(me, [outer[len(outer) - 1 - order[turn]]])) for term in own] + [got], order)
            for (own, order), got in zip(pieces, came)
        ]
    left = rest_size
    pieces = [[term.reshape(rest_size, rows, width) for term in own] for own, _ in pieces]
    for bits in reversed(rest):
        size = 1 << len(bits)
        left //= size
        pieces = [[term.reshape(size, left, rows, width) for term in own] for own in pieces]
        spot = position(me, bits)
        swaps = partners(count, bits)
        sends = [
            (jnp.concatenate([total(own, 0, spot ^ step, kind) for own in pieces], -1), pairs)
            for step, pairs in swaps
        ]
        came = yield sends
        pieces = [
            [pick(term, 0, spot) for term in own]
            + [got[..., place * width : (place + 1) * width] for got in came]
            for place, own in enumerate(pieces)
        ]
    sums = [sum(term.astype(f32) for term in own).reshape(rows, width) for own in pieces]
    return jnp.concatenate(sums, -1)


def plane_sum_kernel(where, *refs, parts):
    keeps, cames, outs = refs[:parts], refs[parts : 2 * parts], refs[2 * parts :]
    for step, out in enumerate(outs):
        place = where[1] ^ step
        start = 0
        for keep, came in zip(keeps, cames):
            lanes = slice(start, start + keep.shape[-1])
            start += keep.shape[-1]
            out[:, lanes] = (keep[place].astype(f32) + came[place].astype(f32)).astype(out.dtype)


def plane_sum(where, keeps, cames, size):
    blocks, rows, _ = keeps[0].shape
    left = blocks // size
    columns = sum(keep.shape[2] for keep in keeps)
    arrays = [array.reshape(size, left, rows, array.shape[2]) for array in (*keeps, *cames)]
    part = pl.BlockSpec((None, rows, columns), lambda j, where: (j, 0, 0))
    return pl.pallas_call(
        functools.partial(plane_sum_kernel, parts=len(keeps)),
        grid_spec=pltpu.PrefetchScalarGridSpec(
            num_scalar_prefetch=1,
            grid=(left,),
            in_specs=[
                pl.BlockSpec((size, None, rows, array.shape[3]), lambda j, where: (0, j, 0, 0))
                for array in arrays
            ],
            out_specs=[part] * size,
        ),
        out_shape=[shape_of((left, rows, columns), bf16)] * size,
        compiler_params=params(1),
        cost_estimate=cost(blocks * rows * columns, blocks * rows * columns * 6),
        name="plane_sum",
    )(where, *arrays)


def line_sum_kernel(where, *refs, size):
    terms, outs = refs[:size], refs[size:]
    for step, out in enumerate(outs):
        place = where[2] ^ step
        out[...] = sum(term[place].astype(f32) for term in terms).astype(out.dtype)


def line_sum(where, terms):
    size, rows, columns = terms[0].shape
    return pl.pallas_call(
        functools.partial(line_sum_kernel, size=len(terms)),
        grid_spec=pltpu.PrefetchScalarGridSpec(
            num_scalar_prefetch=1,
            grid=(1,),
            in_specs=[once((size, rows, columns))] * len(terms),
            out_specs=[once((rows, columns))] * size,
        ),
        out_shape=[shape_of((rows, columns), f32)] + [shape_of((rows, columns), bf16)] * (size - 1),
        compiler_params=params(1),
        cost_estimate=cost(size * size * rows * columns, size * rows * columns * 10),
        name="line_sum",
    )(where, *terms)


def fast_sum_steps(keeps, sends, where, mesh):
    count = mesh.size
    core, outer, rest = bit_groups(mesh)
    cames = yield [(send, partners(count, core)[0][1]) for send in sends]
    own, *sends = plane_sum(where, keeps, cames, 1 << len(outer))
    came = yield [(array, pairs) for array, (_, pairs) in zip(sends, partners(count, outer))]
    own, *sends = line_sum(where, [own, *came])
    came = yield [(array, pairs) for array, (_, pairs) in zip(sends, partners(count, rest[0]))]
    return own + sum(array.astype(f32) for array in came)


def small_sum_steps(parts, mesh):
    count = mesh.size
    core, outer, rest = bit_groups(mesh)
    groups = [core, outer, *reversed(rest)]
    order = [outer, *reversed(rest), core]
    me = lax.axis_index(AXES)
    columns = parts.shape[1]
    held = parts.reshape([1 << len(bits) for bits in order] + [columns])
    for bits in groups:
        axis = order.index(bits)
        spot = position(me, bits)
        swaps = partners(count, bits)
        came = yield [(pick(held, axis, spot ^ step), pairs) for step, pairs in swaps]
        held = pick(held, axis, spot) + sum(came)
    return held.reshape(columns)


def cut_by_core(mesh):
    _, outer, rest = bit_groups(mesh)
    return len(outer) == 2 and len(rest) == 1 and len(rest[0]) == 2


def store_cut(core, outs, lanes, value, rows):
    if len(outs) == 1:
        outs[0][:, lanes] = value.astype(bf16)
        return
    keep, send = outs
    for parity in range(2):
        @pl.when(core == parity)
        def _():
            for device in range(value.shape[0] // rows):
                out = keep if device % 2 == parity else send
                out[device // 2, :, lanes] = value[device * rows : (device + 1) * rows, :].astype(bf16)


def cut_shapes(width, columns, chunk, index, rows):
    if not rows:
        spec = pl.BlockSpec((width, chunk), lambda j, *_: (0, index(j)))
        return [spec], [shape_of((width, columns), bf16)]
    blocks = width // rows // 2
    spec = pl.BlockSpec((blocks, rows, chunk), lambda j, *_: (0, 0, index(j)))
    return [spec] * 2, [shape_of((blocks, rows, columns), bf16)] * 2


def normalize(values):
    center = values - jnp.mean(values, -1, keepdims=True)
    scale = lax.rsqrt(jnp.mean(center * center, -1, keepdims=True) + 1e-05)
    return center * scale, scale


def norm_back(grad, gain, unit, scale):
    inner = grad * gain
    return scale * (
        inner
        - jnp.mean(inner, -1, keepdims=True)
        - unit * jnp.mean(inner * unit, -1, keepdims=True)
    )


def gelu_parts(u):
    phi = 0.5 + 0.5 * lax.erf(u * 0.7071067811865476)
    slope = phi + u * (0.3989422804014327 * jnp.exp2((u * u) * (-0.5 * LOG2E)))
    return u * phi, slope


def column_sum(values):
    return jnp.sum(values, 0, keepdims=True)


def accumulate(ref, value, first):
    @pl.when(first)
    def _():
        ref[...] = value

    @pl.when(jnp.logical_not(first))
    def _():
        ref[...] += value


def first_qkv_kernel(tokens, gain, shift, weight, bias, normed, joined):
    unit, _ = normalize(tokens[...].astype(f32))
    low = (unit * gain[...] + shift[...]).astype(bf16)
    normed[...] = low
    joined[...] = (dot(low, weight[...], NN) + bias[...]).astype(bf16)


def first_qkv(tokens, gain, shift, weight, bias, seq):
    rows, width = tokens.shape
    span = bias.shape[1]
    row = lambda w: pl.BlockSpec((seq, w), lambda i: (i, 0))
    return pl.pallas_call(
        first_qkv_kernel,
        grid=(rows // seq,),
        in_specs=[row(width), once((1, width)), once((1, width)), once((width, span)), once((1, span))],
        out_specs=[row(width), row(span)],
        out_shape=[shape_of((rows, width), bf16), shape_of((rows, span), bf16)],
        compiler_params=params(1),
        cost_estimate=cost(2 * rows * width * span, rows * (2 * width + span) * 2),
        name="first_qkv",
    )(tokens, gain, shift, weight, bias)


def next_qkv_kernel(normed, weight, bias, joined):
    span = bias.shape[1]
    joined[...] = (dot(normed[...], weight[:, :span], NN) + bias[...]).astype(bf16)


def next_qkv(normed, weight, bias, seq):
    rows, width = normed.shape
    span = bias.shape[1]
    return pl.pallas_call(
        next_qkv_kernel,
        grid=(rows // seq,),
        in_specs=[
            pl.BlockSpec((seq, width), lambda i: (i, 0)),
            once(weight.shape),
            once((1, span)),
        ],
        out_specs=pl.BlockSpec((seq, span), lambda i: (i, 0)),
        out_shape=shape_of((rows, span), bf16),
        compiler_params=params(1),
        cost_estimate=cost(2 * rows * width * span, rows * (width + span) * 2),
        name="next_qkv",
    )(normed, weight, bias)


def two_heads(block, padded):
    seq = block.shape[0]
    first = lax.broadcasted_iota(jnp.int32, block.shape, 1) < 64
    zero = jnp.zeros_like(block)
    pad = jnp.zeros((padded - seq, 128), block.dtype)
    return jnp.concatenate(
        [jnp.where(first, block, zero), pad, jnp.where(first, zero, block), pad], 0
    )


def attend_kernel(valid, joined, mixed, raised_out, inverse, *, tile, padded):
    seq = joined.shape[0]
    length = valid[pl.program_id(0)]
    keys = two_heads(joined[:, 128:256], padded)
    values = two_heads(joined[:, 256:], padded)
    row = lax.broadcasted_iota(jnp.int32, (2 * padded, 128), 0)
    lane = lax.broadcasted_iota(jnp.int32, (2 * padded, 128), 1)
    ones = jnp.where((row < padded) == (lane < 64), 1.0, 0.0).astype(bf16)
    values = jnp.concatenate([values, ones], 1)
    column = lax.broadcasted_iota(jnp.int32, (1, padded), 1)
    mask = jnp.where(column < length, 0.0, -1e30).astype(f32)
    for start in range(0, seq, tile):
        scores = dot(joined[start : start + tile, :128], keys, NT)
        halves = []
        for head in range(2):
            part = scores[:, head * padded : (head + 1) * padded] * (0.125 * LOG2E) + mask
            halves.append(jnp.exp2(part - jnp.max(part, 1, keepdims=True)).astype(bf16))
        raised = jnp.concatenate(halves, 1)
        raised_out[start : start + tile, :] = raised
        both = dot(raised, values, NN)
        scale = 1.0 / both[:, 128:]
        inverse[start : start + tile, :] = scale
        mixed[start : start + tile, :] = (both[:, :128] * scale).astype(bf16)


def attend(joined, valid, seq):
    rows, span = joined.shape
    pairs = span // 384
    items = rows // seq
    padded = -(-seq // 128) * 128
    tile = seq // 2 if seq % 32 == 0 else seq
    block = lambda w: pl.BlockSpec((seq, w), lambda i, h, valid: (i, h))
    return pl.pallas_call(
        functools.partial(attend_kernel, tile=tile, padded=padded),
        grid_spec=pltpu.PrefetchScalarGridSpec(
            num_scalar_prefetch=1,
            grid=(items, pairs),
            in_specs=[block(384)],
            out_specs=[
                block(128),
                pl.BlockSpec((None, None, seq, 2 * padded), lambda i, h, valid: (i, h, 0, 0)),
                block(128),
            ],
        ),
        out_shape=[
            shape_of((rows, span // 3), bf16),
            shape_of((items, pairs, seq, 2 * padded), bf16),
            shape_of((rows, span // 3), f32),
        ],
        compiler_params=params(2),
        cost_estimate=cost(
            items * pairs * seq * padded * 2 * 2 * 3 * 128,
            items * pairs * seq * 2 * padded * 2,
            items * pairs * seq * 2 * padded,
        ),
        name="attend",
    )(valid, joined)


def attend_back_kernel(
    where, joined, mixed_grad, mixed, raised, normed, *rest, tile, extra, cut
):
    if extra:
        mixed_a, mixed_b, low_grad, joined_grad, column, *outs, held, total, total_out = rest
    else:
        joined_grad, column, *outs, held, total = rest
    item, pair = pl.program_id(0), pl.program_id(1)
    seq = joined.shape[0]
    span = total.shape[1]
    padded = raised.shape[1] // 2
    base = pl.multiple_of(pair * 384, 384)
    keys = two_heads(joined[:, 128:256], padded)
    values = two_heads(joined[:, 256:], padded)
    first = lax.broadcasted_iota(jnp.int32, (tile, 128), 1) < 64
    for start in range(0, seq, tile):
        rows = slice(start, start + tile)
        grad = mixed_grad[rows, :]
        prob_grad = dot(grad, values, NT)
        product = grad.astype(f32) * mixed[rows, :].astype(f32)
        zero = jnp.zeros_like(product)
        halves = []
        for head in range(2):
            own = jnp.where(first, product, zero) if head == 0 else jnp.where(first, zero, product)
            centre = jnp.sum(own, 1, keepdims=True)
            lanes = slice(head * padded, (head + 1) * padded)
            halves.append((raised[rows, lanes].astype(f32) * (prob_grad[:, lanes] - centre)).astype(bf16))
        score_grad = jnp.concatenate(halves, 1)
        held[rows, :] = score_grad
        joined_grad[rows, pl.ds(base, 128)] = (dot(score_grad, keys, NN) * 0.125).astype(bf16)

    def own_half(both):
        return jnp.concatenate([both[:64, :padded], both[64:, padded:]], 0).T[:seq]

    joined_grad[:, pl.ds(base + 128, 128)] = (
        own_half(dot(joined[:, :128].T, held[...], NN)) * 0.125
    ).astype(bf16)
    joined_grad[:, pl.ds(base + 256, 128)] = own_half(
        dot(mixed_grad[...].T, raised[...], NN)
    ).astype(bf16)

    @pl.when(pair == pl.num_programs(1) - 1)
    def _():
        value = joined_grad[...]
        accumulate(total, dot(normed[...], value, TN), item == 0)
        accumulate(column, column_sum(value.astype(f32)), item == 0)
        if extra:
            both = [dot(mixed_a[...], low_grad[...], TN), dot(mixed_b[...], low_grad[...], TN)]
            accumulate(total_out, jnp.concatenate(both, 0), item == 0)

        @pl.when(item == pl.num_programs(0) - 1)
        def _():
            store_cut(where[0], outs, slice(0, span), total[...], cut)
            if extra:
                store_cut(where[0], outs, slice(span, span + total_out.shape[1]), total_out[...], cut)


def attend_back(mixed_grad, where, joined, mixed, raised, normed, seq, part, cut, others=()):
    rows, span = joined.shape
    width = normed.shape[1]
    items, pairs, _, keys = raised.shape
    tile = seq // 2 if seq % 32 == 0 else seq
    block = lambda w, off=0: pl.BlockSpec((seq, w), lambda i, h, *_: (i, h + off))
    row = lambda w: pl.BlockSpec((seq, w), lambda i, h, *_: (i, 0))
    columns = span + (width if others else 0)
    specs, shapes = cut_shapes(width, columns, columns, lambda j: 0, cut)
    return pl.pallas_call(
        functools.partial(attend_back_kernel, tile=tile, extra=bool(others), cut=cut),
        grid_spec=pltpu.PrefetchScalarGridSpec(
            num_scalar_prefetch=1,
            grid=(items, pairs),
            in_specs=[
                block(384),
                block(128, part * pairs),
                block(128),
                pl.BlockSpec((None, None, seq, keys), lambda i, h, *_: (i, h, 0, 0)),
                row(width),
            ]
            + [row(array.shape[1]) for array in others],
            out_specs=[row(span), pl.BlockSpec((1, span), lambda i, h, *_: (0, 0))] + specs,
            scratch_shapes=[pltpu.VMEM((seq, keys), bf16), pltpu.VMEM((width, span), f32)]
            + ([pltpu.VMEM((width, width), f32)] if others else []),
        ),
        out_shape=[shape_of((rows, span), bf16), shape_of((1, span), f32)] + shapes,
        compiler_params=params(2),
        cost_estimate=cost(),
        name="attend_back",
    )(where, joined, mixed_grad, mixed, raised, normed, *others)


def middle_kernel(tokens, mixed_a, mixed_b, weight, bias, gain, shift, middle, normed):
    width = tokens.shape[1]
    half = width // 2
    value = tokens[...].astype(f32) + bias[...]
    value = value + (
        dot(mixed_a[...], weight[:half, -width:], NN) + dot(mixed_b[...], weight[half:, -width:], NN)
    )
    middle[...] = value
    unit, _ = normalize(value)
    normed[...] = (unit * gain[...] + shift[...]).astype(bf16)


def middle_of(tokens, mixed_a, mixed_b, weight, bias, gain, shift, seq):
    rows, width = tokens.shape
    row = lambda w: pl.BlockSpec((seq, w), lambda i: (i, 0))
    one = once((1, width))
    return pl.pallas_call(
        middle_kernel,
        grid=(rows // seq,),
        in_specs=[row(width), row(width // 2), row(width // 2), once(weight.shape), one, one, one],
        out_specs=[row(width), row(width)],
        out_shape=[shape_of((rows, width), f32), shape_of((rows, width), bf16)],
        compiler_params=params(1),
        cost_estimate=cost(2 * rows * width * width, rows * width * 10),
        name="middle",
    )(tokens, mixed_a, mixed_b, weight, bias, gain, shift)


def mlp_kernel(
    valid, where, normed, cotangent, total_in, back_in, up, down, bias_up, bias_down,
    total_out, back_out, up_sum, *rest, seq, tile, first, last, cut,
):
    *outs, normed_all, grad_all, active, hidden_grad = rest
    step = pl.program_id(0)
    tiles = pl.num_programs(0) - 1
    width = normed.shape[1]

    @pl.when(step < tiles)
    def _():
        span = pl.ds(pl.multiple_of(step * tile, tile), tile)
        each = seq // tile
        place = lax.broadcasted_iota(jnp.int32, (tile, 1), 0) + lax.rem(step, each) * tile
        kept = place < valid[step // each]
        low_in = normed[...]
        grad = jnp.where(kept, cotangent[...].astype(f32), 0.0).astype(bf16)
        hidden = dot(low_in, up[...], NN) + bias_up[...]
        wide = dot(grad, down[...], NT)
        value, slope = gelu_parts(hidden)
        value = value.astype(bf16)
        low = (slope * wide).astype(bf16)
        normed_all[span, :] = low_in
        grad_all[span, :] = grad
        active[span, :] = value
        hidden_grad[span, :] = low
        accumulate(up_sum, column_sum(low.astype(f32)), step == 0)
        total = total_in[...] + dot(value, down[...], NN)
        if first:
            total = total + bias_down[...]
        if last:
            total = jnp.where(kept, total, 0.0)
        total_out[...] = total.astype(total_out.dtype)
        back = dot(low, up[...], NT)
        back_out[...] = back if first else back_in[...] + back

    @pl.when(step == tiles)
    def _():
        store_cut(where[0], outs, slice(0, width), dot(normed_all[...], hidden_grad[...], TN), cut)
        store_cut(where[0], outs, slice(width, 2 * width), dot(active[...], grad_all[...], TN), cut)


def mlp(back, valid, where, normed, cotangent, total, both, bias_up, bias_down, seq, place, last, cut):
    rows, width = normed.shape
    tile = seq // 2 if seq % 32 == 0 else seq
    tiles = rows // tile
    first = back is None
    if first:
        back = total
    row = lambda: pl.BlockSpec((tile, width), lambda j, *_: (jnp.minimum(j, tiles - 1), 0))
    fixed = pl.BlockSpec((tile, width), lambda j, *_: (0, 0))
    square = lambda at: pl.BlockSpec(
        (width, width), lambda j, *_: (0, at), pipeline_mode=pl.Buffered(buffer_count=1)
    )
    specs, shapes = cut_shapes(width, 2 * width, 2 * width, lambda j: 0, cut)
    return pl.pallas_call(
        functools.partial(mlp_kernel, seq=seq, tile=tile, first=first, last=last, cut=cut),
        grid_spec=pltpu.PrefetchScalarGridSpec(
            num_scalar_prefetch=2,
            grid=(tiles + 1,),
            in_specs=[
                row(), row(), row(), fixed if first else row(),
                square(2 * place), square(2 * place + 1), once((1, width)), once((1, width)),
            ],
            out_specs=[row(), row(), pl.BlockSpec((1, width), lambda j, *_: (0, 0))] + specs,
            scratch_shapes=[pltpu.VMEM((rows, width), bf16)] * 4,
        ),
        out_shape=[
            shape_of((rows, width), bf16 if last else f32),
            shape_of((rows, width), f32),
            shape_of((1, width), f32),
        ]
        + shapes,
        compiler_params=params(1),
        cost_estimate=cost(),
        name="mlp",
    )(valid, where, normed, cotangent, total, back, both, both, bias_up, bias_down)


def middle_back_kernel(
    valid, hidden_back, middle, cotangent, gain, weight, inv_a, inv_b,
    middle_grad, low_grad, mixed_grad, gain_sum, shift_sum, bias_sum, down_sum,
):
    item = pl.program_id(0)
    first = item == 0
    seq, width = middle.shape
    half = width // 2
    grad = hidden_back[...]
    unit, scale = normalize(middle[...])
    place = lax.broadcasted_iota(jnp.int32, (seq, 1), 0)
    kept = jnp.where(place < valid[item], cotangent[...].astype(f32), 0.0)
    accumulate(gain_sum, column_sum(grad * unit), first)
    accumulate(shift_sum, column_sum(grad), first)
    accumulate(down_sum, column_sum(kept), first)
    full = kept + norm_back(grad, gain[...], unit, scale)
    middle_grad[...] = full
    low = full.astype(bf16)
    low_grad[...] = low
    accumulate(bias_sum, column_sum(low.astype(f32)), first)
    back = dot(low, weight[:, -width:], NT)
    mixed_grad[:, :half] = (back[:, :half] * inv_a[...]).astype(bf16)
    mixed_grad[:, half:] = (back[:, half:] * inv_b[...]).astype(bf16)


def middle_back(hidden_back, valid, middle, cotangent, gain, weight, inv_a, inv_b, seq):
    rows, width = middle.shape
    row = lambda w: pl.BlockSpec((seq, w), lambda i, valid: (i, 0))
    fixed = lambda s: pl.BlockSpec(s, lambda i, valid: (0, 0))
    return pl.pallas_call(
        middle_back_kernel,
        grid_spec=pltpu.PrefetchScalarGridSpec(
            num_scalar_prefetch=1,
            grid=(rows // seq,),
            in_specs=[
                row(width), row(width), row(width), once((1, width)),
                once(weight.shape), row(width // 2), row(width // 2),
            ],
            out_specs=[row(width), row(width), row(width)] + [fixed((1, width))] * 4,
        ),
        out_shape=[
            shape_of((rows, width), f32),
            shape_of((rows, width), bf16),
            shape_of((rows, width), bf16),
        ]
        + [shape_of((1, width), f32)] * 4,
        compiler_params=params(1),
        cost_estimate=cost(2 * rows * width * width, rows * width * 26),
        name="middle_back",
    )(valid, hidden_back, middle, cotangent, gain, weight, inv_a, inv_b)


def input_back_kernel(grad_a, grad_b, weight_a, weight_b, tokens, middle_grad, gain, input_grad, gain_sum, shift_sum):
    first = pl.program_id(0) == 0
    span = grad_a.shape[1]
    grad = dot(grad_a[...], weight_a[:, :span], NT) + dot(grad_b[...], weight_b[:, :span], NT)
    unit, scale = normalize(tokens[...].astype(f32))
    accumulate(gain_sum, column_sum(grad * unit), first)
    accumulate(shift_sum, column_sum(grad), first)
    full = middle_grad[...] + norm_back(grad, gain[...], unit, scale)
    input_grad[...] = full.astype(bf16)


def input_back(grad_a, grad_b, weight_a, weight_b, tokens, middle_grad, gain, seq):
    rows, width = tokens.shape
    row = lambda w: pl.BlockSpec((seq, w), lambda i: (i, 0))
    fixed = pl.BlockSpec((1, width), lambda i: (0, 0))
    return pl.pallas_call(
        input_back_kernel,
        grid=(rows // seq,),
        in_specs=[row(grad_a.shape[1]), row(grad_b.shape[1]), once(weight_a.shape), once(weight_b.shape)]
        + [row(width), row(width), once((1, width))],
        out_specs=[row(width), fixed, fixed],
        out_shape=[shape_of((rows, width), bf16)] + [shape_of((1, width), f32)] * 2,
        compiler_params=params(1),
        cost_estimate=cost(2 * rows * width * 3 * width, rows * width * 14),
        name="input_back",
    )(grad_a, grad_b, weight_a, weight_b, tokens, middle_grad, gain)


def local(mesh, tokens, cotangent, group, text_len, qkv_w, out_w, mlp_in, mlp_out, gains, biases):
    items, seq, width = tokens.shape
    rows = items * seq
    count = mesh.size
    share = width // count
    wide = mlp_in.shape[0] // share
    chunks = wide // width
    half = width // 2
    span = 3 * half
    valid = (PATCH_SMALL + (PATCH_LARGE - PATCH_SMALL) * group + text_len).astype(jnp.int32)
    flat = tokens.reshape(rows, width)
    cot = cotangent.reshape(rows, width)
    flights = Flights()
    me = lax.axis_index(AXES)
    core, outer, others = bit_groups(mesh)
    where = jnp.stack([position(me, core), position(me, outer), position(me, others[0])]).astype(jnp.int32)
    cut = share if cut_by_core(mesh) and share % 8 == 0 else 0

    def sums(arrays, lengths):
        if cut:
            keeps, sends = zip(*arrays)
            return flights.add(fast_sum_steps(keeps, sends, where, mesh), lengths)
        whole = jnp.concatenate([array for (array,) in arrays], 1)
        return flights.add(sum_steps(whole, mesh, bf16), lengths)


    def by_pairs(matrix, part):
        pieces = []
        for pair in range(part * 3, part * 3 + 3):
            for place in range(3):
                at = place * width + pair * 128
                pieces.append(matrix[:, at : at + 128])
        return jnp.concatenate(pieces, 1)

    own_up = mlp_in.reshape(share, count, chunks, share).transpose(0, 2, 1, 3).reshape(share, chunks, width)
    own_down = mlp_out.reshape(chunks, share, width).transpose(1, 0, 2)
    own_both = jnp.concatenate([own_up, own_down], 2).reshape(share, 2 * wide)

    own_qkv = qkv_w.reshape(share, 3 * width)
    small = jnp.concatenate([gains, biases])
    small_rows = -(-small.shape[0] // 128)
    padded = jnp.pad(small, (0, small_rows * 128 - small.shape[0])).reshape(small_rows, 128)
    padded = jnp.pad(padded, ((0, share - small_rows), (0, 0)))
    job = flights.add(gather_steps(jnp.concatenate([by_pairs(own_qkv, 0), padded], 1), mesh), [])
    flights.finish(len(others))
    own_both = flights.behind(own_both)
    early = chunks // 2 * 2 * width
    both = [
        lax.all_gather(part, AXES, axis=0, tiled=True)
        for part in (own_both[:, :early], own_both[:, early:])
    ]
    flights.finish()
    first = job["result"]
    own_second = jnp.concatenate([by_pairs(own_qkv, 1), out_w.reshape(share, width)], 1)
    second_job = flights.add(gather_steps(own_second, mesh), [1, 1, 1])

    small = first[:, span:].reshape(count, share, 128)[:, :small_rows]
    small = small.reshape(count, small_rows * 128).astype(f32)
    edge = gains.shape[0]
    gain = small[:, :edge].reshape(1, 2 * width)
    bias = small[:, edge : edge + biases.shape[0]].reshape(1, 6 * width + wide)
    gain_one, gain_two = gain[:, :width], gain[:, width:]
    bias_query, bias_value, bias_output, shift_one, shift_two, bias_down = (
        bias[:, p * width : (p + 1) * width] for p in range(6)
    )
    bias_up = bias[:, 6 * width :].reshape(count, chunks, share).transpose(1, 0, 2).reshape(1, wide)
    bias_joined = jnp.concatenate([bias_query, jnp.zeros_like(bias_query), bias_value], 1)
    bias_parts = [by_pairs(bias_joined, part) for part in range(2)]

    normed, joined_a = flights.run(
        lambda x: first_qkv(x, gain_one, shift_one, first, bias_parts[0], seq), flat
    )
    mixed_a, raised_a, inv_a = flights.run(lambda x: attend(x, valid, seq), joined_a)
    flights.finish()
    second = second_job["result"]
    joined_b = next_qkv(normed, second, bias_parts[1], seq)
    mixed_b, raised_b, inv_b = attend(joined_b, valid, seq)
    middle, normed_two = middle_of(
        flat, mixed_a, mixed_b, second, bias_output, gain_two, shift_two, seq
    )

    total, back, up_sums, mlp_jobs, grads = middle, None, [], [], []
    for chunk in range(chunks):
        place = chunk if chunk < chunks // 2 else chunk - chunks // 2
        lanes = slice(chunk * width, (chunk + 1) * width)
        total, back, up_sum, *outs = flights.run(
            lambda x: mlp(
                back, valid, where, x, cot, total, both[chunk >= chunks // 2], bias_up[:, lanes],
                bias_down, seq, place, chunk == chunks - 1, cut,
            ),
            normed_two,
        )
        up_sums.append(up_sum)
        grads.append(outs)
        if chunk in (chunks // 2 - 1, chunks - 1):
            mlp_jobs.append(sums(grads, [1, 1, 1]))
            grads = []
    block_out, hidden_back = total, back
    up_sum = jnp.concatenate(up_sums, 1)

    middle_grad, low_grad, mixed_grad, gain_two_sum, shift_two_sum, bias_out_sum, down_sum = flights.run(
        lambda x: middle_back(x, valid, middle, cot, gain_two, second, inv_a, inv_b, seq), hidden_back
    )
    joined_grad_a, qkv_sum_a, *grads_a = flights.run(
        lambda x: attend_back(
            x, where, joined_a, mixed_a, raised_a, normed, seq, 0, cut, (mixed_a, mixed_b, low_grad)
        ),
        mixed_grad,
    )
    sum_a = sums([grads_a], [1, 1, 1])
    joined_grad_b, qkv_sum_b, *grads_b = flights.run(
        lambda x: attend_back(x, where, joined_b, mixed_b, raised_b, normed, seq, 1, cut), mixed_grad
    )
    sum_b = sums([grads_b], [1, 1, 1])
    input_grad, gain_one_sum, shift_one_sum = flights.run(
        lambda x: input_back(joined_grad_a, x, first, second, flat, middle_grad, gain_one, seq),
        joined_grad_b,
    )

    def by_kind(part_a, part_b):
        return jnp.concatenate(
            [
                piece[:, (3 * pair + place) * 128 : (3 * pair + place + 1) * 128]
                for place in range(3)
                for piece in (part_a, part_b)
                for pair in range(3)
            ],
            1,
        )

    joined_sums = by_kind(qkv_sum_a, qkv_sum_b)
    up_sum = up_sum.reshape(chunks, count, share).transpose(1, 0, 2).reshape(1, wide)
    gain_sums = jnp.concatenate([gain_one_sum, gain_two_sum], 1).reshape(count, edge)
    bias_sums = jnp.concatenate(
        [
            joined_sums[:, :width],
            joined_sums[:, 2 * width :],
            bias_out_sum,
            shift_one_sum,
            shift_two_sum,
            down_sum,
            up_sum,
        ],
        1,
    ).reshape(count, biases.shape[0])
    small_job = flights.add(small_sum_steps(jnp.concatenate([gain_sums, bias_sums], 1), mesh), [])
    flights.finish()
    small_total = small_job["result"]
    mlp_total = jnp.concatenate([job["result"] for job in mlp_jobs], 1).reshape(share, chunks, 2, width)
    up_total = mlp_total[:, :, 0].reshape(share, chunks, count, share).transpose(0, 2, 1, 3)
    down_total = mlp_total[:, :, 1].transpose(1, 0, 2)
    total_a, total_b = sum_a["result"], sum_b["result"]
    return (
        block_out.reshape(tokens.shape),
        input_grad.reshape(tokens.shape),
        by_kind(total_a, total_b).reshape(-1),
        total_a[:, span:].reshape(-1),
        up_total.reshape(-1),
        down_total.reshape(-1),
        small_total[:edge],
        small_total[edge:],
    )


def solution(mesh):
    split = P(AXES)
    whole = P(AXES, None, None)
    return jax.shard_map(
        functools.partial(local, mesh),
        mesh=mesh,
        in_specs=(whole, whole) + (split,) * 8,
        out_specs=(whole, whole) + (split,) * 6,
        check_vma=False,
    )
```

```python
import functools
import math

import jax
import jax.numpy as jnp
from jax import lax
from jax.experimental import pallas as pl
from jax.experimental.pallas import tpu as pltpu
from jax.sharding import PartitionSpec as P

HEADS = 12
PATCH_SMALL = 196
PATCH_LARGE = 576
AXES = ("dp", "fsdp")
bf16 = jnp.bfloat16
f32 = jnp.float32
NN = (((1,), (0,)), ((), ()))
NT = (((1,), (1,)), ((), ()))
TN = (((0,), (0,)), ((), ()))
VMEM_LIMIT = 60 * 2**20
TILE = 304
ATILE = 304
AHEAD = 1
MTILE = 304
MAHEAD = 1
LTILE = 608
LSUB = 304
BOT = 304
BTILE = 304
BAHEAD = 1
LOG2E = 1.4426950408889634


def dot(a, b, dims):
    return lax.dot_general(a, b, dims, preferred_element_type=f32)


def params(n):
    return pltpu.CompilerParams(
        vmem_limit_bytes=VMEM_LIMIT, dimension_semantics=("arbitrary",) * n
    )


def cost(*_):
    return pl.CostEstimate(flops=1, bytes_accessed=1, transcendentals=0)


def tile_of(seq):
    return TILE if seq % TILE == 0 else seq


def once(shape):
    return pl.BlockSpec(
        shape, lambda *_: (0,) * len(shape), pipeline_mode=pl.Buffered(buffer_count=1)
    )


def shape_of(shape, dtype):
    return jax.ShapeDtypeStruct(shape, dtype)


class Flights:
    def __init__(self):
        self.waiting = []
        self.flying = []

    def add(self, steps, lengths):
        job = {"steps": steps, "lengths": list(lengths), "result": None}
        self.advance(job, None)
        return job

    def advance(self, job, came):
        try:
            sends = job["steps"].send(came) if came is not None else next(job["steps"])
        except StopIteration as stop:
            job["result"] = stop.value
            return
        length = job["lengths"].pop(0) if job["lengths"] else 1
        self.waiting.append((job, sends, length))

    def depart(self):
        for job, sends, length in self.waiting:
            came = [lax.ppermute(array, AXES, pairs) for array, pairs in sends]
            self.flying.append([job, came, length])
        self.waiting = []

    def run(self, kernel, operand, *others):
        arrays = [array for _, sends, _ in self.waiting for array, _ in sends]
        if arrays:
            operand, arrays = lax.optimization_barrier((operand, arrays))
            left = iter(arrays)
            self.waiting = [
                (job, [(next(left), pairs) for _, pairs in sends], length)
                for job, sends, length in self.waiting
            ]
        self.depart()
        out = kernel(operand, *others)
        for flight in self.flying:
            flight[2] -= 1
        landed = [flight for flight in self.flying if flight[2] <= 0]
        self.flying = [flight for flight in self.flying if flight[2] > 0]
        if landed:
            out, came = lax.optimization_barrier((out, [flight[1] for flight in landed]))
            for flight, got in zip(landed, came):
                self.advance(flight[0], got)
        return out

    def behind(self, value):
        value, _ = lax.optimization_barrier((value, [array for _, sends, _ in self.waiting for array, _ in sends]))
        return value

    def land(self):
        held, self.flying = self.flying, []
        self.finish(1)
        self.flying += held

    def finish(self, turns=1 << 30):
        while (self.waiting or self.flying) and turns > 0:
            turns -= 1
            self.depart()
            landed, self.flying = self.flying, []
            cames = lax.optimization_barrier([flight[1] for flight in landed])
            for flight, came in zip(landed, cames):
                self.advance(flight[0], came)


def bit_groups(mesh):
    inner = int(math.log2(mesh.shape["fsdp"]))
    outer = int(math.log2(mesh.shape["dp"]))
    rest = [list(range(b, min(b + 2, inner))) for b in range(1, inner, 2)]
    return [0], list(range(inner, inner + outer)), rest


def position(me, bits):
    spot = 0
    for place, bit in enumerate(bits):
        spot = spot + ((me >> bit) & 1) * (1 << place)
    return spot


def partners(count, bits):
    swaps = []
    for step in range(1, 1 << len(bits)):
        mask = 0
        for place, bit in enumerate(bits):
            if (step >> place) & 1:
                mask |= 1 << bit
        swaps.append((step, [(i, i ^ mask) for i in range(count)]))
    return swaps


def gather_steps(shard, mesh, groups):
    count = mesh.size
    me = lax.axis_index(AXES)
    bits = int(math.log2(count))
    rows, columns = shard.shape
    held = shard.reshape((1,) * bits + (rows, columns))
    for group in groups:
        swaps = partners(count, group)
        came = yield [(held, pairs) for _, pairs in swaps]
        shape = list(held.shape)
        for bit in group:
            shape[bits - 1 - bit] = 2
        whole = jnp.zeros(shape, shard.dtype)
        for (step, _), got in zip([(0, None)] + swaps, [held] + came):
            start = [0] * len(shape)
            for place, bit in enumerate(group):
                start[bits - 1 - bit] = ((me >> bit) & 1) ^ ((step >> place) & 1)
            whole = lax.dynamic_update_slice(whole, got, start)
        held = whole
    return held.reshape(count * rows, columns)


def pick(array, axis, index):
    return lax.dynamic_slice_in_dim(array, index, 1, axis)


def total(terms, axis, index, kind):
    return sum(pick(term, axis, index).astype(f32) for term in terms).astype(kind)


def sum_steps(parts, mesh, kind):
    count = mesh.size
    core, outer, rest = bit_groups(mesh)
    me = lax.axis_index(AXES)
    rows, columns = parts.shape[0] // count, parts.shape[1]
    rest_size = mesh.shape["fsdp"] // 2
    held = parts.reshape(mesh.shape["dp"], rest_size, 2, rows, columns)
    spot = position(me, core)
    (got,) = yield [(pick(held, 2, spot ^ 1).astype(kind), partners(count, core)[0][1])]
    terms = [pick(held, 2, spot), got]
    split = 2 if len(outer) == 2 and columns % 256 == 0 else 1
    width = columns // split
    shape = (2,) * len(outer) + (rest_size, 1, rows, width)
    pieces = []
    for piece in range(split):
        own = [term[..., piece * width : (piece + 1) * width].reshape(shape) for term in terms]
        order = list(range(len(outer)))
        pieces.append((own, order if piece == 0 else order[::-1]))
    for turn in range(len(outer)):
        sends = []
        for own, order in pieces:
            axis = order[turn]
            bit = outer[len(outer) - 1 - axis]
            mine = position(me, [bit])
            sends.append((total(own, axis, mine ^ 1, kind), partners(count, [bit])[0][1]))
        came = yield sends
        pieces = [
            ([pick(term, order[turn], position(me, [outer[len(outer) - 1 - order[turn]]])) for term in own] + [got], order)
            for (own, order), got in zip(pieces, came)
        ]
    left = rest_size
    pieces = [[term.reshape(rest_size, rows, width) for term in own] for own, _ in pieces]
    for bits in reversed(rest):
        size = 1 << len(bits)
        left //= size
        pieces = [[term.reshape(size, left, rows, width) for term in own] for own in pieces]
        spot = position(me, bits)
        swaps = partners(count, bits)
        sends = [
            (jnp.concatenate([total(own, 0, spot ^ step, kind) for own in pieces], -1), pairs)
            for step, pairs in swaps
        ]
        came = yield sends
        pieces = [
            [pick(term, 0, spot) for term in own]
            + [got[..., place * width : (place + 1) * width] for got in came]
            for place, own in enumerate(pieces)
        ]
    sums = [sum(term.astype(f32) for term in own).reshape(rows, width) for own in pieces]
    return jnp.concatenate(sums, -1)


def plane_sum_kernel(where, *refs, parts):
    keeps, cames, outs = refs[:parts], refs[parts : 2 * parts], refs[2 * parts :]
    for step, out in enumerate(outs):
        place = where[1] ^ step
        start = 0
        for keep, came in zip(keeps, cames):
            lanes = slice(start, start + keep.shape[-1])
            start += keep.shape[-1]
            out[:, lanes] = keep[place] + came[place]


def plane_sum(where, keeps, cames, size):
    blocks, rows, _ = keeps[0].shape
    left = blocks // size
    columns = sum(keep.shape[2] for keep in keeps)
    arrays = [array.reshape(size, left, rows, array.shape[2]) for array in (*keeps, *cames)]
    part = pl.BlockSpec((None, rows, columns), lambda j, where: (j, 0, 0))
    return pl.pallas_call(
        functools.partial(plane_sum_kernel, parts=len(keeps)),
        grid_spec=pltpu.PrefetchScalarGridSpec(
            num_scalar_prefetch=1,
            grid=(left,),
            in_specs=[
                pl.BlockSpec((size, None, rows, array.shape[3]), lambda j, where: (0, j, 0, 0))
                for array in arrays
            ],
            out_specs=[part] * size,
        ),
        out_shape=[shape_of((left, rows, columns), bf16)] * size,
        compiler_params=params(1),
        cost_estimate=cost(blocks * rows * columns, blocks * rows * columns * 6),
        name="plane_sum",
    )(where, *arrays)


def line_sum_kernel(where, *refs, sizes):
    outs = refs[sum(sizes) :]
    for step, out in enumerate(outs):
        place = where[2] ^ step
        at = start = 0
        for size in sizes:
            terms = refs[at : at + size]
            at += size
            lanes = slice(start, start + terms[0].shape[2])
            start += terms[0].shape[2]
            out[:, lanes] = sum(term[place].astype(f32) for term in terms).astype(out.dtype)


def line_sum(where, groups):
    size, rows, _ = groups[0][0].shape
    columns = sum(group[0].shape[2] for group in groups)
    arrays = [array for group in groups for array in group]
    return pl.pallas_call(
        functools.partial(line_sum_kernel, sizes=[len(group) for group in groups]),
        grid_spec=pltpu.PrefetchScalarGridSpec(
            num_scalar_prefetch=1,
            grid=(1,),
            in_specs=[once(array.shape) for array in arrays],
            out_specs=[once((rows, columns))] * size,
        ),
        out_shape=[shape_of((rows, columns), f32)] + [shape_of((rows, columns), bf16)] * (size - 1),
        compiler_params=params(1),
        cost_estimate=cost(),
        name="line_sum",
    )(where, *arrays)


def fold_first_kernel(where, keep, came, keep_a, send_a, keep_b, send_b):
    slow, fast = where[1] // 2, where[1] % 2
    cut = keep_a.shape[-1]
    for other in range(2):
        for place, out, lanes in (
            (slow * 2 + other, keep_a, slice(0, cut)),
            ((slow ^ 1) * 2 + other, send_a, slice(0, cut)),
            (other * 2 + fast, keep_b, slice(cut, None)),
            (other * 2 + (fast ^ 1), send_b, slice(cut, None)),
        ):
            out[other] = keep[place, :, lanes] + came[place, :, lanes]


def fold_first(where, keep, came):
    blocks, rows, columns = keep.shape
    left = blocks // 4
    cut = columns // 256 * 128
    whole = pl.BlockSpec((4, None, rows, columns), lambda j, where: (0, j, 0, 0))
    spec = lambda w: pl.BlockSpec((2, None, rows, w), lambda j, where: (0, j, 0, 0))
    widths = [cut, cut, columns - cut, columns - cut]
    return pl.pallas_call(
        fold_first_kernel,
        grid_spec=pltpu.PrefetchScalarGridSpec(
            num_scalar_prefetch=1,
            grid=(left,),
            in_specs=[whole, whole],
            out_specs=[spec(w) for w in widths],
        ),
        out_shape=[shape_of((2, left, rows, w), bf16) for w in widths],
        compiler_params=params(1),
        cost_estimate=cost(),
        name="fold_first",
    )(where, *(array.reshape(4, left, rows, columns) for array in (keep, came)))


def fold_second_kernel(where, keep_a, came_a, keep_b, came_b, own_a, send_a, own_b, send_b):
    slow, fast = where[1] // 2, where[1] % 2
    for keep, came, mine, own, send in (
        (keep_a, came_a, fast, own_a, send_a),
        (keep_b, came_b, slow, own_b, send_b),
    ):
        for place, out in ((mine, own), (mine ^ 1, send)):
            out[...] = keep[place] + came[place]


def fold_second(where, keep_a, came_a, keep_b, came_b):
    arrays = (keep_a, came_a, keep_b, came_b)
    _, left, rows, _ = keep_a.shape
    widths = [keep_a.shape[3], keep_a.shape[3], keep_b.shape[3], keep_b.shape[3]]
    return pl.pallas_call(
        fold_second_kernel,
        grid_spec=pltpu.PrefetchScalarGridSpec(
            num_scalar_prefetch=1,
            grid=(left,),
            in_specs=[pl.BlockSpec((2, None, rows, w), lambda j, where: (0, j, 0, 0)) for w in widths],
            out_specs=[pl.BlockSpec((None, rows, w), lambda j, where: (j, 0, 0)) for w in widths],
        ),
        out_shape=[shape_of((left, rows, w), bf16) for w in widths],
        compiler_params=params(1),
        cost_estimate=cost(),
        name="fold_second",
    )(where, *arrays)


def line_first_kernel(where, *refs, sizes):
    keep, send = refs[sum(sizes) :]
    fast = where[2] % 2
    for slow in range(2):
        for place, out in ((slow * 2 + fast, keep), (slow * 2 + (fast ^ 1), send)):
            at = start = 0
            for size in sizes:
                terms = refs[at : at + size]
                at += size
                lanes = slice(start, start + terms[0].shape[2])
                start += terms[0].shape[2]
                first, second = terms
                out[slow, :, lanes] = first[place] + second[place]


def line_first(where, groups):
    size, rows, _ = groups[0][0].shape
    columns = sum(group[0].shape[2] for group in groups)
    arrays = [array for group in groups for array in group]
    return pl.pallas_call(
        functools.partial(line_first_kernel, sizes=[len(group) for group in groups]),
        grid_spec=pltpu.PrefetchScalarGridSpec(
            num_scalar_prefetch=1,
            grid=(1,),
            in_specs=[once(array.shape) for array in arrays],
            out_specs=[once((size // 2, rows, columns))] * 2,
        ),
        out_shape=[shape_of((size // 2, rows, columns), bf16)] * 2,
        compiler_params=params(1),
        cost_estimate=cost(),
        name="line_first",
    )(where, *arrays)


def swap_steps(send, mesh):
    core, _, _ = bit_groups(mesh)
    (came,) = yield [(send, partners(mesh.size, core)[0][1])]
    return came


def fast_sum_steps(keeps, cames, where, mesh):
    count = mesh.size
    _, outer, rest = bit_groups(mesh)
    own, *sends = plane_sum(where, keeps, cames, 1 << len(outer))
    came = yield [(array, pairs) for array, (_, pairs) in zip(sends, partners(count, outer))]
    own, *sends = line_sum(where, [[own, *came]])
    came = yield [(array, pairs) for array, (_, pairs) in zip(sends, partners(count, rest[0]))]
    return own + sum(array.astype(f32) for array in came)


def fold_sum_steps(keep, send, where, mesh):
    count = mesh.size
    core, outer, rest = bit_groups(mesh)
    (came,) = yield [(send, partners(count, core)[0][1])]
    shape = (count // 2, keep.shape[0] * 2 // count, keep.shape[1])
    fast, slow = (partners(count, [bit])[0][1] for bit in outer)
    keep_a, send_a, keep_b, send_b = fold_first(where, keep.reshape(shape), came.reshape(shape))
    came_a, came_b = yield [(send_a, slow), (send_b, fast)]
    own_a, send_a, own_b, send_b = fold_second(where, keep_a, came_a, keep_b, came_b)
    came_a, came_b = yield [(send_a, fast), (send_b, slow)]
    keep, send = line_first(where, [[own_a, came_a], [own_b, came_b]])
    (came,) = yield [(send, partners(count, [rest[0][0]])[0][1])]
    me = lax.axis_index(AXES)
    spot = position(me, [rest[0][1]])
    both = [keep, came]
    (last,) = yield [(total(both, 0, spot ^ 1, bf16), partners(count, [rest[0][1]])[0][1])]
    done = (total(both, 0, spot, f32) + last.astype(f32)).reshape(2, shape[1] // 2, shape[2])
    spot = position(me, core)
    (came,) = yield [(pick(done, 0, spot ^ 1), partners(count, core)[0][1])]
    own, came = pick(done, 0, spot)[0], came[0]
    return jnp.where(spot == 0, own, came), jnp.where(spot == 0, came, own)


def small_sum_steps(parts, mesh):
    count = mesh.size
    core, outer, rest = bit_groups(mesh)
    groups = [core, outer, *reversed(rest)]
    order = [outer, *reversed(rest), core]
    me = lax.axis_index(AXES)
    columns = parts.shape[1]
    held = parts.reshape([1 << len(bits) for bits in order] + [columns])
    for bits in groups:
        axis = order.index(bits)
        spot = position(me, bits)
        swaps = partners(count, bits)
        came = yield [(pick(held, axis, spot ^ step), pairs) for step, pairs in swaps]
        held = pick(held, axis, spot) + sum(came)
    return held.reshape(columns)


def cut_by_core(mesh):
    _, outer, rest = bit_groups(mesh)
    return len(outer) == 2 and len(rest) == 1 and len(rest[0]) == 2


def store_cut(core, outs, lanes, value, rows):
    if len(outs) == 1:
        outs[0][:, lanes] = value.astype(bf16)
        return
    keep, send = outs
    for parity in range(2):
        @pl.when(core == parity)
        def _():
            for device in range(value.shape[0] // rows):
                out = keep if device % 2 == parity else send
                out[device // 2, :, lanes] = value[device * rows : (device + 1) * rows, :].astype(bf16)


def cut_shapes(width, columns, chunk, index, rows):
    if not rows:
        spec = pl.BlockSpec((width, chunk), lambda j, *_: (0, index(j)))
        return [spec], [shape_of((width, columns), bf16)]
    blocks = width // rows // 2
    spec = pl.BlockSpec((blocks, rows, chunk), lambda j, *_: (0, 0, index(j)))
    return [spec] * 2, [shape_of((blocks, rows, columns), bf16)] * 2


def normalize(values):
    center = values - jnp.mean(values, -1, keepdims=True)
    scale = lax.rsqrt(jnp.mean(center * center, -1, keepdims=True) + 1e-05)
    return center * scale, scale


def norm_back(grad, gain, unit, scale):
    inner = grad * gain
    return scale * (
        inner
        - jnp.mean(inner, -1, keepdims=True)
        - unit * jnp.mean(inner * unit, -1, keepdims=True)
    )


def gelu_parts(u):
    phi = 0.5 + 0.5 * lax.erf(u * 0.7071067811865476)
    slope = phi + u * (0.3989422804014327 * jnp.exp2((u * u) * (-0.5 * LOG2E)))
    return u * phi, slope


def column_sum(values):
    return jnp.sum(values, 0, keepdims=True)


def accumulate(ref, value, first):
    @pl.when(first)
    def _():
        ref[...] = value

    @pl.when(jnp.logical_not(first))
    def _():
        ref[...] += value


def two_heads(block, padded):
    seq = block.shape[0]
    first = lax.broadcasted_iota(jnp.int32, block.shape, 1) < 64
    zero = jnp.zeros_like(block)
    pad = jnp.zeros((padded - seq, 128), block.dtype)
    return jnp.concatenate(
        [jnp.where(first, block, zero), pad, jnp.where(first, zero, block), pad], 0
    )


def attend_kernel(valid, *refs, tile, padded, first, pairs):
    if first:
        tokens, gain, shift, weight, bias, normed, joined, mixed, raised_out, inverse = refs
    else:
        (
            normed, weight, bias, tokens, mixed_first, bias_out, gain, shift,
            joined, mixed, raised_out, inverse, middle, normed_two,
        ) = refs
    seq, span = joined.shape
    for start in range(0, seq, tile):
        rows = slice(start, start + tile)
        if first:
            unit, _ = normalize(tokens[rows, :].astype(f32))
            low = (unit * gain[...] + shift[...]).astype(bf16)
            normed[rows, :] = low
        else:
            low = normed[rows, :]
        joined[rows, :] = (dot(low, weight[:, :span], NN) + bias[...]).astype(bf16)

    column = lax.broadcasted_iota(jnp.int32, (1, padded), 1)
    mask = jnp.where(column < valid[pl.program_id(0)], 0.0, -1e30).astype(f32)
    places = [(pair, start) for pair in range(pairs) for start in range(0, seq, ATILE)]
    keys, values = {}, {}
    row = lax.broadcasted_iota(jnp.int32, (2 * padded, 128), 0)
    lane = lax.broadcasted_iota(jnp.int32, (2 * padded, 128), 1)
    ones = jnp.where((row < padded) == (lane < 64), 1.0, 0.0).astype(bf16)

    def scores_at(pair, start):
        if pair not in keys:
            at = pair * 384
            keys[pair] = two_heads(joined[:, at + 128 : at + 256], padded)
            values[pair] = jnp.concatenate([two_heads(joined[:, at + 256 : at + 384], padded), ones], 1)
        return dot(joined[start : start + ATILE, pair * 384 : pair * 384 + 128], keys[pair], NT)

    ahead = [scores_at(*place) for place in places[:AHEAD]]
    for index, (pair, start) in enumerate(places):
        rows = slice(start, start + ATILE)
        if index + AHEAD < len(places):
            ahead.append(scores_at(*places[index + AHEAD]))
        scores = ahead.pop(0)
        halves = []
        for head in range(2):
            part = scores[:, head * padded : (head + 1) * padded] * (0.125 * LOG2E) + mask
            halves.append(jnp.exp2(part - jnp.max(part, 1, keepdims=True)).astype(bf16))
        raised = jnp.concatenate(halves, 1)
        raised_out[pair, rows, :] = raised
        both = dot(raised, values[pair], NN)
        scale = 1.0 / both[:, 128:]
        inverse[rows, pair * 128 : (pair + 1) * 128] = scale
        mixed[rows, pair * 128 : (pair + 1) * 128] = (both[:, :128] * scale).astype(bf16)
    if first:
        return
    width = tokens.shape[1]
    for start in range(0, seq, tile):
        rows = slice(start, start + tile)
        value = tokens[rows, :].astype(f32) + bias_out[...]
        value = value + dot(mixed_first[rows, :], weight[: width // 2, -width:], NN)
        value = value + dot(mixed[rows, :], weight[width // 2 :, -width:], NN)
        middle[rows, :] = value
        unit, _ = normalize(value)
        normed_two[rows, :] = (unit * gain[...] + shift[...]).astype(bf16)


def attend(start, valid, weight, bias, seq, norm=None, after=None):
    rows, width = start.shape
    span = bias.shape[1]
    pairs = span // 384
    items = rows // seq
    padded = -(-seq // 128) * 128
    row = lambda w: pl.BlockSpec((seq, w), lambda i, *_: (i, 0))
    one = once((1, width))
    main = [once(weight.shape), once((1, span))]
    if norm:
        specs, arrays = [row(width), one, one, *main], [start, *norm, weight, bias]
    else:
        specs = [row(width), *main, row(width), row(width // 2), one, one, one]
        arrays = [start, weight, bias, *after]
    outs = [
        row(span),
        row(span // 3),
        pl.BlockSpec((None, pairs, seq, 2 * padded), lambda i, *_: (i, 0, 0, 0)),
        row(span // 3),
    ]
    shapes = [
        shape_of((rows, span), bf16),
        shape_of((rows, span // 3), bf16),
        shape_of((items, pairs, seq, 2 * padded), bf16),
        shape_of((rows, span // 3), f32),
    ]
    if norm:
        outs, shapes = [row(width)] + outs, [shape_of((rows, width), bf16)] + shapes
    else:
        outs += [row(width)] * 2
        shapes += [shape_of((rows, width), f32), shape_of((rows, width), bf16)]
    return pl.pallas_call(
        functools.partial(attend_kernel, tile=tile_of(seq), padded=padded, first=bool(norm), pairs=pairs),
        grid_spec=pltpu.PrefetchScalarGridSpec(
            num_scalar_prefetch=1, grid=(items,), in_specs=specs, out_specs=outs
        ),
        out_shape=shapes,
        compiler_params=params(1),
        cost_estimate=cost(),
        name="attend",
    )(valid, *arrays)


def attend_back_kernel(
    where, joined, mixed_grad, mixed, raised, inverse, normed, *rest, pairs, extra, cut
):
    if extra:
        mixed_a, mixed_b, low_grad, joined_grad, column, *outs, held, scaled, total, total_out = rest
    else:
        joined_grad, column, *outs, held, scaled, total = rest
    item = pl.program_id(0)
    seq, span = joined.shape
    padded = raised.shape[2] // 2
    first = lax.broadcasted_iota(jnp.int32, (BTILE, 128), 1) < 64
    places = [(pair, start) for pair in range(pairs) for start in range(0, seq, BTILE)]
    keys, values = {}, {}

    def prob_grad_at(pair, start):
        at = pair * 384
        if pair not in keys:
            keys[pair] = two_heads(joined[:, at + 128 : at + 256], padded)
            values[pair] = two_heads(joined[:, at + 256 : at + 384], padded)
        rows, lanes = slice(start, start + BTILE), slice(pair * 128, (pair + 1) * 128)
        grad = (mixed_grad[rows, lanes].astype(f32) * inverse[rows, lanes]).astype(bf16)
        scaled[rows, lanes] = grad
        return grad, dot(grad, values[pair], NT)

    def own_half(both):
        return jnp.concatenate([both[:64, :padded], both[64:, padded:]], 0).T[:seq]

    ahead = [prob_grad_at(*place) for place in places[:BAHEAD]]
    for index, (pair, start) in enumerate(places):
        rows, lanes = slice(start, start + BTILE), slice(pair * 128, (pair + 1) * 128)
        at = pair * 384
        if index + BAHEAD < len(places):
            ahead.append(prob_grad_at(*places[index + BAHEAD]))
        grad, prob_grad = ahead.pop(0)
        product = grad.astype(f32) * mixed[rows, lanes].astype(f32)
        zero = jnp.zeros_like(product)
        halves = []
        for head in range(2):
            own = jnp.where(first, product, zero) if head == 0 else jnp.where(first, zero, product)
            centre = jnp.sum(own, 1, keepdims=True)
            half = slice(head * padded, (head + 1) * padded)
            halves.append((raised[pair, rows, half].astype(f32) * (prob_grad[:, half] - centre)).astype(bf16))
        score_grad = jnp.concatenate(halves, 1)
        held[rows, :] = score_grad
        joined_grad[rows, at : at + 128] = (dot(score_grad, keys[pair], NN) * 0.125).astype(bf16)
        if start + BTILE == seq:
            joined_grad[:, at + 128 : at + 256] = (
                own_half(dot(joined[:, at : at + 128].T, held[...], NN)) * 0.125
            ).astype(bf16)
            joined_grad[:, at + 256 : at + 384] = own_half(
                dot(scaled[:, lanes].T, raised[pair], NN)
            ).astype(bf16)

    value = joined_grad[...]
    accumulate(total, dot(normed[...], value, TN), item == 0)
    accumulate(column, column_sum(value.astype(f32)), item == 0)
    if extra:
        both = [dot(mixed_a[...], low_grad[...], TN), dot(mixed_b[...], low_grad[...], TN)]
        accumulate(total_out, jnp.concatenate(both, 0), item == 0)

    @pl.when(item == pl.num_programs(0) - 1)
    def _():
        store_cut(where[0], outs, slice(0, span), total[...], cut)
        if extra:
            store_cut(where[0], outs, slice(span, span + total_out.shape[1]), total_out[...], cut)


def attend_back(mixed_grad, where, joined, mixed, raised, inverse, normed, seq, part, cut, others=()):
    rows, span = joined.shape
    width = normed.shape[1]
    items, pairs, _, keys = raised.shape
    row = lambda w, off=0: pl.BlockSpec((seq, w), lambda i, *_: (i, off))
    columns = span + (width if others else 0)
    specs, shapes = cut_shapes(width, columns, columns, lambda j: 0, cut)
    return pl.pallas_call(
        functools.partial(attend_back_kernel, pairs=pairs, extra=bool(others), cut=cut),
        grid_spec=pltpu.PrefetchScalarGridSpec(
            num_scalar_prefetch=1,
            grid=(items,),
            in_specs=[
                row(span),
                row(span // 3, part),
                row(span // 3),
                pl.BlockSpec((None, pairs, seq, keys), lambda i, *_: (i, 0, 0, 0)),
                row(span // 3),
                row(width),
            ]
            + [row(array.shape[1]) for array in others],
            out_specs=[row(span), pl.BlockSpec((1, span), lambda i, *_: (0, 0))] + specs,
            scratch_shapes=[
                pltpu.VMEM((seq, keys), bf16),
                pltpu.VMEM((seq, span // 3), bf16),
                pltpu.VMEM((width, span), f32),
            ]
            + ([pltpu.VMEM((width, width), f32)] if others else []),
        ),
        out_shape=[shape_of((rows, span), bf16), shape_of((1, span), f32)] + shapes,
        compiler_params=params(1),
        cost_estimate=cost(),
        name="attend_back",
    )(where, joined, mixed_grad, mixed, raised, inverse, normed, *others)


def mlp_kernel(
    valid, where, normed, cotangent, up, down, bias_up,
    active, hidden_grad, up_sum, *rest, seq, tile, cut,
):
    *outs, grad = rest
    rows, width = normed.shape

    @pl.when(pl.program_id(0) == 0)
    def _():
        place = lax.broadcasted_iota(jnp.int32, (seq, 1), 0)
        for item in range(rows // seq):
            span = slice(item * seq, (item + 1) * seq)
            grad[span, :] = jnp.where(place < valid[item], cotangent[span, :].astype(f32), 0.0).astype(bf16)

    def ahead_of(start):
        span = slice(start, start + MTILE)
        return dot(normed[span, :], up[...], NN), dot(grad[span, :], down[...], NT)

    column = jnp.zeros(up_sum.shape, f32)
    starts = list(range(0, rows, MTILE))
    ahead = [ahead_of(start) for start in starts[:MAHEAD]]
    for index, start in enumerate(starts):
        span = slice(start, start + MTILE)
        if index + MAHEAD < len(starts):
            ahead.append(ahead_of(starts[index + MAHEAD]))
        hidden, wide = ahead.pop(0)
        value, slope = gelu_parts(hidden + bias_up[...])
        low = (slope * wide).astype(bf16)
        active[span, :] = value.astype(bf16)
        hidden_grad[span, :] = low
        column = column + column_sum(low.astype(f32))
    up_sum[...] = column
    first = dot(normed[...], hidden_grad[...], TN).astype(bf16)
    second = dot(active[...], grad[...], TN).astype(bf16)
    if cut:
        keep, send = outs
        for core in range(2):
            @pl.when(where[0] == core)
            def _():
                (keep, send)[core][...] = first
                (send, keep)[core][...] = second
    else:
        outs[0][:, :width] = first
        outs[0][:, width:] = second


def mlp(normed, valid, where, cotangent, both, bias_up, seq, cut):
    rows, width = normed.shape
    wide = both.shape[1] // 2
    chunks = wide // width
    whole = once((rows, width))
    square = lambda off: pl.BlockSpec((width, width), lambda j, *_: (0, j + off))
    row = pl.BlockSpec((rows, width), lambda j, *_: (0, j))
    one = pl.BlockSpec((1, width), lambda j, *_: (0, j))
    if cut:
        specs = [pl.BlockSpec((width, width), lambda j, *_: (0, j))] * 2
        shapes = [shape_of((width, wide), bf16)] * 2
    else:
        specs, shapes = cut_shapes(width, 2 * wide, 2 * width, lambda j: j, 0)
    return pl.pallas_call(
        functools.partial(mlp_kernel, seq=seq, tile=tile_of(seq), cut=cut),
        grid_spec=pltpu.PrefetchScalarGridSpec(
            num_scalar_prefetch=2,
            grid=(chunks,),
            in_specs=[whole, whole, square(0), square(chunks), one],
            out_specs=[row, row, one] + specs,
            scratch_shapes=[pltpu.VMEM((rows, width), bf16)],
        ),
        out_shape=[
            shape_of((rows, width * chunks), bf16),
            shape_of((rows, width * chunks), bf16),
            shape_of((1, width * chunks), f32),
        ]
        + shapes,
        compiler_params=params(1),
        cost_estimate=cost(),
        name="mlp",
    )(valid, where, normed, cotangent, both, both, bias_up)


def block_out_kernel(valid, active, downs, middle, bias_down, *rest, seq, begin):
    block_out = rest[-1]
    tile, width = middle.shape
    step = pl.program_id(0) + begin // tile
    place = lax.broadcasted_iota(jnp.int32, (tile, 1), 0) + lax.rem(step, seq // tile) * tile
    value = middle[...] + bias_down[...]
    for at in range(0, downs.shape[1], width):
        value = value + dot(active[:, at : at + width], downs[:, at : at + width], NN)
    block_out[...] = jnp.where(place < valid[step // (seq // tile)], value, 0.0).astype(bf16)


def half_of(both, second):
    width, columns = both.shape
    return pl.BlockSpec(
        (width, columns // 2), lambda j, *_: (0, second), pipeline_mode=pl.Buffered(buffer_count=1)
    )


def block_out_of(middle, valid, active, both, bias_down, seq, begin, end, before=None):
    rows, width = middle.shape
    tile = BOT if seq % BOT == 0 else seq
    skip = begin // tile
    row = lambda w: pl.BlockSpec((tile, w), lambda j, *_: (j + skip, 0))
    specs = [row(active.shape[1]), half_of(both, 1), row(width), once((1, width))]
    arrays = [active, both, middle, bias_down]
    aliases = {}
    if before is not None:
        aliases = {len(arrays) + 1: 0}
        specs.append(pl.BlockSpec(memory_space=pl.ANY))
        arrays.append(before)
    return pl.pallas_call(
        functools.partial(block_out_kernel, seq=seq, begin=begin),
        grid_spec=pltpu.PrefetchScalarGridSpec(
            num_scalar_prefetch=1,
            grid=((end - begin) // tile,),
            in_specs=specs,
            out_specs=row(width),
        ),
        out_shape=shape_of((rows, width), bf16),
        input_output_aliases=aliases,
        compiler_params=params(1),
        cost_estimate=cost(),
        name="block_out",
    )(valid, *arrays)


def middle_back_kernel(
    valid, hidden_grad, ups, middle, cotangent, gain, weight,
    low_grad, mixed_grad, gain_sum, shift_sum, bias_sum, down_sum, *, seq, sub,
):
    step = pl.program_id(0)
    tile, width = middle.shape
    each = seq // tile
    starts = list(range(0, tile, sub))
    ahead = [dot(hidden_grad[:sub, :], ups[...], NT)]
    sums = [jnp.zeros((1, width), f32)] * 4
    for index, start in enumerate(starts):
        rows = slice(start, start + sub)
        if index + 1 < len(starts):
            ahead.append(dot(hidden_grad[start + sub : start + 2 * sub, :], ups[...], NT))
        grad = ahead.pop(0)
        unit, scale = normalize(middle[rows, :])
        place = lax.broadcasted_iota(jnp.int32, (sub, 1), 0) + (lax.rem(step, each) * tile + start)
        kept = jnp.where(place < valid[step // each], cotangent[rows, :].astype(f32), 0.0)
        low = (kept + norm_back(grad, gain[...], unit, scale)).astype(bf16)
        low_grad[rows, :] = low
        mixed_grad[rows, :] = dot(low, weight[:, -width:], NT).astype(bf16)
        terms = (grad * unit, grad, low.astype(f32), kept)
        sums = [before + column_sum(term) for before, term in zip(sums, terms)]
    for ref, value in zip((gain_sum, shift_sum, bias_sum, down_sum), sums):
        accumulate(ref, value, step == 0)


def middle_back(middle, valid, hidden_grad, both, cotangent, gain, weight, seq):
    rows, width = middle.shape
    tile = LTILE if seq % LTILE == 0 else seq
    sub = LSUB if tile % LSUB == 0 else tile
    row = lambda w: pl.BlockSpec((tile, w), lambda j, *_: (j, 0))
    one = pl.BlockSpec((1, width), lambda j, *_: (0, 0))
    return pl.pallas_call(
        functools.partial(middle_back_kernel, seq=seq, sub=sub),
        grid_spec=pltpu.PrefetchScalarGridSpec(
            num_scalar_prefetch=1,
            grid=(rows // tile,),
            in_specs=[
                row(hidden_grad.shape[1]), half_of(both, 0), row(width), row(width),
                once((1, width)), once(weight.shape),
            ],
            out_specs=[row(width), row(width)] + [one] * 4,
        ),
        out_shape=[shape_of((rows, width), bf16)] * 2 + [shape_of((1, width), f32)] * 4,
        compiler_params=params(1),
        cost_estimate=cost(),
        name="middle_back",
    )(valid, hidden_grad, both, middle, cotangent, gain, weight)


def input_back_kernel(
    grad_a, grad_b, weight_a, weight_b, tokens, low_grad, gain, input_grad, gain_sum, shift_sum, *, sub
):
    span = grad_a.shape[1]
    tile, width = tokens.shape

    def ahead_of(start):
        rows = slice(start, start + sub)
        return dot(grad_a[rows, :], weight_a[:, :span], NT) + dot(grad_b[rows, :], weight_b[:, :span], NT)

    starts = list(range(0, tile, sub))
    ahead = [ahead_of(0)]
    sums = [jnp.zeros((1, width), f32)] * 2
    for index, start in enumerate(starts):
        rows = slice(start, start + sub)
        if index + 1 < len(starts):
            ahead.append(ahead_of(start + sub))
        grad = ahead.pop(0)
        unit, scale = normalize(tokens[rows, :].astype(f32))
        sums = [before + column_sum(term) for before, term in zip(sums, (grad * unit, grad))]
        full = low_grad[rows, :].astype(f32) + norm_back(grad, gain[...], unit, scale)
        input_grad[rows, :] = full.astype(bf16)
    for ref, value in zip((gain_sum, shift_sum), sums):
        accumulate(ref, value, pl.program_id(0) == 0)


def input_back(grad_a, grad_b, weight_a, weight_b, tokens, low_grad, gain, seq):
    rows, width = tokens.shape
    tile = LTILE if seq % LTILE == 0 else seq
    sub = LSUB if tile % LSUB == 0 else tile
    row = lambda w: pl.BlockSpec((tile, w), lambda i: (i, 0))
    fixed = pl.BlockSpec((1, width), lambda i: (0, 0))
    return pl.pallas_call(
        functools.partial(input_back_kernel, sub=sub),
        grid=(rows // tile,),
        in_specs=[row(grad_a.shape[1]), row(grad_b.shape[1]), once(weight_a.shape), once(weight_b.shape)]
        + [row(width), row(width), once((1, width))],
        out_specs=[row(width), fixed, fixed],
        out_shape=[shape_of((rows, width), bf16)] + [shape_of((1, width), f32)] * 2,
        compiler_params=params(1),
        cost_estimate=cost(),
        name="input_back",
    )(grad_a, grad_b, weight_a, weight_b, tokens, low_grad, gain)


def local(mesh, tokens, cotangent, group, text_len, qkv_w, out_w, mlp_in, mlp_out, gains, biases):
    items, seq, width = tokens.shape
    rows = items * seq
    count = mesh.size
    share = width // count
    wide = mlp_in.shape[0] // share
    chunks = wide // width
    half = width // 2
    span = 3 * half
    valid = (PATCH_SMALL + (PATCH_LARGE - PATCH_SMALL) * group + text_len).astype(jnp.int32)
    flat = tokens.reshape(rows, width)
    cot = cotangent.reshape(rows, width)
    flights = Flights()
    me = lax.axis_index(AXES)
    core, outer, others = bit_groups(mesh)
    where = jnp.stack([position(me, core), position(me, outer), position(me, others[0])]).astype(jnp.int32)
    cut = share if cut_by_core(mesh) and share % 8 == 0 else 0

    def mlp_sums(arrays):
        if cut:
            return flights.add(fold_sum_steps(*arrays, where, mesh), [])
        return flights.add(sum_steps(arrays[0], mesh, bf16), [])

    def swap(arrays):
        return flights.add(swap_steps(arrays[1], mesh), []) if cut else None

    def sums_after(arrays, swaps):
        if cut:
            keeps, cames = [keep for keep, _ in arrays], [job["result"] for job in swaps]
            return flights.add(fast_sum_steps(keeps, cames, where, mesh), [])
        return flights.add(sum_steps(arrays[0][0], mesh, bf16), [])


    def by_pairs(matrix, part):
        pieces = []
        for pair in range(part * 3, part * 3 + 3):
            for place in range(3):
                at = place * width + pair * 128
                pieces.append(matrix[:, at : at + 128])
        return jnp.concatenate(pieces, 1)

    own_up = mlp_in.reshape(share, count, chunks, share).transpose(0, 2, 1, 3).reshape(share, wide)
    own_down = mlp_out.reshape(chunks, share, width).transpose(1, 0, 2).reshape(share, wide)
    own_both = jnp.concatenate([own_up, own_down], 1)

    own_qkv = qkv_w.reshape(share, 3 * width)
    small = jnp.concatenate([gains, biases])
    small_rows = -(-small.shape[0] // 128)
    padded = jnp.pad(small, (0, small_rows * 128 - small.shape[0])).reshape(small_rows, 128)
    padded = jnp.pad(padded, ((0, share - small_rows), (0, 0)))
    job = flights.add(
        gather_steps(jnp.concatenate([by_pairs(own_qkv, 0), padded], 1), mesh, [*others, outer, core]), []
    )
    flights.finish(len(others))
    own_both = flights.behind(own_both)
    both = lax.all_gather(own_both, AXES, axis=0, tiled=True)
    own_second = jnp.concatenate([by_pairs(own_qkv, 1), out_w.reshape(share, width)], 1)
    singles = [[bit] for group in reversed(others) for bit in reversed(group)]
    second_job = flights.add(gather_steps(own_second, mesh, [*singles, outer, core]), [])
    flights.finish(2)
    first = job["result"]

    small = first[:, span:].reshape(count, share, 128)[:, :small_rows]
    small = small.reshape(count, small_rows * 128).astype(f32)
    edge = gains.shape[0]
    gain = small[:, :edge].reshape(1, 2 * width)
    bias = small[:, edge : edge + biases.shape[0]].reshape(1, 6 * width + wide)
    gain_one, gain_two = gain[:, :width], gain[:, width:]
    bias_query, bias_value, bias_output, shift_one, shift_two, bias_down = (
        bias[:, p * width : (p + 1) * width] for p in range(6)
    )
    bias_up = bias[:, 6 * width :].reshape(count, chunks, share).transpose(1, 0, 2).reshape(1, wide)
    bias_joined = jnp.concatenate([bias_query, jnp.zeros_like(bias_query), bias_value], 1)
    bias_parts = [by_pairs(bias_joined, part) for part in range(2)]

    normed, joined_a, mixed_a, raised_a, inverse_a = flights.run(
        lambda x: attend(x, valid, first, bias_parts[0], seq, (gain_one, shift_one)), flat
    )
    flights.finish()
    second = second_job["result"]
    joined_b, mixed_b, raised_b, inverse_b, middle, normed_two = attend(
        normed, valid, second, bias_parts[1], seq,
        after=(flat, mixed_a, bias_output, gain_two, shift_two),
    )

    active, hidden_grad, up_sum, *mlp_grads = mlp(
        normed_two, valid, where, cot, both, bias_up, seq, cut
    )
    mlp_job = mlp_sums(mlp_grads)

    low_grad, mixed_grad, gain_two_sum, shift_two_sum, bias_out_sum, down_sum = flights.run(
        lambda x: middle_back(x, valid, hidden_grad, both, cot, gain_two, second, seq), middle
    )
    joined_grad_a, qkv_sum_a, *grads_a = flights.run(
        lambda x: attend_back(
            x, where, joined_a, mixed_a, raised_a, inverse_a, normed, seq, 0, cut, (mixed_a, mixed_b, low_grad)
        ),
        mixed_grad,
    )
    swap_a = swap(grads_a)
    joined_grad_b, qkv_sum_b, *grads_b = flights.run(
        lambda x: attend_back(x, where, joined_b, mixed_b, raised_b, inverse_b, normed, seq, 1, cut), mixed_grad
    )
    sum_a = sums_after([grads_a], [swap_a])
    swap_b = swap(grads_b)
    input_grad, gain_one_sum, shift_one_sum = flights.run(
        lambda x: input_back(joined_grad_a, x, first, second, flat, low_grad, gain_one, seq),
        joined_grad_b,
    )

    def by_kind(part_a, part_b):
        return jnp.concatenate(
            [
                piece[:, (3 * pair + place) * 128 : (3 * pair + place + 1) * 128]
                for place in range(3)
                for piece in (part_a, part_b)
                for pair in range(3)
            ],
            1,
        )

    joined_sums = by_kind(qkv_sum_a, qkv_sum_b)
    up_sum = up_sum.reshape(chunks, count, share).transpose(1, 0, 2).reshape(1, wide)
    gain_sums = jnp.concatenate([gain_one_sum, gain_two_sum], 1).reshape(count, edge)
    bias_sums = jnp.concatenate(
        [
            joined_sums[:, :width],
            joined_sums[:, 2 * width :],
            bias_out_sum,
            shift_one_sum,
            shift_two_sum,
            down_sum,
            up_sum,
        ],
        1,
    ).reshape(count, biases.shape[0])
    small = jnp.concatenate([gain_sums, bias_sums], 1)
    if cut:
        small = jnp.pad(small, ((0, 0), (0, small_rows * 128 - small.shape[1])))
        small = small.reshape(count // 2, 2, small_rows, 128)
        spot = position(me, core)
        small = [
            jnp.pad(pick(small, 1, place)[:, 0], ((0, 0), (0, share - small_rows), (0, 0))).astype(bf16)
            for place in (spot, spot ^ 1)
        ]
        swap_small = swap(small)
    else:
        small_job = flights.add(small_sum_steps(small, mesh), [])
        sum_b = sums_after([grads_b], [swap_b])
    cuts = [item * seq for item in range(items + 1)]
    block_out = None
    for begin, end in zip(cuts, cuts[1:]):
        if begin < end:
            block_out = flights.run(
                lambda x: block_out_of(
                    x, valid, active, both, bias_down, seq, begin, end, block_out
                ),
                middle,
            )
            if cut and begin == 0:
                sum_b = sums_after([grads_b, small], [swap_b, swap_small])
    flights.finish()
    total_a, total_b = sum_a["result"], sum_b["result"]
    if cut:
        small_total = total_b[:small_rows, span:].reshape(-1)
        small_total = small_total[: edge + biases.shape[0]]
    else:
        small_total = small_job["result"]
    if cut:
        up_total, down_total = mlp_job["result"]
    else:
        mlp_total = mlp_job["result"].reshape(share, chunks, 2, width)
        up_total, down_total = mlp_total[:, :, 0], mlp_total[:, :, 1]
    up_total = up_total.reshape(share, chunks, count, share).transpose(0, 2, 1, 3)
    down_total = down_total.reshape(share, chunks, width).transpose(1, 0, 2)
    return (
        block_out.reshape(tokens.shape),
        input_grad.reshape(tokens.shape),
        by_kind(total_a, total_b).reshape(-1),
        total_a[:, span:].reshape(-1),
        up_total.reshape(-1),
        down_total.reshape(-1),
        small_total[:edge],
        small_total[edge:],
    )


def solution(mesh):
    split = P(AXES)
    whole = P(AXES, None, None)
    return jax.shard_map(
        functools.partial(local, mesh),
        mesh=mesh,
        in_specs=(whole, whole) + (split,) * 8,
        out_specs=(whole, whole) + (split,) * 6,
        check_vma=False,
    )
```

```python
import functools
import math

import jax
import jax.numpy as jnp
from jax import lax
from jax.experimental import pallas as pl
from jax.experimental.pallas import tpu as pltpu
from jax.sharding import PartitionSpec as P

HEADS = 12
PATCH_SMALL = 196
PATCH_LARGE = 576
AXES = ("dp", "fsdp")
bf16 = jnp.bfloat16
f32 = jnp.float32
NN = (((1,), (0,)), ((), ()))
NT = (((1,), (1,)), ((), ()))
TN = (((0,), (0,)), ((), ()))
VMEM_LIMIT = 60 * 2**20
TILE = 304
ATILE = 304
AHEAD = 1
MTILE = 304
MAHEAD = 1
LTILE = 608
LSUB = 304
BOT = 304
BTILE = 304
BAHEAD = 1
LOG2E = 1.4426950408889634


def dot(a, b, dims):
    return lax.dot_general(a, b, dims, preferred_element_type=f32)


def params(n):
    return pltpu.CompilerParams(
        vmem_limit_bytes=VMEM_LIMIT, dimension_semantics=("arbitrary",) * n
    )


def cost(*_):
    return pl.CostEstimate(flops=1, bytes_accessed=1, transcendentals=0)


def tile_of(seq):
    return TILE if seq % TILE == 0 else seq


def once(shape):
    return pl.BlockSpec(
        shape, lambda *_: (0,) * len(shape), pipeline_mode=pl.Buffered(buffer_count=1)
    )


def shape_of(shape, dtype):
    return jax.ShapeDtypeStruct(shape, dtype)


class Flights:
    def __init__(self):
        self.waiting = []
        self.flying = []

    def add(self, steps, lengths):
        job = {"steps": steps, "lengths": list(lengths), "result": None}
        self.advance(job, None)
        return job

    def advance(self, job, came):
        try:
            sends = job["steps"].send(came) if came is not None else next(job["steps"])
        except StopIteration as stop:
            job["result"] = stop.value
            return
        length = job["lengths"].pop(0) if job["lengths"] else 1
        self.waiting.append((job, sends, length))

    def depart(self):
        for job, sends, length in self.waiting:
            came = [lax.ppermute(array, AXES, pairs) for array, pairs in sends]
            self.flying.append([job, came, length])
        self.waiting = []

    def run(self, kernel, operand, *others):
        arrays = [array for _, sends, _ in self.waiting for array, _ in sends]
        if arrays:
            operand, arrays = lax.optimization_barrier((operand, arrays))
            left = iter(arrays)
            self.waiting = [
                (job, [(next(left), pairs) for _, pairs in sends], length)
                for job, sends, length in self.waiting
            ]
        self.depart()
        out = kernel(operand, *others)
        for flight in self.flying:
            flight[2] -= 1
        landed = [flight for flight in self.flying if flight[2] <= 0]
        self.flying = [flight for flight in self.flying if flight[2] > 0]
        if landed:
            out, came = lax.optimization_barrier((out, [flight[1] for flight in landed]))
            for flight, got in zip(landed, came):
                self.advance(flight[0], got)
        return out

    def finish(self, turns=None):
        turn = 0
        while (self.waiting or self.flying) and turn != turns:
            turn += 1
            self.depart()
            for flight in self.flying:
                flight[2] -= 1
            landed = [flight for flight in self.flying if turns is None or flight[2] <= 0]
            self.flying = [flight for flight in self.flying if not (turns is None or flight[2] <= 0)]
            cames = lax.optimization_barrier([flight[1] for flight in landed])
            for flight, came in zip(landed, cames):
                self.advance(flight[0], came)


def bit_groups(mesh):
    inner = int(math.log2(mesh.shape["fsdp"]))
    outer = int(math.log2(mesh.shape["dp"]))
    rest = [list(range(b, min(b + 2, inner))) for b in range(1, inner, 2)]
    return [0], list(range(inner, inner + outer)), rest


def position(me, bits):
    spot = 0
    for place, bit in enumerate(bits):
        spot = spot + ((me >> bit) & 1) * (1 << place)
    return spot


def partners(count, bits):
    swaps = []
    for step in range(1, 1 << len(bits)):
        mask = 0
        for place, bit in enumerate(bits):
            if (step >> place) & 1:
                mask |= 1 << bit
        swaps.append((step, [(i, i ^ mask) for i in range(count)]))
    return swaps


def gather_steps(shard, mesh, groups):
    count = mesh.size
    me = lax.axis_index(AXES)
    bits = int(math.log2(count))
    rows, columns = shard.shape
    held = shard.reshape((1,) * bits + (rows, columns))
    for group in groups:
        swaps = partners(count, group)
        came = yield [(held, pairs) for _, pairs in swaps]
        shape = list(held.shape)
        for bit in group:
            shape[bits - 1 - bit] = 2
        whole = jnp.zeros(shape, shard.dtype)
        for (step, _), got in zip([(0, None)] + swaps, [held] + came):
            start = [0] * len(shape)
            for place, bit in enumerate(group):
                start[bits - 1 - bit] = ((me >> bit) & 1) ^ ((step >> place) & 1)
            whole = lax.dynamic_update_slice(whole, got, start)
        held = whole
    return held.reshape(count * rows, columns)


def pick(array, axis, index):
    return lax.dynamic_slice_in_dim(array, index, 1, axis)


def total(terms, axis, index, kind):
    return sum(pick(term, axis, index).astype(f32) for term in terms).astype(kind)


def sum_steps(parts, mesh, kind):
    count = mesh.size
    core, outer, rest = bit_groups(mesh)
    me = lax.axis_index(AXES)
    rows, columns = parts.shape[0] // count, parts.shape[1]
    rest_size = mesh.shape["fsdp"] // 2
    held = parts.reshape(mesh.shape["dp"], rest_size, 2, rows, columns)
    spot = position(me, core)
    (got,) = yield [(pick(held, 2, spot ^ 1).astype(kind), partners(count, core)[0][1])]
    terms = [pick(held, 2, spot), got]
    split = 2 if len(outer) == 2 and columns % 256 == 0 else 1
    width = columns // split
    shape = (2,) * len(outer) + (rest_size, 1, rows, width)
    pieces = []
    for piece in range(split):
        own = [term[..., piece * width : (piece + 1) * width].reshape(shape) for term in terms]
        order = list(range(len(outer)))
        pieces.append((own, order if piece == 0 else order[::-1]))
    for turn in range(len(outer)):
        sends = []
        for own, order in pieces:
            axis = order[turn]
            bit = outer[len(outer) - 1 - axis]
            mine = position(me, [bit])
            sends.append((total(own, axis, mine ^ 1, kind), partners(count, [bit])[0][1]))
        came = yield sends
        pieces = [
            ([pick(term, order[turn], position(me, [outer[len(outer) - 1 - order[turn]]])) for term in own] + [got], order)
            for (own, order), got in zip(pieces, came)
        ]
    left = rest_size
    pieces = [[term.reshape(rest_size, rows, width) for term in own] for own, _ in pieces]
    for bits in reversed(rest):
        size = 1 << len(bits)
        left //= size
        pieces = [[term.reshape(size, left, rows, width) for term in own] for own in pieces]
        spot = position(me, bits)
        swaps = partners(count, bits)
        sends = [
            (jnp.concatenate([total(own, 0, spot ^ step, kind) for own in pieces], -1), pairs)
            for step, pairs in swaps
        ]
        came = yield sends
        pieces = [
            [pick(term, 0, spot) for term in own]
            + [got[..., place * width : (place + 1) * width] for got in came]
            for place, own in enumerate(pieces)
        ]
    sums = [sum(term.astype(f32) for term in own).reshape(rows, width) for own in pieces]
    return jnp.concatenate(sums, -1)


def plane_sum_kernel(where, *refs, parts):
    keeps, cames, outs = refs[:parts], refs[parts : 2 * parts], refs[2 * parts :]
    for step, out in enumerate(outs):
        place = where[1] ^ step
        start = 0
        for keep, came in zip(keeps, cames):
            lanes = slice(start, start + keep.shape[-1])
            start += keep.shape[-1]
            out[:, lanes] = keep[place] + came[place]


def plane_sum(where, keeps, cames, size):
    blocks, rows, _ = keeps[0].shape
    left = blocks // size
    columns = sum(keep.shape[2] for keep in keeps)
    arrays = [array.reshape(size, left, rows, array.shape[2]) for array in (*keeps, *cames)]
    part = pl.BlockSpec((None, rows, columns), lambda j, where: (j, 0, 0))
    return pl.pallas_call(
        functools.partial(plane_sum_kernel, parts=len(keeps)),
        grid_spec=pltpu.PrefetchScalarGridSpec(
            num_scalar_prefetch=1,
            grid=(left,),
            in_specs=[
                pl.BlockSpec((size, None, rows, array.shape[3]), lambda j, where: (0, j, 0, 0))
                for array in arrays
            ],
            out_specs=[part] * size,
        ),
        out_shape=[shape_of((left, rows, columns), bf16)] * size,
        compiler_params=params(1),
        cost_estimate=cost(blocks * rows * columns, blocks * rows * columns * 6),
        name="plane_sum",
    )(where, *arrays)


def line_sum_kernel(where, *refs, sizes):
    outs = refs[sum(sizes) :]
    for step, out in enumerate(outs):
        place = where[2] ^ step
        at = start = 0
        for size in sizes:
            terms = refs[at : at + size]
            at += size
            lanes = slice(start, start + terms[0].shape[2])
            start += terms[0].shape[2]
            out[:, lanes] = sum(term[place].astype(f32) for term in terms).astype(out.dtype)


def line_sum(where, groups):
    size, rows, _ = groups[0][0].shape
    columns = sum(group[0].shape[2] for group in groups)
    arrays = [array for group in groups for array in group]
    return pl.pallas_call(
        functools.partial(line_sum_kernel, sizes=[len(group) for group in groups]),
        grid_spec=pltpu.PrefetchScalarGridSpec(
            num_scalar_prefetch=1,
            grid=(1,),
            in_specs=[once(array.shape) for array in arrays],
            out_specs=[once((rows, columns))] * size,
        ),
        out_shape=[shape_of((rows, columns), f32)] + [shape_of((rows, columns), bf16)] * (size - 1),
        compiler_params=params(1),
        cost_estimate=cost(),
        name="line_sum",
    )(where, *arrays)


def send_sum_kernel(where, *refs, sizes):
    at = 0
    for size, out in zip(sizes, refs[sum(sizes) :]):
        out[...] = sum(term[...].astype(f32) for term in refs[at : at + size]).astype(out.dtype)
        at += size


def fold_first(where, keep, came):
    _, _, left, rows, columns = keep.shape
    cut = columns // 2
    spec_a = pl.BlockSpec((None, 2, None, rows, cut), lambda j, where: ((where[1] // 2) ^ 1, 0, j, 0, 0))
    spec_b = pl.BlockSpec((2, None, None, rows, cut), lambda j, where: (0, (where[1] % 2) ^ 1, j, 0, 1))
    return pl.pallas_call(
        functools.partial(send_sum_kernel, sizes=[2, 2]),
        grid_spec=pltpu.PrefetchScalarGridSpec(
            num_scalar_prefetch=1,
            grid=(left,),
            in_specs=[spec_a, spec_a, spec_b, spec_b],
            out_specs=[pl.BlockSpec((2, None, rows, cut), lambda j, where: (0, j, 0, 0))] * 2,
        ),
        out_shape=[shape_of((2, left, rows, cut), bf16)] * 2,
        compiler_params=params(1),
        cost_estimate=cost(),
        name="fold_first",
    )(where, keep, came, keep, came)


def fold_second(where, keep, came, came_a, came_b):
    _, _, left, rows, columns = keep.shape
    cut = columns // 2
    spec_a = pl.BlockSpec(
        (None, None, None, rows, cut), lambda j, where: (where[1] // 2, (where[1] % 2) ^ 1, j, 0, 0)
    )
    spec_b = pl.BlockSpec(
        (None, None, None, rows, cut), lambda j, where: ((where[1] // 2) ^ 1, where[1] % 2, j, 0, 1)
    )
    half_a = pl.BlockSpec((None, None, rows, cut), lambda j, where: ((where[1] % 2) ^ 1, j, 0, 0))
    half_b = pl.BlockSpec((None, None, rows, cut), lambda j, where: ((where[1] // 2) ^ 1, j, 0, 0))
    return pl.pallas_call(
        functools.partial(send_sum_kernel, sizes=[3, 3]),
        grid_spec=pltpu.PrefetchScalarGridSpec(
            num_scalar_prefetch=1,
            grid=(left,),
            in_specs=[spec_a, spec_a, half_a, spec_b, spec_b, half_b],
            out_specs=[pl.BlockSpec((None, rows, cut), lambda j, where: (j, 0, 0))] * 2,
        ),
        out_shape=[shape_of((left, rows, cut), bf16)] * 2,
        compiler_params=params(1),
        cost_estimate=cost(),
        name="fold_second",
    )(where, keep, came, came_a, keep, came, came_b)


def line_first_kernel(where, *refs):
    *terms, keep, send = refs
    fast = where[2] % 2
    cut = terms[0].shape[-1]
    for slow in range(2):
        for place, out in ((slow * 2 + fast, keep), (slow * 2 + (fast ^ 1), send)):
            for half in range(2):
                own = terms[4 * half : 4 * half + 4]
                lanes = slice(half * cut, (half + 1) * cut)
                out[slow, :, lanes] = sum(term[place].astype(f32) for term in own).astype(out.dtype)


def line_first(where, keep, came, came_a, came_b, last_a, last_b):
    _, _, size, rows, columns = keep.shape
    cut = columns // 2
    whole = lambda half: pl.BlockSpec(
        (None, None, size, rows, cut), lambda j, where: (where[1] // 2, where[1] % 2, 0, 0, half)
    )
    half_a = pl.BlockSpec((None, size, rows, cut), lambda j, where: (where[1] % 2, 0, 0, 0))
    half_b = pl.BlockSpec((None, size, rows, cut), lambda j, where: (where[1] // 2, 0, 0, 0))
    last = pl.BlockSpec((size, rows, cut), lambda j, where: (0, 0, 0))
    return pl.pallas_call(
        line_first_kernel,
        grid_spec=pltpu.PrefetchScalarGridSpec(
            num_scalar_prefetch=1,
            grid=(1,),
            in_specs=[whole(0), whole(0), half_a, last, whole(1), whole(1), half_b, last],
            out_specs=[once((size // 2, rows, columns))] * 2,
        ),
        out_shape=[shape_of((size // 2, rows, columns), bf16)] * 2,
        compiler_params=params(1),
        cost_estimate=cost(),
        name="line_first",
    )(where, keep, came, came_a, last_a, keep, came, came_b, last_b)


def swap_steps(send, mesh):
    core, _, _ = bit_groups(mesh)
    (came,) = yield [(send, partners(mesh.size, core)[0][1])]
    return came


def fast_sum_steps(keeps, cames, where, mesh):
    count = mesh.size
    _, outer, rest = bit_groups(mesh)
    own, *sends = plane_sum(where, keeps, cames, 1 << len(outer))
    came = yield [(array, pairs) for array, (_, pairs) in zip(sends, partners(count, outer))]
    own, *sends = line_sum(where, [[own, *came]])
    came = yield [(array, pairs) for array, (_, pairs) in zip(sends, partners(count, rest[0]))]
    return own + sum(array.astype(f32) for array in came)


def fold_sum_steps(keep, send, where, mesh):
    count = mesh.size
    core, outer, rest = bit_groups(mesh)
    (came,) = yield [(send, partners(count, core)[0][1])]
    shape = (2, 2, 1 << len(rest[0]), keep.shape[0] * 2 // count, keep.shape[1])
    keep, came = keep.reshape(shape), came.reshape(shape)
    fast, slow = (partners(count, [bit])[0][1] for bit in outer)
    send_a, send_b = fold_first(where, keep, came)
    came_a, came_b = yield [(send_a, slow), (send_b, fast)]
    send_a, send_b = fold_second(where, keep, came, came_a, came_b)
    last_a, last_b = yield [(send_a, fast), (send_b, slow)]
    keep, send = line_first(where, keep, came, came_a, came_b, last_a, last_b)
    (came,) = yield [(send, partners(count, [rest[0][0]])[0][1])]
    me = lax.axis_index(AXES)
    spot = position(me, [rest[0][1]])
    both = [keep, came]
    (last,) = yield [(total(both, 0, spot ^ 1, bf16), partners(count, [rest[0][1]])[0][1])]
    done = (total(both, 0, spot, f32) + last.astype(f32)).reshape(2, shape[3] // 2, shape[4])
    spot = position(me, core)
    (came,) = yield [(pick(done, 0, spot ^ 1), partners(count, core)[0][1])]
    own, came = pick(done, 0, spot)[0], came[0]
    return jnp.where(spot == 0, own, came), jnp.where(spot == 0, came, own)


def small_sum_steps(parts, mesh):
    count = mesh.size
    core, outer, rest = bit_groups(mesh)
    groups = [core, outer, *reversed(rest)]
    order = [outer, *reversed(rest), core]
    me = lax.axis_index(AXES)
    columns = parts.shape[1]
    held = parts.reshape([1 << len(bits) for bits in order] + [columns])
    for bits in groups:
        axis = order.index(bits)
        spot = position(me, bits)
        swaps = partners(count, bits)
        came = yield [(pick(held, axis, spot ^ step), pairs) for step, pairs in swaps]
        held = pick(held, axis, spot) + sum(came)
    return held.reshape(columns)


def cut_by_core(mesh):
    _, outer, rest = bit_groups(mesh)
    return len(outer) == 2 and len(rest) == 1 and len(rest[0]) == 2


def store_cut(core, outs, lanes, value, rows):
    if len(outs) == 1:
        outs[0][:, lanes] = value.astype(bf16)
        return
    keep, send = outs
    for parity in range(2):
        @pl.when(core == parity)
        def _():
            for device in range(value.shape[0] // rows):
                out = keep if device % 2 == parity else send
                out[device // 2, :, lanes] = value[device * rows : (device + 1) * rows, :].astype(bf16)


def cut_shapes(width, columns, chunk, index, rows):
    if not rows:
        spec = pl.BlockSpec((width, chunk), lambda j, *_: (0, index(j)))
        return [spec], [shape_of((width, columns), bf16)]
    blocks = width // rows // 2
    spec = pl.BlockSpec((blocks, rows, chunk), lambda j, *_: (0, 0, index(j)))
    return [spec] * 2, [shape_of((blocks, rows, columns), bf16)] * 2


def normalize(values):
    center = values - jnp.mean(values, -1, keepdims=True)
    scale = lax.rsqrt(jnp.mean(center * center, -1, keepdims=True) + 1e-05)
    return center * scale, scale


def norm_back(grad, gain, unit, scale):
    inner = grad * gain
    return scale * (
        inner
        - jnp.mean(inner, -1, keepdims=True)
        - unit * jnp.mean(inner * unit, -1, keepdims=True)
    )


def gelu_parts(u):
    phi = 0.5 + 0.5 * lax.erf(u * 0.7071067811865476)
    slope = phi + u * (0.3989422804014327 * jnp.exp2((u * u) * (-0.5 * LOG2E)))
    return u * phi, slope


def column_sum(values):
    return jnp.sum(values, 0, keepdims=True)


def accumulate(ref, value, first):
    @pl.when(first)
    def _():
        ref[...] = value

    @pl.when(jnp.logical_not(first))
    def _():
        ref[...] += value


def two_heads(block, padded):
    seq = block.shape[0]
    first = lax.broadcasted_iota(jnp.int32, block.shape, 1) < 64
    zero = jnp.zeros_like(block)
    pad = jnp.zeros((padded - seq, 128), block.dtype)
    return jnp.concatenate(
        [jnp.where(first, block, zero), pad, jnp.where(first, zero, block), pad], 0
    )


def attend_kernel(valid, *refs, tile, padded, first, pairs):
    if first:
        tokens, gain, shift, weight, bias, normed, joined, mixed, raised_out, inverse = refs
    else:
        (
            normed, weight, bias, tokens, mixed_first, bias_out, gain, shift,
            joined, mixed, raised_out, inverse, middle, normed_two,
        ) = refs
    seq, span = joined.shape
    for start in range(0, seq, tile):
        rows = slice(start, start + tile)
        if first:
            unit, _ = normalize(tokens[rows, :].astype(f32))
            low = (unit * gain[...] + shift[...]).astype(bf16)
            normed[rows, :] = low
        else:
            low = normed[rows, :]
        joined[rows, :] = (dot(low, weight[:, :span], NN) + bias[...]).astype(bf16)

    column = lax.broadcasted_iota(jnp.int32, (1, padded), 1)
    mask = jnp.where(column < valid[pl.program_id(0)], 0.0, -1e30).astype(f32)
    places = [(pair, start) for pair in range(pairs) for start in range(0, seq, ATILE)]
    keys, values = {}, {}
    row = lax.broadcasted_iota(jnp.int32, (2 * padded, 128), 0)
    lane = lax.broadcasted_iota(jnp.int32, (2 * padded, 128), 1)
    ones = jnp.where((row < padded) == (lane < 64), 1.0, 0.0).astype(bf16)

    def scores_at(pair, start):
        if pair not in keys:
            at = pair * 384
            keys[pair] = two_heads(joined[:, at + 128 : at + 256], padded)
            values[pair] = jnp.concatenate([two_heads(joined[:, at + 256 : at + 384], padded), ones], 1)
        return dot(joined[start : start + ATILE, pair * 384 : pair * 384 + 128], keys[pair], NT)

    ahead = [scores_at(*place) for place in places[:AHEAD]]
    for index, (pair, start) in enumerate(places):
        rows = slice(start, start + ATILE)
        if index + AHEAD < len(places):
            ahead.append(scores_at(*places[index + AHEAD]))
        scores = ahead.pop(0)
        halves = []
        for head in range(2):
            part = scores[:, head * padded : (head + 1) * padded] * (0.125 * LOG2E) + mask
            halves.append(jnp.exp2(part - jnp.max(part, 1, keepdims=True)).astype(bf16))
        raised = jnp.concatenate(halves, 1)
        raised_out[pair, rows, :] = raised
        both = dot(raised, values[pair], NN)
        scale = 1.0 / both[:, 128:]
        inverse[rows, pair * 128 : (pair + 1) * 128] = scale
        mixed[rows, pair * 128 : (pair + 1) * 128] = (both[:, :128] * scale).astype(bf16)
    if first:
        return
    width = tokens.shape[1]
    for start in range(0, seq, tile):
        rows = slice(start, start + tile)
        value = tokens[rows, :].astype(f32) + bias_out[...]
        value = value + dot(mixed_first[rows, :], weight[: width // 2, -width:], NN)
        value = value + dot(mixed[rows, :], weight[width // 2 :, -width:], NN)
        middle[rows, :] = value
        unit, _ = normalize(value)
        normed_two[rows, :] = (unit * gain[...] + shift[...]).astype(bf16)


def attend(start, valid, weight, bias, seq, norm=None, after=None):
    rows, width = start.shape
    span = bias.shape[1]
    pairs = span // 384
    items = rows // seq
    padded = -(-seq // 128) * 128
    row = lambda w: pl.BlockSpec((seq, w), lambda i, *_: (i, 0))
    one = once((1, width))
    main = [once(weight.shape), once((1, span))]
    if norm:
        specs, arrays = [row(width), one, one, *main], [start, *norm, weight, bias]
    else:
        specs = [row(width), *main, row(width), row(width // 2), one, one, one]
        arrays = [start, weight, bias, *after]
    outs = [
        row(span),
        row(span // 3),
        pl.BlockSpec((None, pairs, seq, 2 * padded), lambda i, *_: (i, 0, 0, 0)),
        row(span // 3),
    ]
    shapes = [
        shape_of((rows, span), bf16),
        shape_of((rows, span // 3), bf16),
        shape_of((items, pairs, seq, 2 * padded), bf16),
        shape_of((rows, span // 3), f32),
    ]
    if norm:
        outs, shapes = [row(width)] + outs, [shape_of((rows, width), bf16)] + shapes
    else:
        outs += [row(width)] * 2
        shapes += [shape_of((rows, width), f32), shape_of((rows, width), bf16)]
    return pl.pallas_call(
        functools.partial(attend_kernel, tile=tile_of(seq), padded=padded, first=bool(norm), pairs=pairs),
        grid_spec=pltpu.PrefetchScalarGridSpec(
            num_scalar_prefetch=1, grid=(items,), in_specs=specs, out_specs=outs
        ),
        out_shape=shapes,
        compiler_params=params(1),
        cost_estimate=cost(),
        name="attend",
    )(valid, *arrays)


def attend_back_kernel(where, *refs, pairs, extra, cut):
    lists = [refs[kind * pairs : (kind + 1) * pairs] for kind in range(5)]
    joined, mixed_grad, mixed, raised, inverse = lists
    normed, *rest = refs[5 * pairs :]
    if extra:
        mixed_a, mixed_b, low_grad, joined_grad, column, *outs, held, scaled, total, total_out = rest
    else:
        joined_grad, column, *outs, held, scaled, total = rest
    item = pl.program_id(0)
    seq, span = joined_grad.shape
    padded = raised[0].shape[1] // 2
    tile = BTILE if seq % BTILE == 0 else seq
    first = lax.broadcasted_iota(jnp.int32, (tile, 128), 1) < 64
    places = [(pair, start) for pair in range(pairs) for start in range(0, seq, tile)]
    keys, values = {}, {}

    def prob_grad_at(pair, start):
        if pair not in keys:
            keys[pair] = two_heads(joined[pair][:, 128:256], padded)
            values[pair] = two_heads(joined[pair][:, 256:], padded)
        rows = slice(start, start + tile)
        grad = (mixed_grad[pair][rows, :].astype(f32) * inverse[pair][rows, :]).astype(bf16)
        scaled[pair, rows, :] = grad
        return grad, dot(grad, values[pair], NT)

    def own_half(both):
        return jnp.concatenate([both[:64, :padded], both[64:, padded:]], 0).T[:seq]

    ahead = [prob_grad_at(*place) for place in places[:BAHEAD]]
    for index, (pair, start) in enumerate(places):
        rows = slice(start, start + tile)
        at = pair * 384
        if index + BAHEAD < len(places):
            ahead.append(prob_grad_at(*places[index + BAHEAD]))
        grad, prob_grad = ahead.pop(0)
        product = grad.astype(f32) * mixed[pair][rows, :].astype(f32)
        zero = jnp.zeros_like(product)
        halves = []
        for head in range(2):
            own = jnp.where(first, product, zero) if head == 0 else jnp.where(first, zero, product)
            centre = jnp.sum(own, 1, keepdims=True)
            half = slice(head * padded, (head + 1) * padded)
            halves.append((raised[pair][rows, half].astype(f32) * (prob_grad[:, half] - centre)).astype(bf16))
        score_grad = jnp.concatenate(halves, 1)
        held[rows, :] = score_grad
        joined_grad[rows, at : at + 128] = (dot(score_grad, keys[pair], NN) * 0.125).astype(bf16)
        if start + tile == seq:
            joined_grad[:, at + 128 : at + 256] = (
                own_half(dot(joined[pair][:, :128].T, held[...], NN)) * 0.125
            ).astype(bf16)
            joined_grad[:, at + 256 : at + 384] = own_half(
                dot(scaled[pair].T, raised[pair][...], NN)
            ).astype(bf16)

    value = joined_grad[...]
    accumulate(total, dot(normed[...], value, TN), item == 0)
    accumulate(column, column_sum(value.astype(f32)), item == 0)
    if extra:
        both = [dot(mixed_a[...], low_grad[...], TN), dot(mixed_b[...], low_grad[...], TN)]
        accumulate(total_out, jnp.concatenate(both, 0), item == 0)

    @pl.when(item == pl.num_programs(0) - 1)
    def _():
        store_cut(where[0], outs, slice(0, span), total[...], cut)
        if extra:
            store_cut(where[0], outs, slice(span, span + total_out.shape[1]), total_out[...], cut)


def attend_back(mixed_grad, where, joined, mixed, raised, inverse, normed, seq, part, chosen, cut, others=()):
    rows, width = normed.shape
    items, in_part, _, keys = raised.shape
    pairs = len(chosen)
    span = 384 * pairs
    row = lambda w, off=0: pl.BlockSpec((seq, w), lambda i, *_: (i, off))
    each = lambda w, off=0: [row(w, off + pair) for pair in chosen]
    weights = [
        pl.BlockSpec((None, None, seq, keys), functools.partial(lambda at, i, *_: (i, at, 0, 0), pair))
        for pair in chosen
    ]
    columns = span + (width if others else 0)
    specs, shapes = cut_shapes(width, columns, columns, lambda j: 0, cut)
    return pl.pallas_call(
        functools.partial(attend_back_kernel, pairs=pairs, extra=bool(others), cut=cut),
        grid_spec=pltpu.PrefetchScalarGridSpec(
            num_scalar_prefetch=1,
            grid=(items,),
            in_specs=[
                *each(384), *each(128, part * in_part), *each(128), *weights, *each(128), row(width)
            ]
            + [row(array.shape[1]) for array in others],
            out_specs=[row(span), pl.BlockSpec((1, span), lambda i, *_: (0, 0))] + specs,
            scratch_shapes=[
                pltpu.VMEM((seq, keys), bf16),
                pltpu.VMEM((pairs, seq, 128), bf16),
                pltpu.VMEM((width, span), f32),
            ]
            + ([pltpu.VMEM((width, width), f32)] if others else []),
        ),
        out_shape=[shape_of((rows, span), bf16), shape_of((1, span), f32)] + shapes,
        compiler_params=params(1),
        cost_estimate=cost(),
        name="attend_back",
    )(
        where, *[joined] * pairs, *[mixed_grad] * pairs, *[mixed] * pairs, *[raised] * pairs,
        *[inverse] * pairs, normed, *others,
    )


def mlp_kernel(
    valid, where, normed, cotangent, up, down, bias_up,
    active, hidden_grad, up_sum, *rest, seq, tile, cut,
):
    *outs, grad = rest
    rows, width = normed.shape

    @pl.when(pl.program_id(0) == 0)
    def _():
        place = lax.broadcasted_iota(jnp.int32, (seq, 1), 0)
        for item in range(rows // seq):
            span = slice(item * seq, (item + 1) * seq)
            grad[span, :] = jnp.where(place < valid[item], cotangent[span, :].astype(f32), 0.0).astype(bf16)

    def ahead_of(start):
        span = slice(start, start + MTILE)
        return dot(normed[span, :], up[...], NN), dot(grad[span, :], down[...], NT)

    column = jnp.zeros(up_sum.shape, f32)
    starts = list(range(0, rows, MTILE))
    ahead = [ahead_of(start) for start in starts[:MAHEAD]]
    for index, start in enumerate(starts):
        span = slice(start, start + MTILE)
        if index + MAHEAD < len(starts):
            ahead.append(ahead_of(starts[index + MAHEAD]))
        hidden, wide = ahead.pop(0)
        value, slope = gelu_parts(hidden + bias_up[...])
        low = (slope * wide).astype(bf16)
        active[span, :] = value.astype(bf16)
        hidden_grad[span, :] = low
        column = column + column_sum(low.astype(f32))
    up_sum[...] = column
    first = dot(normed[...], hidden_grad[...], TN).astype(bf16)
    second = dot(active[...], grad[...], TN).astype(bf16)
    if cut:
        keep, send = outs
        for core in range(2):
            @pl.when(where[0] == core)
            def _():
                (keep, send)[core][...] = first
                (send, keep)[core][...] = second
    else:
        outs[0][:, :width] = first
        outs[0][:, width:] = second


def mlp(normed, valid, where, cotangent, both, bias_up, seq, cut):
    rows, width = normed.shape
    wide = both.shape[1] // 2
    chunks = wide // width
    whole = once((rows, width))
    square = lambda off: pl.BlockSpec((width, width), lambda j, *_: (0, j + off))
    row = pl.BlockSpec((rows, width), lambda j, *_: (0, j))
    one = pl.BlockSpec((1, width), lambda j, *_: (0, j))
    if cut:
        specs = [pl.BlockSpec((width, width), lambda j, *_: (0, j))] * 2
        shapes = [shape_of((width, wide), bf16)] * 2
    else:
        specs, shapes = cut_shapes(width, 2 * wide, 2 * width, lambda j: j, 0)
    return pl.pallas_call(
        functools.partial(mlp_kernel, seq=seq, tile=tile_of(seq), cut=cut),
        grid_spec=pltpu.PrefetchScalarGridSpec(
            num_scalar_prefetch=2,
            grid=(chunks,),
            in_specs=[whole, whole, square(0), square(chunks), one],
            out_specs=[row, row, one] + specs,
            scratch_shapes=[pltpu.VMEM((rows, width), bf16)],
        ),
        out_shape=[
            shape_of((rows, width * chunks), bf16),
            shape_of((rows, width * chunks), bf16),
            shape_of((1, width * chunks), f32),
        ]
        + shapes,
        compiler_params=params(1),
        cost_estimate=cost(),
        name="mlp",
    )(valid, where, normed, cotangent, both, both, bias_up)


def block_out_kernel(valid, active, downs, middle, bias_down, *rest, seq, begin):
    block_out = rest[-1]
    tile, width = middle.shape
    step = pl.program_id(0) + begin // tile
    place = lax.broadcasted_iota(jnp.int32, (tile, 1), 0) + lax.rem(step, seq // tile) * tile
    value = middle[...] + bias_down[...]
    for at in range(0, downs.shape[1], width):
        value = value + dot(active[:, at : at + width], downs[:, at : at + width], NN)
    block_out[...] = jnp.where(place < valid[step // (seq // tile)], value, 0.0).astype(bf16)


def half_of(both, second):
    width, columns = both.shape
    return pl.BlockSpec(
        (width, columns // 2), lambda j, *_: (0, second), pipeline_mode=pl.Buffered(buffer_count=1)
    )


def block_out_of(middle, valid, active, both, bias_down, seq, begin, end, before=None):
    rows, width = middle.shape
    tile = BOT if seq % BOT == 0 else seq
    skip = begin // tile
    row = lambda w: pl.BlockSpec((tile, w), lambda j, *_: (j + skip, 0))
    specs = [row(active.shape[1]), half_of(both, 1), row(width), once((1, width))]
    arrays = [active, both, middle, bias_down]
    aliases = {}
    if before is not None:
        aliases = {len(arrays) + 1: 0}
        specs.append(pl.BlockSpec(memory_space=pl.ANY))
        arrays.append(before)
    return pl.pallas_call(
        functools.partial(block_out_kernel, seq=seq, begin=begin),
        grid_spec=pltpu.PrefetchScalarGridSpec(
            num_scalar_prefetch=1,
            grid=((end - begin) // tile,),
            in_specs=specs,
            out_specs=row(width),
        ),
        out_shape=shape_of((rows, width), bf16),
        input_output_aliases=aliases,
        compiler_params=params(1),
        cost_estimate=cost(),
        name="block_out",
    )(valid, *arrays)


def middle_back_kernel(
    valid, hidden_grad, ups, middle, cotangent, gain, weight,
    low_grad, mixed_grad, gain_sum, shift_sum, bias_sum, down_sum, *, seq, sub,
):
    step = pl.program_id(0)
    tile, width = middle.shape
    each = seq // tile
    starts = list(range(0, tile, sub))
    ahead = [dot(hidden_grad[:sub, :], ups[...], NT)]
    sums = [jnp.zeros((1, width), f32)] * 4
    for index, start in enumerate(starts):
        rows = slice(start, start + sub)
        if index + 1 < len(starts):
            ahead.append(dot(hidden_grad[start + sub : start + 2 * sub, :], ups[...], NT))
        grad = ahead.pop(0)
        unit, scale = normalize(middle[rows, :])
        place = lax.broadcasted_iota(jnp.int32, (sub, 1), 0) + (lax.rem(step, each) * tile + start)
        kept = jnp.where(place < valid[step // each], cotangent[rows, :].astype(f32), 0.0)
        low = (kept + norm_back(grad, gain[...], unit, scale)).astype(bf16)
        low_grad[rows, :] = low
        mixed_grad[rows, :] = dot(low, weight[:, -width:], NT).astype(bf16)
        terms = (grad * unit, grad, low.astype(f32), kept)
        sums = [before + column_sum(term) for before, term in zip(sums, terms)]
    for ref, value in zip((gain_sum, shift_sum, bias_sum, down_sum), sums):
        accumulate(ref, value, step == 0)


def middle_back(middle, valid, hidden_grad, both, cotangent, gain, weight, seq):
    rows, width = middle.shape
    tile = LTILE if seq % LTILE == 0 else seq
    sub = LSUB if tile % LSUB == 0 else tile
    row = lambda w: pl.BlockSpec((tile, w), lambda j, *_: (j, 0))
    one = pl.BlockSpec((1, width), lambda j, *_: (0, 0))
    return pl.pallas_call(
        functools.partial(middle_back_kernel, seq=seq, sub=sub),
        grid_spec=pltpu.PrefetchScalarGridSpec(
            num_scalar_prefetch=1,
            grid=(rows // tile,),
            in_specs=[
                row(hidden_grad.shape[1]), half_of(both, 0), row(width), row(width),
                once((1, width)), once(weight.shape),
            ],
            out_specs=[row(width), row(width)] + [one] * 4,
        ),
        out_shape=[shape_of((rows, width), bf16)] * 2 + [shape_of((1, width), f32)] * 4,
        compiler_params=params(1),
        cost_estimate=cost(),
        name="middle_back",
    )(valid, hidden_grad, both, middle, cotangent, gain, weight)


def input_back_kernel(*refs, spans, sub):
    grads = refs[: len(spans)]
    weights = refs[len(spans) : len(spans) + 2]
    tokens, low_grad, gain, input_grad, gain_sum, shift_sum = refs[len(spans) + 2 :]
    tile, width = tokens.shape

    def ahead_of(start):
        rows = slice(start, start + sub)
        terms = [
            dot(grad[rows, :], weights[which][:, lanes], NT) for grad, (which, lanes) in zip(grads, spans)
        ]
        return sum(terms[1:], terms[0])

    starts = list(range(0, tile, sub))
    ahead = [ahead_of(0)]
    sums = [jnp.zeros((1, width), f32)] * 2
    for index, start in enumerate(starts):
        rows = slice(start, start + sub)
        if index + 1 < len(starts):
            ahead.append(ahead_of(start + sub))
        grad = ahead.pop(0)
        unit, scale = normalize(tokens[rows, :].astype(f32))
        sums = [before + column_sum(term) for before, term in zip(sums, (grad * unit, grad))]
        full = low_grad[rows, :].astype(f32) + norm_back(grad, gain[...], unit, scale)
        input_grad[rows, :] = full.astype(bf16)
    for ref, value in zip((gain_sum, shift_sum), sums):
        accumulate(ref, value, pl.program_id(0) == 0)


def input_back(last, others, spans, weights, tokens, low_grad, gain, seq):
    rows, width = tokens.shape
    tile = LTILE if seq % LTILE == 0 else seq
    sub = LSUB if tile % LSUB == 0 else tile
    row = lambda w: pl.BlockSpec((tile, w), lambda i: (i, 0))
    fixed = pl.BlockSpec((1, width), lambda i: (0, 0))
    grads = [*others, last]
    return pl.pallas_call(
        functools.partial(input_back_kernel, spans=spans, sub=sub),
        grid=(rows // tile,),
        in_specs=[row(grad.shape[1]) for grad in grads]
        + [once(weight.shape) for weight in weights]
        + [row(width), row(width), once((1, width))],
        out_specs=[row(width), fixed, fixed],
        out_shape=[shape_of((rows, width), bf16)] + [shape_of((1, width), f32)] * 2,
        compiler_params=params(1),
        cost_estimate=cost(),
        name="input_back",
    )(*grads, *weights, tokens, low_grad, gain)


def local(mesh, tokens, cotangent, group, text_len, qkv_w, out_w, mlp_in, mlp_out, gains, biases):
    items, seq, width = tokens.shape
    rows = items * seq
    count = mesh.size
    share = width // count
    wide = mlp_in.shape[0] // share
    chunks = wide // width
    half = width // 2
    span = 3 * half
    valid = (PATCH_SMALL + (PATCH_LARGE - PATCH_SMALL) * group + text_len).astype(jnp.int32)
    flat = tokens.reshape(rows, width)
    cot = cotangent.reshape(rows, width)
    flights = Flights()
    me = lax.axis_index(AXES)
    core, outer, others = bit_groups(mesh)
    where = jnp.stack([position(me, core), position(me, outer), position(me, others[0])]).astype(jnp.int32)
    cut = share if cut_by_core(mesh) and share % 8 == 0 else 0

    def mlp_sums(arrays):
        if cut:
            return flights.add(fold_sum_steps(*arrays, where, mesh), [])
        return flights.add(sum_steps(arrays[0], mesh, bf16), [])

    def swap(arrays):
        return flights.add(swap_steps(arrays[1], mesh), []) if cut else None

    def sums_after(arrays, swaps):
        if cut:
            keeps, cames = [keep for keep, _ in arrays], [job["result"] for job in swaps]
            return flights.add(fast_sum_steps(keeps, cames, where, mesh), [])
        return flights.add(sum_steps(arrays[0][0], mesh, bf16), [])


    def by_pairs(matrix, part):
        rows = matrix.shape[0]
        cubes = matrix.reshape(rows, 3, 2, half // 128, 128)[:, :, part]
        return cubes.transpose(0, 2, 1, 3).reshape(rows, span)

    def by_kind(part_a, part_b):
        rows = part_a.shape[0]
        cubes = [piece[:, :span].reshape(rows, half // 128, 3, 128) for piece in (part_a, part_b)]
        return jnp.stack(cubes, 1).transpose(0, 3, 1, 2, 4).reshape(rows, 3 * width)

    own_up = mlp_in.reshape(share, count, chunks, share).transpose(0, 2, 1, 3).reshape(share, wide)
    own_down = mlp_out.reshape(chunks, share, width).transpose(1, 0, 2).reshape(share, wide)
    own_both = jnp.concatenate([own_up, own_down], 1)

    own_qkv = qkv_w.reshape(share, 3 * width)
    small = jnp.concatenate([gains, biases])
    small_rows = -(-small.shape[0] // 128)
    padded = jnp.pad(small, (0, small_rows * 128 - small.shape[0])).reshape(small_rows, 128)
    padded = jnp.pad(padded, ((0, share - small_rows), (0, 0)))
    both = lax.all_gather(own_both, AXES, axis=0, tiled=True)
    own_first = jnp.concatenate([by_pairs(own_qkv, 0), padded], 1)
    own_second = jnp.concatenate([by_pairs(own_qkv, 1), out_w.reshape(share, width)], 1)
    singles = [[bit] for group in reversed(others) for bit in reversed(group)]
    job = flights.add(gather_steps(own_first, mesh, [*others, outer, core]), [])
    second_job = flights.add(gather_steps(own_second, mesh, [*singles, outer, core]), [1] * len(singles) + [2])
    flights.finish(len(others) + 2)
    first = job["result"]
    small = first[:, span:].reshape(count, share, 128)[:, :small_rows]
    small = small.reshape(count, small_rows * 128).astype(f32)
    edge = gains.shape[0]
    gain = small[:, :edge].reshape(1, 2 * width)
    bias = small[:, edge : edge + biases.shape[0]].reshape(1, 6 * width + wide)
    gain_one, gain_two = gain[:, :width], gain[:, width:]
    bias_query, bias_value, bias_output, shift_one, shift_two, bias_down = (
        bias[:, p * width : (p + 1) * width] for p in range(6)
    )
    bias_up = bias[:, 6 * width :].reshape(count, chunks, share).transpose(1, 0, 2).reshape(1, wide)
    bias_joined = jnp.concatenate([bias_query, jnp.zeros_like(bias_query), bias_value], 1)
    bias_parts = [by_pairs(bias_joined, part) for part in range(2)]

    normed, joined_a, mixed_a, raised_a, inverse_a = flights.run(
        lambda x: attend(x, valid, first, bias_parts[0], seq, (gain_one, shift_one)), flat
    )
    flights.finish()
    second = second_job["result"]
    joined_b, mixed_b, raised_b, inverse_b, middle, normed_two = attend(
        normed, valid, second, bias_parts[1], seq,
        after=(flat, mixed_a, bias_output, gain_two, shift_two),
    )

    active, hidden_grad, up_sum, *mlp_grads = mlp(
        normed_two, valid, where, cot, both, bias_up, seq, cut
    )
    mlp_job = mlp_sums(mlp_grads)

    low_grad, mixed_grad, gain_two_sum, shift_two_sum, bias_out_sum, down_sum = flights.run(
        lambda x: middle_back(x, valid, hidden_grad, both, cot, gain_two, second, seq), middle
    )
    joined_grad_a, qkv_sum_a, *grads_a = flights.run(
        lambda x: attend_back(
            x, where, joined_a, mixed_a, raised_a, inverse_a, normed, seq, 0, range(half // 128), cut,
            (mixed_a, mixed_b, low_grad),
        ),
        mixed_grad,
    )
    swap_a = swap(grads_a)
    joined_grad_b, qkv_sum_b, *grads_b = flights.run(
        lambda x: attend_back(
            x, where, joined_b, mixed_b, raised_b, inverse_b, normed, seq, 1, range(1), cut
        ),
        mixed_grad,
    )
    sum_a = sums_after([grads_a], [swap_a])
    swap_b = swap(grads_b)
    joined_grad_c, qkv_sum_c, *grads_c = flights.run(
        lambda x: attend_back(
            x, where, joined_b, mixed_b, raised_b, inverse_b, normed, seq, 1, range(1, half // 128), cut
        ),
        mixed_grad,
    )
    swap_c = swap(grads_c)
    spans = ((0, slice(0, span)), (1, slice(0, 384)), (1, slice(384, span)))
    input_grad, gain_one_sum, shift_one_sum = flights.run(
        lambda x: input_back(
            x, [joined_grad_a, joined_grad_b], spans, [first, second], flat, low_grad, gain_one, seq
        ),
        joined_grad_c,
    )
    qkv_sum_b = jnp.concatenate([qkv_sum_b, qkv_sum_c], 1)

    joined_sums = by_kind(qkv_sum_a, qkv_sum_b)
    up_sum = up_sum.reshape(chunks, count, share).transpose(1, 0, 2).reshape(1, wide)
    gain_sums = jnp.concatenate([gain_one_sum, gain_two_sum], 1).reshape(count, edge)
    bias_sums = jnp.concatenate(
        [
            joined_sums[:, :width],
            joined_sums[:, 2 * width :],
            bias_out_sum,
            shift_one_sum,
            shift_two_sum,
            down_sum,
            up_sum,
        ],
        1,
    ).reshape(count, biases.shape[0])
    small = jnp.concatenate([gain_sums, bias_sums], 1)
    if cut:
        small = jnp.pad(small, ((0, 0), (0, small_rows * 128 - small.shape[1])))
        small = small.reshape(count // 2, 2, small_rows, 128)
        spot = position(me, core)
        small = [
            jnp.pad(pick(small, 1, place)[:, 0], ((0, 0), (0, share - small_rows), (0, 0))).astype(bf16)
            for place in (spot, spot ^ 1)
        ]
        swap_small = swap(small)
    else:
        small_job = flights.add(small_sum_steps(small, mesh), [])
        grads_b = [jnp.concatenate([grads_b[0], grads_c[0]], 1)]
        sum_b = sums_after([grads_b], [None])
    cuts = [0, items // 2 * seq, rows]
    block_out = None
    for begin, end in zip(cuts, cuts[1:]):
        if begin < end:
            block_out = flights.run(
                lambda x: block_out_of(
                    x, valid, active, both, bias_down, seq, begin, end, block_out
                ),
                middle,
            )
            if cut and begin == 0:
                sum_b = sums_after([grads_b, grads_c, small], [swap_b, swap_c, swap_small])
    flights.finish()
    total_a, total_b = sum_a["result"], sum_b["result"]
    if cut:
        small_total = total_b[:small_rows, span:].reshape(-1)
        small_total = small_total[: edge + biases.shape[0]]
    else:
        small_total = small_job["result"]
    if cut:
        up_total, down_total = mlp_job["result"]
    else:
        mlp_total = mlp_job["result"].reshape(share, chunks, 2, width)
        up_total, down_total = mlp_total[:, :, 0], mlp_total[:, :, 1]
    up_total = up_total.reshape(share, chunks, count, share).transpose(0, 2, 1, 3)
    down_total = down_total.reshape(share, chunks, width).transpose(1, 0, 2)
    return (
        block_out.reshape(tokens.shape),
        input_grad.reshape(tokens.shape),
        by_kind(total_a, total_b).reshape(-1),
        total_a[:, span:].reshape(-1),
        up_total.reshape(-1),
        down_total.reshape(-1),
        small_total[:edge],
        small_total[edge:],
    )


def solution(mesh):
    split = P(AXES)
    whole = P(AXES, None, None)
    return jax.shard_map(
        functools.partial(local, mesh),
        mesh=mesh,
        in_specs=(whole, whole) + (split,) * 8,
        out_specs=(whole, whole) + (split,) * 6,
        check_vma=False,
    )
```

```python
import functools
import math

import jax
import jax.numpy as jnp
from jax import lax
from jax.experimental import pallas as pl
from jax.experimental.pallas import tpu as pltpu
from jax.sharding import PartitionSpec as P

HEADS = 12
PATCH_SMALL = 196
PATCH_LARGE = 576
AXES = ("dp", "fsdp")
bf16 = jnp.bfloat16
f32 = jnp.float32
NN = (((1,), (0,)), ((), ()))
NT = (((1,), (1,)), ((), ()))
TN = (((0,), (0,)), ((), ()))
VMEM_LIMIT = 60 * 2**20
TILE = 304
ATILE = 304
AHEAD = 1
MTILE = 304
MAHEAD = 1
LTILE = 608
LSUB = 304
BOT = 304
BTILE = 304
BAHEAD = 1
LOG2E = 1.4426950408889634


def dot(a, b, dims):
    return lax.dot_general(a, b, dims, preferred_element_type=f32)


def params(n):
    return pltpu.CompilerParams(
        vmem_limit_bytes=VMEM_LIMIT, dimension_semantics=("arbitrary",) * n
    )


def cost(*_):
    return pl.CostEstimate(flops=1, bytes_accessed=1, transcendentals=0)


def tile_of(seq):
    return TILE if seq % TILE == 0 else seq


def once(shape):
    return pl.BlockSpec(
        shape, lambda *_: (0,) * len(shape), pipeline_mode=pl.Buffered(buffer_count=1)
    )


def shape_of(shape, dtype):
    return jax.ShapeDtypeStruct(shape, dtype)


class Flights:
    def __init__(self):
        self.waiting = []
        self.flying = []

    def add(self, steps, lengths):
        job = {"steps": steps, "lengths": list(lengths), "result": None}
        self.advance(job, None)
        return job

    def advance(self, job, came):
        try:
            sends = job["steps"].send(came) if came is not None else next(job["steps"])
        except StopIteration as stop:
            job["result"] = lax.optimization_barrier(stop.value)
            return
        length = job["lengths"].pop(0) if job["lengths"] else 1
        self.waiting.append((job, sends, length))

    def depart(self):
        for job, sends, length in self.waiting:
            came = [lax.ppermute(array, AXES, pairs) for array, pairs in sends]
            self.flying.append([job, came, length])
        self.waiting = []

    def run(self, kernel, operand, *others):
        arrays = [array for _, sends, _ in self.waiting for array, _ in sends]
        if arrays:
            operand, arrays = lax.optimization_barrier((operand, arrays))
            left = iter(arrays)
            self.waiting = [
                (job, [(next(left), pairs) for _, pairs in sends], length)
                for job, sends, length in self.waiting
            ]
        self.depart()
        out = kernel(operand, *others)
        for flight in self.flying:
            flight[2] -= 1
        landed = [flight for flight in self.flying if flight[2] <= 0]
        self.flying = [flight for flight in self.flying if flight[2] > 0]
        if landed:
            out, came = lax.optimization_barrier((out, [flight[1] for flight in landed]))
            for flight, got in zip(landed, came):
                self.advance(flight[0], got)
        return out

    def finish(self, turns=None):
        turn = 0
        while (self.waiting or self.flying) and turn != turns:
            turn += 1
            self.depart()
            for flight in self.flying:
                flight[2] -= 1
            landed = [flight for flight in self.flying if turns is None or flight[2] <= 0]
            self.flying = [flight for flight in self.flying if not (turns is None or flight[2] <= 0)]
            cames = lax.optimization_barrier([flight[1] for flight in landed])
            for flight, came in zip(landed, cames):
                self.advance(flight[0], came)


def bit_groups(mesh):
    inner = int(math.log2(mesh.shape["fsdp"]))
    outer = int(math.log2(mesh.shape["dp"]))
    rest = [list(range(b, min(b + 2, inner))) for b in range(1, inner, 2)]
    return [0], list(range(inner, inner + outer)), rest


def position(me, bits):
    spot = 0
    for place, bit in enumerate(bits):
        spot = spot + ((me >> bit) & 1) * (1 << place)
    return spot


def partners(count, bits):
    swaps = []
    for step in range(1, 1 << len(bits)):
        mask = 0
        for place, bit in enumerate(bits):
            if (step >> place) & 1:
                mask |= 1 << bit
        swaps.append((step, [(i, i ^ mask) for i in range(count)]))
    return swaps


def gather_steps(shard, mesh, groups):
    count = mesh.size
    me = lax.axis_index(AXES)
    bits = int(math.log2(count))
    rows, columns = shard.shape
    held = shard.reshape((1,) * bits + (rows, columns))
    for group in groups:
        swaps = partners(count, group)
        came = yield [(held, pairs) for _, pairs in swaps]
        shape = list(held.shape)
        for bit in group:
            shape[bits - 1 - bit] = 2
        whole = jnp.zeros(shape, shard.dtype)
        for (step, _), got in zip([(0, None)] + swaps, [held] + came):
            start = [0] * len(shape)
            for place, bit in enumerate(group):
                start[bits - 1 - bit] = ((me >> bit) & 1) ^ ((step >> place) & 1)
            whole = lax.dynamic_update_slice(whole, got, start)
        held = whole
    return held.reshape(count * rows, columns)


def pick(array, axis, index):
    return lax.dynamic_slice_in_dim(array, index, 1, axis)


def total(terms, axis, index, kind):
    return sum(pick(term, axis, index).astype(f32) for term in terms).astype(kind)


def sum_steps(parts, mesh, kind):
    count = mesh.size
    core, outer, rest = bit_groups(mesh)
    me = lax.axis_index(AXES)
    rows, columns = parts.shape[0] // count, parts.shape[1]
    rest_size = mesh.shape["fsdp"] // 2
    held = parts.reshape(mesh.shape["dp"], rest_size, 2, rows, columns)
    spot = position(me, core)
    (got,) = yield [(pick(held, 2, spot ^ 1).astype(kind), partners(count, core)[0][1])]
    terms = [pick(held, 2, spot), got]
    split = 2 if len(outer) == 2 and columns % 256 == 0 else 1
    width = columns // split
    shape = (2,) * len(outer) + (rest_size, 1, rows, width)
    pieces = []
    for piece in range(split):
        own = [term[..., piece * width : (piece + 1) * width].reshape(shape) for term in terms]
        order = list(range(len(outer)))
        pieces.append((own, order if piece == 0 else order[::-1]))
    for turn in range(len(outer)):
        sends = []
        for own, order in pieces:
            axis = order[turn]
            bit = outer[len(outer) - 1 - axis]
            mine = position(me, [bit])
            sends.append((total(own, axis, mine ^ 1, kind), partners(count, [bit])[0][1]))
        came = yield sends
        pieces = [
            ([pick(term, order[turn], position(me, [outer[len(outer) - 1 - order[turn]]])) for term in own] + [got], order)
            for (own, order), got in zip(pieces, came)
        ]
    left = rest_size
    pieces = [[term.reshape(rest_size, rows, width) for term in own] for own, _ in pieces]
    for bits in reversed(rest):
        size = 1 << len(bits)
        left //= size
        pieces = [[term.reshape(size, left, rows, width) for term in own] for own in pieces]
        spot = position(me, bits)
        swaps = partners(count, bits)
        sends = [
            (jnp.concatenate([total(own, 0, spot ^ step, kind) for own in pieces], -1), pairs)
            for step, pairs in swaps
        ]
        came = yield sends
        pieces = [
            [pick(term, 0, spot) for term in own]
            + [got[..., place * width : (place + 1) * width] for got in came]
            for place, own in enumerate(pieces)
        ]
    sums = [sum(term.astype(f32) for term in own).reshape(rows, width) for own in pieces]
    return jnp.concatenate(sums, -1)


def send_sum_kernel(where, *refs, sizes):
    at = 0
    for size, out in zip(sizes, refs[sum(sizes) :]):
        out[...] = sum(term[...].astype(f32) for term in refs[at : at + size]).astype(out.dtype)
        at += size


def fold_first(where, keep, came):
    _, _, left, rows, columns = keep.shape
    cut = columns // 2
    spec_a = pl.BlockSpec((None, 2, 2, rows, cut), lambda j, where: ((where[1] // 2) ^ 1, 0, j, 0, 0))
    spec_b = pl.BlockSpec((2, None, 2, rows, cut), lambda j, where: (0, (where[1] % 2) ^ 1, j, 0, 1))
    return pl.pallas_call(
        functools.partial(send_sum_kernel, sizes=[2, 2]),
        grid_spec=pltpu.PrefetchScalarGridSpec(
            num_scalar_prefetch=1,
            grid=(left // 2,),
            in_specs=[spec_a, spec_a, spec_b, spec_b],
            out_specs=[pl.BlockSpec((2, 2, rows, cut), lambda j, where: (0, j, 0, 0))] * 2,
        ),
        out_shape=[shape_of((2, left, rows, cut), bf16)] * 2,
        compiler_params=params(1),
        cost_estimate=cost(),
        name="fold_first",
    )(where, keep, came, keep, came)


def fold_second(where, keep, came, came_a, came_b):
    _, _, left, rows, columns = keep.shape
    cut = columns // 2
    spec_a = pl.BlockSpec(
        (None, None, 2, rows, cut), lambda j, where: (where[1] // 2, (where[1] % 2) ^ 1, j, 0, 0)
    )
    spec_b = pl.BlockSpec(
        (None, None, 2, rows, cut), lambda j, where: ((where[1] // 2) ^ 1, where[1] % 2, j, 0, 1)
    )
    half_a = pl.BlockSpec((None, 2, rows, cut), lambda j, where: ((where[1] % 2) ^ 1, j, 0, 0))
    half_b = pl.BlockSpec((None, 2, rows, cut), lambda j, where: ((where[1] // 2) ^ 1, j, 0, 0))
    return pl.pallas_call(
        functools.partial(send_sum_kernel, sizes=[3, 3]),
        grid_spec=pltpu.PrefetchScalarGridSpec(
            num_scalar_prefetch=1,
            grid=(left // 2,),
            in_specs=[spec_a, spec_a, half_a, spec_b, spec_b, half_b],
            out_specs=[pl.BlockSpec((2, rows, cut), lambda j, where: (j, 0, 0))] * 2,
        ),
        out_shape=[shape_of((left, rows, cut), bf16)] * 2,
        compiler_params=params(1),
        cost_estimate=cost(),
        name="fold_second",
    )(where, keep, came, came_a, keep, came, came_b)


def line_first_kernel(where, *refs):
    *terms, keep, send = refs
    fast = where[2] % 2
    cut = terms[0].shape[-1]
    for slow in range(2):
        for place, out in ((slow * 2 + fast, keep), (slow * 2 + (fast ^ 1), send)):
            for half in range(2):
                own = terms[4 * half : 4 * half + 4]
                lanes = slice(half * cut, (half + 1) * cut)
                out[slow, :, lanes] = sum(term[place].astype(f32) for term in own).astype(out.dtype)


def line_first(where, keep, came, came_a, came_b, last_a, last_b):
    _, _, size, rows, columns = keep.shape
    cut = columns // 2
    whole = lambda half: pl.BlockSpec(
        (None, None, size, rows, cut), lambda j, where: (where[1] // 2, where[1] % 2, 0, 0, half)
    )
    half_a = pl.BlockSpec((None, size, rows, cut), lambda j, where: (where[1] % 2, 0, 0, 0))
    half_b = pl.BlockSpec((None, size, rows, cut), lambda j, where: (where[1] // 2, 0, 0, 0))
    last = pl.BlockSpec((size, rows, cut), lambda j, where: (0, 0, 0))
    return pl.pallas_call(
        line_first_kernel,
        grid_spec=pltpu.PrefetchScalarGridSpec(
            num_scalar_prefetch=1,
            grid=(1,),
            in_specs=[whole(0), whole(0), half_a, last, whole(1), whole(1), half_b, last],
            out_specs=[once((size // 2, rows, columns))] * 2,
        ),
        out_shape=[shape_of((size // 2, rows, columns), bf16)] * 2,
        compiler_params=params(1),
        cost_estimate=cost(),
        name="line_first",
    )(where, keep, came, came_a, last_a, keep, came, came_b, last_b)


def swap_steps(send, mesh):
    core, _, _ = bit_groups(mesh)
    (came,) = yield [(send, partners(mesh.size, core)[0][1])]
    return came


def part_of(terms, axis, index, kind):
    total = None
    for term in terms:
        if term.shape[axis] != 1:
            term = pick(term, axis, index)
        total = term.astype(f32) if total is None else total + term.astype(f32)
    return total.astype(kind)


def fast_sum_steps(keeps, cames, where, mesh):
    count = mesh.size
    _, outer, rest = bit_groups(mesh)
    me = lax.axis_index(AXES)
    spot = position(me, outer)
    size, line = 1 << len(outer), 1 << len(rest[0])
    terms = []
    for pair in zip(keeps, cames):
        for array in pair:
            lead = keeps[0].shape[2] - array.shape[2]
            array = jnp.pad(array, ((0, 0), (0, 0), (lead, 0))) if lead else array
            terms.append(array.reshape((size, line) + array.shape[1:]))
    sends = [part_of(terms, 0, spot ^ step, bf16)[0] for step in range(1, size)]
    terms = [pick(term, 0, spot)[0] for term in terms]
    came = yield [(array, pairs) for array, (_, pairs) in zip(sends, partners(count, outer))]
    terms = terms + came
    spot = position(me, rest[0])
    came = yield [
        (part_of(terms, 0, spot ^ step, bf16)[0], pairs) for step, pairs in partners(count, rest[0])
    ]
    return part_of(terms, 0, spot, f32)[0] + sum(array.astype(f32) for array in came)


def fold_sum_steps(keep, send, where, mesh):
    count = mesh.size
    core, outer, rest = bit_groups(mesh)
    (came,) = yield [(send, partners(count, core)[0][1])]
    shape = (2, 2, 1 << len(rest[0]), keep.shape[0] * 2 // count, keep.shape[1])
    keep, came = keep.reshape(shape), came.reshape(shape)
    fast, slow = (partners(count, [bit])[0][1] for bit in outer)
    send_a, send_b = fold_first(where, keep, came)
    came_a, came_b = yield [(send_a, slow), (send_b, fast)]
    send_a, send_b = fold_second(where, keep, came, came_a, came_b)
    last_a, last_b = yield [(send_a, fast), (send_b, slow)]
    keep, send = line_first(where, keep, came, came_a, came_b, last_a, last_b)
    (came,) = yield [(send, partners(count, [rest[0][0]])[0][1])]
    me = lax.axis_index(AXES)
    spot = position(me, [rest[0][1]])
    both = [keep, came]
    (last,) = yield [(total(both, 0, spot ^ 1, bf16), partners(count, [rest[0][1]])[0][1])]
    done = (total(both, 0, spot, f32) + last.astype(f32)).reshape(2, shape[3] // 2, shape[4])
    spot = position(me, core)
    (came,) = yield [(pick(done, 0, spot ^ 1), partners(count, core)[0][1])]
    own, came = pick(done, 0, spot)[0], came[0]
    return jnp.where(spot == 0, own, came), jnp.where(spot == 0, came, own)


def small_sum_steps(parts, mesh):
    count = mesh.size
    core, outer, rest = bit_groups(mesh)
    groups = [core, outer, *reversed(rest)]
    order = [outer, *reversed(rest), core]
    me = lax.axis_index(AXES)
    columns = parts.shape[1]
    held = parts.reshape([1 << len(bits) for bits in order] + [columns])
    for bits in groups:
        axis = order.index(bits)
        spot = position(me, bits)
        swaps = partners(count, bits)
        came = yield [(pick(held, axis, spot ^ step), pairs) for step, pairs in swaps]
        held = pick(held, axis, spot) + sum(came)
    return held.reshape(columns)


def cut_by_core(mesh):
    _, outer, rest = bit_groups(mesh)
    return len(outer) == 2 and len(rest) == 1 and len(rest[0]) == 2


def store_cut(core, outs, lanes, value, rows):
    if len(outs) == 1:
        outs[0][:, lanes] = value.astype(bf16)
        return
    keep, send = outs
    for parity in range(2):
        @pl.when(core == parity)
        def _():
            for device in range(value.shape[0] // rows):
                out = keep if device % 2 == parity else send
                out[device // 2, :, lanes] = value[device * rows : (device + 1) * rows, :].astype(bf16)


def cut_shapes(width, columns, chunk, index, rows):
    if not rows:
        spec = pl.BlockSpec((width, chunk), lambda j, *_: (0, index(j)))
        return [spec], [shape_of((width, columns), bf16)]
    blocks = width // rows // 2
    spec = pl.BlockSpec((blocks, rows, chunk), lambda j, *_: (0, 0, index(j)))
    return [spec] * 2, [shape_of((blocks, rows, columns), bf16)] * 2


def normalize(values):
    center = values - jnp.mean(values, -1, keepdims=True)
    scale = lax.rsqrt(jnp.mean(center * center, -1, keepdims=True) + 1e-05)
    return center * scale, scale


def norm_back(grad, gain, unit, scale):
    inner = grad * gain
    return scale * (
        inner
        - jnp.mean(inner, -1, keepdims=True)
        - unit * jnp.mean(inner * unit, -1, keepdims=True)
    )


def gelu_parts(u):
    phi = 0.5 + 0.5 * lax.erf(u * 0.7071067811865476)
    slope = phi + u * (0.3989422804014327 * jnp.exp2((u * u) * (-0.5 * LOG2E)))
    return u * phi, slope


def column_sum(values):
    return jnp.sum(values, 0, keepdims=True)


def accumulate(ref, value, first):
    @pl.when(first)
    def _():
        ref[...] = value

    @pl.when(jnp.logical_not(first))
    def _():
        ref[...] += value


def two_heads(block, padded):
    seq = block.shape[0]
    first = lax.broadcasted_iota(jnp.int32, block.shape, 1) < 64
    zero = jnp.zeros_like(block)
    pad = jnp.zeros((padded - seq, 128), block.dtype)
    return jnp.concatenate(
        [jnp.where(first, block, zero), pad, jnp.where(first, zero, block), pad], 0
    )


def attend_kernel(valid, *refs, tile, padded, first, pairs):
    if first:
        tokens, gain, shift, weight, bias, normed, joined, mixed, raised_out, inverse = refs
    else:
        (
            normed, weight, bias, tokens, mixed_first, bias_out, gain, shift,
            joined, mixed, raised_out, inverse, middle, normed_two,
        ) = refs
    seq, span = joined.shape
    for start in range(0, seq, tile):
        rows = slice(start, start + tile)
        if first:
            unit, _ = normalize(tokens[rows, :].astype(f32))
            low = (unit * gain[...] + shift[...]).astype(bf16)
            normed[rows, :] = low
        else:
            low = normed[rows, :]
        joined[rows, :] = (dot(low, weight[:, :span], NN) + bias[...]).astype(bf16)

    column = lax.broadcasted_iota(jnp.int32, (1, padded), 1)
    mask = jnp.where(column < valid[pl.program_id(0)], 0.0, -1e30).astype(f32)
    places = [(pair, start) for pair in range(pairs) for start in range(0, seq, ATILE)]
    keys, values = {}, {}
    row = lax.broadcasted_iota(jnp.int32, (2 * padded, 128), 0)
    lane = lax.broadcasted_iota(jnp.int32, (2 * padded, 128), 1)
    ones = jnp.where((row < padded) == (lane < 64), 1.0, 0.0).astype(bf16)

    def scores_at(pair, start):
        if pair not in keys:
            at = pair * 384
            keys[pair] = two_heads(joined[:, at + 128 : at + 256], padded)
            values[pair] = jnp.concatenate([two_heads(joined[:, at + 256 : at + 384], padded), ones], 1)
        return dot(joined[start : start + ATILE, pair * 384 : pair * 384 + 128], keys[pair], NT)

    ahead = [scores_at(*place) for place in places[:AHEAD]]
    for index, (pair, start) in enumerate(places):
        rows = slice(start, start + ATILE)
        if index + AHEAD < len(places):
            ahead.append(scores_at(*places[index + AHEAD]))
        scores = ahead.pop(0)
        halves = []
        for head in range(2):
            part = scores[:, head * padded : (head + 1) * padded] * (0.125 * LOG2E) + mask
            halves.append(jnp.exp2(part - jnp.max(part, 1, keepdims=True)).astype(bf16))
        raised = jnp.concatenate(halves, 1)
        raised_out[pair, rows, :] = raised
        both = dot(raised, values[pair], NN)
        scale = 1.0 / both[:, 128:]
        inverse[rows, pair * 128 : (pair + 1) * 128] = scale
        mixed[rows, pair * 128 : (pair + 1) * 128] = (both[:, :128] * scale).astype(bf16)
    if first:
        return
    width = tokens.shape[1]
    for start in range(0, seq, tile):
        rows = slice(start, start + tile)
        value = tokens[rows, :].astype(f32) + bias_out[...]
        value = value + dot(mixed_first[rows, :], weight[: width // 2, -width:], NN)
        value = value + dot(mixed[rows, :], weight[width // 2 :, -width:], NN)
        middle[rows, :] = value
        unit, _ = normalize(value)
        normed_two[rows, :] = (unit * gain[...] + shift[...]).astype(bf16)


def attend(start, valid, weight, bias, seq, norm=None, after=None):
    rows, width = start.shape
    span = bias.shape[1]
    pairs = span // 384
    items = rows // seq
    padded = -(-seq // 128) * 128
    row = lambda w: pl.BlockSpec((seq, w), lambda i, *_: (i, 0))
    one = once((1, width))
    main = [once(weight.shape), once((1, span))]
    if norm:
        specs, arrays = [row(width), one, one, *main], [start, *norm, weight, bias]
    else:
        specs = [row(width), *main, row(width), row(width // 2), one, one, one]
        arrays = [start, weight, bias, *after]
    outs = [
        row(span),
        row(span // 3),
        pl.BlockSpec((None, pairs, seq, 2 * padded), lambda i, *_: (i, 0, 0, 0)),
        row(span // 3),
    ]
    shapes = [
        shape_of((rows, span), bf16),
        shape_of((rows, span // 3), bf16),
        shape_of((items, pairs, seq, 2 * padded), bf16),
        shape_of((rows, span // 3), f32),
    ]
    if norm:
        outs, shapes = [row(width)] + outs, [shape_of((rows, width), bf16)] + shapes
    else:
        outs += [row(width)] * 2
        shapes += [shape_of((rows, width), f32), shape_of((rows, width), bf16)]
    return pl.pallas_call(
        functools.partial(attend_kernel, tile=tile_of(seq), padded=padded, first=bool(norm), pairs=pairs),
        grid_spec=pltpu.PrefetchScalarGridSpec(
            num_scalar_prefetch=1, grid=(items,), in_specs=specs, out_specs=outs
        ),
        out_shape=shapes,
        compiler_params=params(1),
        cost_estimate=cost(),
        name="attend",
    )(valid, *arrays)


def attend_back_kernel(where, *refs, pairs, extra, carry, cut):
    lists = [refs[kind * pairs : (kind + 1) * pairs] for kind in range(5)]
    joined, mixed_grad, mixed, raised, inverse = lists
    normed, *rest = refs[5 * pairs :]
    carried, rest = rest[:carry], rest[carry:]
    if extra:
        mixed_a, mixed_b, low_grad, joined_grad, column, *outs, held, scaled, total, total_out = rest
    else:
        joined_grad, column, *outs, held, scaled, total = rest
    item = pl.program_id(0)
    seq, span = joined_grad.shape
    padded = raised[0].shape[1] // 2
    tile = BTILE if seq % BTILE == 0 else seq
    first = lax.broadcasted_iota(jnp.int32, (tile, 128), 1) < 64
    places = [(pair, start) for pair in range(pairs) for start in range(0, seq, tile)]
    keys, values = {}, {}

    def prob_grad_at(pair, start):
        if pair not in keys:
            keys[pair] = two_heads(joined[pair][:, 128:256], padded)
            values[pair] = two_heads(joined[pair][:, 256:], padded)
        rows = slice(start, start + tile)
        grad = (mixed_grad[pair][rows, :].astype(f32) * inverse[pair][rows, :]).astype(bf16)
        scaled[pair, rows, :] = grad
        return grad, dot(grad, values[pair], NT)

    def own_half(both):
        return jnp.concatenate([both[:64, :padded], both[64:, padded:]], 0).T[:seq]

    ahead = [prob_grad_at(*place) for place in places[:BAHEAD]]
    for index, (pair, start) in enumerate(places):
        rows = slice(start, start + tile)
        at = pair * 384
        if index + BAHEAD < len(places):
            ahead.append(prob_grad_at(*places[index + BAHEAD]))
        grad, prob_grad = ahead.pop(0)
        product = grad.astype(f32) * mixed[pair][rows, :].astype(f32)
        zero = jnp.zeros_like(product)
        halves = []
        for head in range(2):
            own = jnp.where(first, product, zero) if head == 0 else jnp.where(first, zero, product)
            centre = jnp.sum(own, 1, keepdims=True)
            half = slice(head * padded, (head + 1) * padded)
            halves.append((raised[pair][rows, half].astype(f32) * (prob_grad[:, half] - centre)).astype(bf16))
        score_grad = jnp.concatenate(halves, 1)
        held[rows, :] = score_grad
        joined_grad[rows, at : at + 128] = (dot(score_grad, keys[pair], NN) * 0.125).astype(bf16)
        if start + tile == seq:
            joined_grad[:, at + 128 : at + 256] = (
                own_half(dot(joined[pair][:, :128].T, held[...], NN)) * 0.125
            ).astype(bf16)
            joined_grad[:, at + 256 : at + 384] = own_half(
                dot(scaled[pair].T, raised[pair][...], NN)
            ).astype(bf16)

    value = joined_grad[...]
    accumulate(total, dot(normed[...], value, TN), item == 0)
    accumulate(column, column_sum(value.astype(f32)), item == 0)
    if extra:
        both = [dot(mixed_a[...], low_grad[...], TN), dot(mixed_b[...], low_grad[...], TN)]
        accumulate(total_out, jnp.concatenate(both, 0), item == 0)

    @pl.when(item == pl.num_programs(0) - 1)
    def _():
        begin = 0
        for before, out in zip(carried, outs):
            begin = before.shape[-1]
            out[..., :begin] = before[...]
            if out.shape[-1] > begin + span:
                out[..., begin + span :] = jnp.zeros(out.shape[:-1] + (out.shape[-1] - begin - span,), bf16)
        store_cut(where[0], outs, slice(begin, begin + span), total[...], cut)
        if extra:
            store_cut(where[0], outs, slice(span, span + total_out.shape[1]), total_out[...], cut)


def attend_back(mixed_grad, where, joined, mixed, raised, inverse, normed, seq, part, chosen, cut, others=(), carried=()):
    rows, width = normed.shape
    items, in_part, _, keys = raised.shape
    pairs = len(chosen)
    span = 384 * pairs
    row = lambda w, off=0: pl.BlockSpec((seq, w), lambda i, *_: (i, off))
    each = lambda w, off=0: [row(w, off + pair) for pair in chosen]
    weights = [
        pl.BlockSpec((None, None, seq, keys), functools.partial(lambda at, i, *_: (i, at, 0, 0), pair))
        for pair in chosen
    ]
    columns = span + (width if others else 0) + (carried[0].shape[-1] + 128 if carried else 0)
    specs, shapes = cut_shapes(width, columns, columns, lambda j: 0, cut)
    return pl.pallas_call(
        functools.partial(
            attend_back_kernel, pairs=pairs, extra=bool(others), carry=len(carried), cut=cut
        ),
        grid_spec=pltpu.PrefetchScalarGridSpec(
            num_scalar_prefetch=1,
            grid=(items,),
            in_specs=[
                *each(384), *each(128, part * in_part), *each(128), *weights, *each(128), row(width)
            ]
            + [once(array.shape) for array in carried]
            + [row(array.shape[1]) for array in others],
            out_specs=[row(span), pl.BlockSpec((1, span), lambda i, *_: (0, 0))] + specs,
            scratch_shapes=[
                pltpu.VMEM((seq, keys), bf16),
                pltpu.VMEM((pairs, seq, 128), bf16),
                pltpu.VMEM((width, span), f32),
            ]
            + ([pltpu.VMEM((width, width), f32)] if others else []),
        ),
        out_shape=[shape_of((rows, span), bf16), shape_of((1, span), f32)] + shapes,
        compiler_params=params(1),
        cost_estimate=cost(),
        name="attend_back",
    )(
        where, *[joined] * pairs, *[mixed_grad] * pairs, *[mixed] * pairs, *[raised] * pairs,
        *[inverse] * pairs, normed, *carried, *others,
    )


def mlp_kernel(
    valid, where, normed, cotangent, up, down, bias_up,
    active, hidden_grad, up_sum, *rest, seq, tile, cut,
):
    *outs, grad = rest
    rows, width = normed.shape

    @pl.when(pl.program_id(0) == 0)
    def _():
        place = lax.broadcasted_iota(jnp.int32, (seq, 1), 0)
        for item in range(rows // seq):
            span = slice(item * seq, (item + 1) * seq)
            grad[span, :] = jnp.where(place < valid[item], cotangent[span, :].astype(f32), 0.0).astype(bf16)

    def ahead_of(start):
        span = slice(start, start + MTILE)
        return dot(normed[span, :], up[...], NN), dot(grad[span, :], down[...], NT)

    column = jnp.zeros(up_sum.shape, f32)
    starts = list(range(0, rows, MTILE))
    ahead = [ahead_of(start) for start in starts[:MAHEAD]]
    for index, start in enumerate(starts):
        span = slice(start, start + MTILE)
        if index + MAHEAD < len(starts):
            ahead.append(ahead_of(starts[index + MAHEAD]))
        hidden, wide = ahead.pop(0)
        value, slope = gelu_parts(hidden + bias_up[...])
        low = (slope * wide).astype(bf16)
        active[span, :] = value.astype(bf16)
        hidden_grad[span, :] = low
        column = column + column_sum(low.astype(f32))
    up_sum[...] = column
    first = dot(normed[...], hidden_grad[...], TN).astype(bf16)
    second = dot(active[...], grad[...], TN).astype(bf16)
    if cut:
        keep, send = outs
        for core in range(2):
            @pl.when(where[0] == core)
            def _():
                (keep, send)[core][...] = first
                (send, keep)[core][...] = second
    else:
        outs[0][:, :width] = first
        outs[0][:, width:] = second


def mlp(normed, valid, where, cotangent, both, bias_up, seq, cut):
    rows, width = normed.shape
    wide = both.shape[1] // 2
    chunks = wide // width
    whole = once((rows, width))
    square = lambda off: pl.BlockSpec((width, width), lambda j, *_: (0, j + off))
    row = pl.BlockSpec((rows, width), lambda j, *_: (0, j))
    one = pl.BlockSpec((1, width), lambda j, *_: (0, j))
    if cut:
        specs = [pl.BlockSpec((width, width), lambda j, *_: (0, j))] * 2
        shapes = [shape_of((width, wide), bf16)] * 2
    else:
        specs, shapes = cut_shapes(width, 2 * wide, 2 * width, lambda j: j, 0)
    return pl.pallas_call(
        functools.partial(mlp_kernel, seq=seq, tile=tile_of(seq), cut=cut),
        grid_spec=pltpu.PrefetchScalarGridSpec(
            num_scalar_prefetch=2,
            grid=(chunks,),
            in_specs=[whole, whole, square(0), square(chunks), one],
            out_specs=[row, row, one] + specs,
            scratch_shapes=[pltpu.VMEM((rows, width), bf16)],
        ),
        out_shape=[
            shape_of((rows, width * chunks), bf16),
            shape_of((rows, width * chunks), bf16),
            shape_of((1, width * chunks), f32),
        ]
        + shapes,
        compiler_params=params(1),
        cost_estimate=cost(),
        name="mlp",
    )(valid, where, normed, cotangent, both, both, bias_up)


def block_out_kernel(valid, active, downs, middle, bias_down, *rest, seq, begin):
    block_out = rest[-1]
    tile, width = middle.shape
    step = pl.program_id(0) + begin // tile
    place = lax.broadcasted_iota(jnp.int32, (tile, 1), 0) + lax.rem(step, seq // tile) * tile
    value = middle[...] + bias_down[...]
    for at in range(0, downs.shape[1], width):
        value = value + dot(active[:, at : at + width], downs[:, at : at + width], NN)
    block_out[...] = jnp.where(place < valid[step // (seq // tile)], value, 0.0).astype(bf16)


def half_of(both, second):
    width, columns = both.shape
    return pl.BlockSpec(
        (width, columns // 2), lambda j, *_: (0, second), pipeline_mode=pl.Buffered(buffer_count=1)
    )


def block_out_of(middle, valid, active, both, bias_down, seq, begin, end, before=None):
    rows, width = middle.shape
    tile = BOT if seq % BOT == 0 else seq
    skip = begin // tile
    row = lambda w: pl.BlockSpec((tile, w), lambda j, *_: (j + skip, 0))
    specs = [row(active.shape[1]), half_of(both, 1), row(width), once((1, width))]
    arrays = [active, both, middle, bias_down]
    aliases = {}
    if before is not None:
        aliases = {len(arrays) + 1: 0}
        specs.append(pl.BlockSpec(memory_space=pl.ANY))
        arrays.append(before)
    return pl.pallas_call(
        functools.partial(block_out_kernel, seq=seq, begin=begin),
        grid_spec=pltpu.PrefetchScalarGridSpec(
            num_scalar_prefetch=1,
            grid=((end - begin) // tile,),
            in_specs=specs,
            out_specs=row(width),
        ),
        out_shape=shape_of((rows, width), bf16),
        input_output_aliases=aliases,
        compiler_params=params(1),
        cost_estimate=cost(),
        name="block_out",
    )(valid, *arrays)


def middle_back_kernel(
    valid, hidden_grad, ups, middle, cotangent, gain, weight,
    low_grad, mixed_grad, gain_sum, shift_sum, bias_sum, down_sum, *, seq, sub,
):
    step = pl.program_id(0)
    tile, width = middle.shape
    each = seq // tile
    starts = list(range(0, tile, sub))
    ahead = [dot(hidden_grad[:sub, :], ups[...], NT)]
    sums = [jnp.zeros((1, width), f32)] * 4
    for index, start in enumerate(starts):
        rows = slice(start, start + sub)
        if index + 1 < len(starts):
            ahead.append(dot(hidden_grad[start + sub : start + 2 * sub, :], ups[...], NT))
        grad = ahead.pop(0)
        unit, scale = normalize(middle[rows, :])
        place = lax.broadcasted_iota(jnp.int32, (sub, 1), 0) + (lax.rem(step, each) * tile + start)
        kept = jnp.where(place < valid[step // each], cotangent[rows, :].astype(f32), 0.0)
        low = (kept + norm_back(grad, gain[...], unit, scale)).astype(bf16)
        low_grad[rows, :] = low
        mixed_grad[rows, :] = dot(low, weight[:, -width:], NT).astype(bf16)
        terms = (grad * unit, grad, low.astype(f32), kept)
        sums = [before + column_sum(term) for before, term in zip(sums, terms)]
    for ref, value in zip((gain_sum, shift_sum, bias_sum, down_sum), sums):
        accumulate(ref, value, step == 0)


def middle_back(middle, valid, hidden_grad, both, cotangent, gain, weight, seq):
    rows, width = middle.shape
    tile = LTILE if seq % LTILE == 0 else seq
    sub = LSUB if tile % LSUB == 0 else tile
    row = lambda w: pl.BlockSpec((tile, w), lambda j, *_: (j, 0))
    one = pl.BlockSpec((1, width), lambda j, *_: (0, 0))
    return pl.pallas_call(
        functools.partial(middle_back_kernel, seq=seq, sub=sub),
        grid_spec=pltpu.PrefetchScalarGridSpec(
            num_scalar_prefetch=1,
            grid=(rows // tile,),
            in_specs=[
                row(hidden_grad.shape[1]), half_of(both, 0), row(width), row(width),
                once((1, width)), once(weight.shape),
            ],
            out_specs=[row(width), row(width)] + [one] * 4,
        ),
        out_shape=[shape_of((rows, width), bf16)] * 2 + [shape_of((1, width), f32)] * 4,
        compiler_params=params(1),
        cost_estimate=cost(),
        name="middle_back",
    )(valid, hidden_grad, both, middle, cotangent, gain, weight)


def input_back_kernel(*refs, spans, sub):
    grads = refs[: len(spans)]
    weights = refs[len(spans) : len(spans) + 2]
    tokens, low_grad, gain, input_grad, gain_sum, shift_sum = refs[len(spans) + 2 :]
    tile, width = tokens.shape

    def ahead_of(start):
        rows = slice(start, start + sub)
        terms = [
            dot(grad[rows, :], weights[which][:, lanes], NT) for grad, (which, lanes) in zip(grads, spans)
        ]
        return sum(terms[1:], terms[0])

    starts = list(range(0, tile, sub))
    ahead = [ahead_of(0)]
    sums = [jnp.zeros((1, width), f32)] * 2
    for index, start in enumerate(starts):
        rows = slice(start, start + sub)
        if index + 1 < len(starts):
            ahead.append(ahead_of(start + sub))
        grad = ahead.pop(0)
        unit, scale = normalize(tokens[rows, :].astype(f32))
        sums = [before + column_sum(term) for before, term in zip(sums, (grad * unit, grad))]
        full = low_grad[rows, :].astype(f32) + norm_back(grad, gain[...], unit, scale)
        input_grad[rows, :] = full.astype(bf16)
    for ref, value in zip((gain_sum, shift_sum), sums):
        accumulate(ref, value, pl.program_id(0) == 0)


def input_back(last, others, spans, weights, tokens, low_grad, gain, seq):
    rows, width = tokens.shape
    tile = LTILE if seq % LTILE == 0 else seq
    sub = LSUB if tile % LSUB == 0 else tile
    row = lambda w: pl.BlockSpec((tile, w), lambda i: (i, 0))
    fixed = pl.BlockSpec((1, width), lambda i: (0, 0))
    grads = [*others, last]
    return pl.pallas_call(
        functools.partial(input_back_kernel, spans=spans, sub=sub),
        grid=(rows // tile,),
        in_specs=[row(grad.shape[1]) for grad in grads]
        + [once(weight.shape) for weight in weights]
        + [row(width), row(width), once((1, width))],
        out_specs=[row(width), fixed, fixed],
        out_shape=[shape_of((rows, width), bf16)] + [shape_of((1, width), f32)] * 2,
        compiler_params=params(1),
        cost_estimate=cost(),
        name="input_back",
    )(*grads, *weights, tokens, low_grad, gain)


def local(mesh, tokens, cotangent, group, text_len, qkv_w, out_w, mlp_in, mlp_out, gains, biases):
    items, seq, width = tokens.shape
    rows = items * seq
    count = mesh.size
    share = width // count
    wide = mlp_in.shape[0] // share
    chunks = wide // width
    half = width // 2
    span = 3 * half
    valid = (PATCH_SMALL + (PATCH_LARGE - PATCH_SMALL) * group + text_len).astype(jnp.int32)
    flat = tokens.reshape(rows, width)
    cot = cotangent.reshape(rows, width)
    flights = Flights()
    me = lax.axis_index(AXES)
    core, outer, others = bit_groups(mesh)
    where = jnp.stack([position(me, core), position(me, outer), position(me, others[0])]).astype(jnp.int32)
    cut = share if cut_by_core(mesh) and share % 8 == 0 else 0

    def mlp_sums(arrays):
        if cut:
            return flights.add(fold_sum_steps(*arrays, where, mesh), [])
        return flights.add(sum_steps(arrays[0], mesh, bf16), [])

    def swap(arrays):
        return flights.add(swap_steps(arrays[1], mesh), []) if cut else None

    def sums_after(arrays, swaps):
        if cut:
            keeps, cames = [keep for keep, _ in arrays], [job["result"] for job in swaps]
            return flights.add(fast_sum_steps(keeps, cames, where, mesh), [])
        return flights.add(sum_steps(arrays[0][0], mesh, bf16), [])


    def by_pairs(matrix, part):
        rows = matrix.shape[0]
        cubes = matrix.reshape(rows, 3, 2, half // 128, 128)[:, :, part]
        return cubes.transpose(0, 2, 1, 3).reshape(rows, span)

    def by_kind(part_a, part_b):
        rows = part_a.shape[0]
        cubes = [piece[:, :span].reshape(rows, half // 128, 3, 128) for piece in (part_a, part_b)]
        return jnp.stack(cubes, 1).transpose(0, 3, 1, 2, 4).reshape(rows, 3 * width)

    own_up = mlp_in.reshape(share, count, chunks, share).transpose(0, 2, 1, 3).reshape(share, wide)
    own_down = mlp_out.reshape(chunks, share, width).transpose(1, 0, 2).reshape(share, wide)
    own_both = jnp.concatenate([own_up, own_down], 1)

    own_qkv = qkv_w.reshape(share, 3 * width)
    small = jnp.concatenate([gains, biases])
    small_rows = -(-small.shape[0] // 128)
    padded = jnp.pad(small, (0, small_rows * 128 - small.shape[0])).reshape(small_rows, 128)
    padded = jnp.pad(padded, ((0, share - small_rows), (0, 0)))
    both = lax.all_gather(own_both, AXES, axis=0, tiled=True)
    own_first = jnp.concatenate([by_pairs(own_qkv, 0), padded], 1)
    own_second = jnp.concatenate([by_pairs(own_qkv, 1), out_w.reshape(share, width)], 1)
    singles = [[bit] for group in reversed(others) for bit in reversed(group)]
    job = flights.add(gather_steps(own_first, mesh, [*others, outer, core]), [])
    second_job = flights.add(gather_steps(own_second, mesh, [*singles, outer, core]), [1] * len(singles) + [2])
    flights.finish(len(others) + 2)
    first = job["result"]
    small = first[:, span:].reshape(count, share, 128)[:, :small_rows]
    small = small.reshape(count, small_rows * 128).astype(f32)
    edge = gains.shape[0]
    gain = small[:, :edge].reshape(1, 2 * width)
    bias = small[:, edge : edge + biases.shape[0]].reshape(1, 6 * width + wide)
    gain_one, gain_two = gain[:, :width], gain[:, width:]
    bias_query, bias_value, bias_output, shift_one, shift_two, bias_down = (
        bias[:, p * width : (p + 1) * width] for p in range(6)
    )
    bias_up = bias[:, 6 * width :].reshape(count, chunks, share).transpose(1, 0, 2).reshape(1, wide)
    bias_joined = jnp.concatenate([bias_query, jnp.zeros_like(bias_query), bias_value], 1)
    bias_parts = [by_pairs(bias_joined, part) for part in range(2)]

    normed, joined_a, mixed_a, raised_a, inverse_a = flights.run(
        lambda x: attend(x, valid, first, bias_parts[0], seq, (gain_one, shift_one)), flat
    )
    flights.finish()
    second = second_job["result"]
    joined_b, mixed_b, raised_b, inverse_b, middle, normed_two = attend(
        normed, valid, second, bias_parts[1], seq,
        after=(flat, mixed_a, bias_output, gain_two, shift_two),
    )

    active, hidden_grad, up_sum, *mlp_grads = mlp(
        normed_two, valid, where, cot, both, bias_up, seq, cut
    )
    mlp_job = mlp_sums(mlp_grads)

    low_grad, mixed_grad, gain_two_sum, shift_two_sum, bias_out_sum, down_sum = flights.run(
        lambda x: middle_back(x, valid, hidden_grad, both, cot, gain_two, second, seq), middle
    )
    joined_grad_a, qkv_sum_a, *grads_a = flights.run(
        lambda x: attend_back(
            x, where, joined_a, mixed_a, raised_a, inverse_a, normed, seq, 0, range(half // 128), cut,
            (mixed_a, mixed_b, low_grad),
        ),
        mixed_grad,
    )
    swap_a = swap(grads_a)
    joined_grad_b, qkv_sum_b, *grads_b = flights.run(
        lambda x: attend_back(
            x, where, joined_b, mixed_b, raised_b, inverse_b, normed, seq, 1, range(1), cut
        ),
        mixed_grad,
    )
    sum_a = sums_after([grads_a], [swap_a])
    joined_grad_c, qkv_sum_c, *grads_b = flights.run(
        lambda x: attend_back(
            x, where, joined_b, mixed_b, raised_b, inverse_b, normed, seq, 1, range(1, half // 128), cut,
            carried=grads_b,
        ),
        mixed_grad,
    )
    swap_b = swap(grads_b)
    spans = ((0, slice(0, span)), (1, slice(0, 384)), (1, slice(384, span)))
    input_grad, gain_one_sum, shift_one_sum = flights.run(
        lambda x: input_back(
            x, [joined_grad_a, joined_grad_b], spans, [first, second], flat, low_grad, gain_one, seq
        ),
        joined_grad_c,
    )
    qkv_sum_b = jnp.concatenate([qkv_sum_b, qkv_sum_c], 1)

    joined_sums = by_kind(qkv_sum_a, qkv_sum_b)
    up_sum = up_sum.reshape(chunks, count, share).transpose(1, 0, 2).reshape(1, wide)
    gain_sums = jnp.concatenate([gain_one_sum, gain_two_sum], 1).reshape(count, edge)
    bias_sums = jnp.concatenate(
        [
            joined_sums[:, :width],
            joined_sums[:, 2 * width :],
            bias_out_sum,
            shift_one_sum,
            shift_two_sum,
            down_sum,
            up_sum,
        ],
        1,
    ).reshape(count, biases.shape[0])
    small = jnp.concatenate([gain_sums, bias_sums], 1)
    if cut:
        small = jnp.pad(small, ((0, 0), (0, small_rows * 128 - small.shape[1])))
        small = small.reshape(count // 2, 2, small_rows, 128)
        spot = position(me, core)
        small = [
            jnp.pad(pick(small, 1, place)[:, 0], ((0, 0), (0, share - small_rows), (0, 0))).astype(bf16)
            for place in (spot, spot ^ 1)
        ]
        swap_small = swap(small)
    else:
        small_job = flights.add(small_sum_steps(small, mesh), [])
        sum_b = sums_after([grads_b], [None])
    cuts = [0, items // 2 * seq, rows]
    block_out = None
    for begin, end in zip(cuts, cuts[1:]):
        if begin < end:
            block_out = flights.run(
                lambda x: block_out_of(
                    x, valid, active, both, bias_down, seq, begin, end, block_out
                ),
                middle,
            )
            if cut and begin == 0:
                sum_b = sums_after([grads_b, small], [swap_b, swap_small])
    flights.finish()
    total_a, total_b = sum_a["result"], sum_b["result"]
    if cut:
        small_total = total_b[:small_rows, span:].reshape(-1)
        small_total = small_total[: edge + biases.shape[0]]
    else:
        small_total = small_job["result"]
    if cut:
        up_total, down_total = mlp_job["result"]
    else:
        mlp_total = mlp_job["result"].reshape(share, chunks, 2, width)
        up_total, down_total = mlp_total[:, :, 0], mlp_total[:, :, 1]
    up_total = up_total.reshape(share, chunks, count, share).transpose(0, 2, 1, 3)
    down_total = down_total.reshape(share, chunks, width).transpose(1, 0, 2)
    return (
        block_out.reshape(tokens.shape),
        input_grad.reshape(tokens.shape),
        by_kind(total_a, total_b).reshape(-1),
        total_a[:, span:].reshape(-1),
        up_total.reshape(-1),
        down_total.reshape(-1),
        small_total[:edge],
        small_total[edge:],
    )


def solution(mesh):
    split = P(AXES)
    whole = P(AXES, None, None)
    return jax.shard_map(
        functools.partial(local, mesh),
        mesh=mesh,
        in_specs=(whole, whole) + (split,) * 8,
        out_specs=(whole, whole) + (split,) * 6,
        check_vma=False,
    )
```

```python
import functools
import math

import jax
import jax.numpy as jnp
from jax import lax
from jax.experimental import pallas as pl
from jax.experimental.pallas import tpu as pltpu
from jax.sharding import PartitionSpec as P

HEADS = 12
PATCH_SMALL = 196
PATCH_LARGE = 576
AXES = ("dp", "fsdp")
bf16 = jnp.bfloat16
f32 = jnp.float32
NN = (((1,), (0,)), ((), ()))
NT = (((1,), (1,)), ((), ()))
TN = (((0,), (0,)), ((), ()))
VMEM_LIMIT = 60 * 2**20
TILE = 304
ATILE = 304
AHEAD = 1
MTILE = 304
MAHEAD = 1
LTILE = 608
LSUB = 304
BOT = 304
BTILE = 304
BAHEAD = 1
LOG2E = 1.4426950408889634


def dot(a, b, dims):
    return lax.dot_general(a, b, dims, preferred_element_type=f32)


def params(n):
    return pltpu.CompilerParams(
        vmem_limit_bytes=VMEM_LIMIT, dimension_semantics=("arbitrary",) * n
    )


def cost(*_):
    return pl.CostEstimate(flops=1, bytes_accessed=1, transcendentals=0)


def tile_of(seq):
    return TILE if seq % TILE == 0 else seq


def once(shape):
    return pl.BlockSpec(
        shape, lambda *_: (0,) * len(shape), pipeline_mode=pl.Buffered(buffer_count=1)
    )


def shape_of(shape, dtype):
    return jax.ShapeDtypeStruct(shape, dtype)


class Flights:
    def __init__(self):
        self.waiting = []
        self.flying = []

    def add(self, steps, lengths):
        job = {"steps": steps, "lengths": list(lengths), "result": None}
        self.advance(job, None)
        return job

    def advance(self, job, came):
        try:
            sends = job["steps"].send(came) if came is not None else next(job["steps"])
        except StopIteration as stop:
            job["result"] = lax.optimization_barrier(stop.value)
            return
        length = job["lengths"].pop(0) if job["lengths"] else 1
        self.waiting.append((job, sends, length))

    def depart(self):
        for job, sends, length in self.waiting:
            came = [lax.ppermute(array, AXES, pairs) for array, pairs in sends]
            self.flying.append([job, came, length])
        self.waiting = []

    def run(self, kernel, operand, *others):
        arrays = [array for _, sends, _ in self.waiting for array, _ in sends]
        if arrays:
            operand, arrays = lax.optimization_barrier((operand, arrays))
            left = iter(arrays)
            self.waiting = [
                (job, [(next(left), pairs) for _, pairs in sends], length)
                for job, sends, length in self.waiting
            ]
        self.depart()
        out = kernel(operand, *others)
        for flight in self.flying:
            flight[2] -= 1
        landed = [flight for flight in self.flying if flight[2] <= 0]
        self.flying = [flight for flight in self.flying if flight[2] > 0]
        if landed:
            out, came = lax.optimization_barrier((out, [flight[1] for flight in landed]))
            for flight, got in zip(landed, came):
                self.advance(flight[0], got)
        return out

    def finish(self, turns=None):
        turn = 0
        while (self.waiting or self.flying) and turn != turns:
            turn += 1
            self.depart()
            for flight in self.flying:
                flight[2] -= 1
            landed = [flight for flight in self.flying if turns is None or flight[2] <= 0]
            self.flying = [flight for flight in self.flying if not (turns is None or flight[2] <= 0)]
            cames = lax.optimization_barrier([flight[1] for flight in landed])
            for flight, came in zip(landed, cames):
                self.advance(flight[0], came)


def bit_groups(mesh):
    inner = int(math.log2(mesh.shape["fsdp"]))
    outer = int(math.log2(mesh.shape["dp"]))
    rest = [list(range(b, min(b + 2, inner))) for b in range(1, inner, 2)]
    return [0], list(range(inner, inner + outer)), rest


def position(me, bits):
    spot = 0
    for place, bit in enumerate(bits):
        spot = spot + ((me >> bit) & 1) * (1 << place)
    return spot


def partners(count, bits):
    swaps = []
    for step in range(1, 1 << len(bits)):
        mask = 0
        for place, bit in enumerate(bits):
            if (step >> place) & 1:
                mask |= 1 << bit
        swaps.append((step, [(i, i ^ mask) for i in range(count)]))
    return swaps


def gather_steps(shard, mesh, groups):
    count = mesh.size
    me = lax.axis_index(AXES)
    bits = int(math.log2(count))
    rows, columns = shard.shape
    held = shard.reshape((1,) * bits + (rows, columns))
    for group in groups:
        swaps = partners(count, group)
        came = yield [(held, pairs) for _, pairs in swaps]
        shape = list(held.shape)
        for bit in group:
            shape[bits - 1 - bit] = 2
        whole = jnp.zeros(shape, shard.dtype)
        for (step, _), got in zip([(0, None)] + swaps, [held] + came):
            start = [0] * len(shape)
            for place, bit in enumerate(group):
                start[bits - 1 - bit] = ((me >> bit) & 1) ^ ((step >> place) & 1)
            whole = lax.dynamic_update_slice(whole, got, start)
        held = whole
    return held.reshape(count * rows, columns)


def pick(array, axis, index):
    return lax.dynamic_slice_in_dim(array, index, 1, axis)


def total(terms, axis, index, kind):
    return sum(pick(term, axis, index).astype(f32) for term in terms).astype(kind)


def sum_steps(parts, mesh, kind):
    count = mesh.size
    core, outer, rest = bit_groups(mesh)
    me = lax.axis_index(AXES)
    rows, columns = parts.shape[0] // count, parts.shape[1]
    rest_size = mesh.shape["fsdp"] // 2
    held = parts.reshape(mesh.shape["dp"], rest_size, 2, rows, columns)
    spot = position(me, core)
    (got,) = yield [(pick(held, 2, spot ^ 1).astype(kind), partners(count, core)[0][1])]
    terms = [pick(held, 2, spot), got]
    split = 2 if len(outer) == 2 and columns % 256 == 0 else 1
    width = columns // split
    shape = (2,) * len(outer) + (rest_size, 1, rows, width)
    pieces = []
    for piece in range(split):
        own = [term[..., piece * width : (piece + 1) * width].reshape(shape) for term in terms]
        order = list(range(len(outer)))
        pieces.append((own, order if piece == 0 else order[::-1]))
    for turn in range(len(outer)):
        sends = []
        for own, order in pieces:
            axis = order[turn]
            bit = outer[len(outer) - 1 - axis]
            mine = position(me, [bit])
            sends.append((total(own, axis, mine ^ 1, kind), partners(count, [bit])[0][1]))
        came = yield sends
        pieces = [
            ([pick(term, order[turn], position(me, [outer[len(outer) - 1 - order[turn]]])) for term in own] + [got], order)
            for (own, order), got in zip(pieces, came)
        ]
    left = rest_size
    pieces = [[term.reshape(rest_size, rows, width) for term in own] for own, _ in pieces]
    for bits in reversed(rest):
        size = 1 << len(bits)
        left //= size
        pieces = [[term.reshape(size, left, rows, width) for term in own] for own in pieces]
        spot = position(me, bits)
        swaps = partners(count, bits)
        sends = [
            (jnp.concatenate([total(own, 0, spot ^ step, kind) for own in pieces], -1), pairs)
            for step, pairs in swaps
        ]
        came = yield sends
        pieces = [
            [pick(term, 0, spot) for term in own]
            + [got[..., place * width : (place + 1) * width] for got in came]
            for place, own in enumerate(pieces)
        ]
    sums = [sum(term.astype(f32) for term in own).reshape(rows, width) for own in pieces]
    return jnp.concatenate(sums, -1)


def send_sum_kernel(where, *refs, sizes):
    at = 0
    for size, out in zip(sizes, refs[sum(sizes) :]):
        out[...] = sum(term[...].astype(f32) for term in refs[at : at + size]).astype(out.dtype)
        at += size


def fold_first(where, keep, came):
    _, _, left, rows, columns = keep.shape
    cut = columns // 2
    spec_a = pl.BlockSpec((None, 2, 2, rows, cut), lambda j, where: ((where[1] // 2) ^ 1, 0, j, 0, 0))
    spec_b = pl.BlockSpec((2, None, 2, rows, cut), lambda j, where: (0, (where[1] % 2) ^ 1, j, 0, 1))
    return pl.pallas_call(
        functools.partial(send_sum_kernel, sizes=[2, 2]),
        grid_spec=pltpu.PrefetchScalarGridSpec(
            num_scalar_prefetch=1,
            grid=(left // 2,),
            in_specs=[spec_a, spec_a, spec_b, spec_b],
            out_specs=[pl.BlockSpec((2, 2, rows, cut), lambda j, where: (0, j, 0, 0))] * 2,
        ),
        out_shape=[shape_of((2, left, rows, cut), bf16)] * 2,
        compiler_params=params(1),
        cost_estimate=cost(),
        name="fold_first",
    )(where, keep, came, keep, came)


def fold_second(where, keep, came, came_a, came_b):
    _, _, left, rows, columns = keep.shape
    cut = columns // 2
    spec_a = pl.BlockSpec(
        (None, None, 2, rows, cut), lambda j, where: (where[1] // 2, (where[1] % 2) ^ 1, j, 0, 0)
    )
    spec_b = pl.BlockSpec(
        (None, None, 2, rows, cut), lambda j, where: ((where[1] // 2) ^ 1, where[1] % 2, j, 0, 1)
    )
    half_a = pl.BlockSpec((None, 2, rows, cut), lambda j, where: ((where[1] % 2) ^ 1, j, 0, 0))
    half_b = pl.BlockSpec((None, 2, rows, cut), lambda j, where: ((where[1] // 2) ^ 1, j, 0, 0))
    return pl.pallas_call(
        functools.partial(send_sum_kernel, sizes=[3, 3]),
        grid_spec=pltpu.PrefetchScalarGridSpec(
            num_scalar_prefetch=1,
            grid=(left // 2,),
            in_specs=[spec_a, spec_a, half_a, spec_b, spec_b, half_b],
            out_specs=[pl.BlockSpec((2, rows, cut), lambda j, where: (j, 0, 0))] * 2,
        ),
        out_shape=[shape_of((left, rows, cut), bf16)] * 2,
        compiler_params=params(1),
        cost_estimate=cost(),
        name="fold_second",
    )(where, keep, came, came_a, keep, came, came_b)


def line_first_kernel(where, *refs):
    *terms, keep, send = refs
    fast = where[2] % 2
    cut = terms[0].shape[-1]
    for slow in range(2):
        for place, out in ((slow * 2 + fast, keep), (slow * 2 + (fast ^ 1), send)):
            for half in range(2):
                own = terms[4 * half : 4 * half + 4]
                lanes = slice(half * cut, (half + 1) * cut)
                out[slow, :, lanes] = sum(term[place].astype(f32) for term in own).astype(out.dtype)


def line_first(where, keep, came, came_a, came_b, last_a, last_b):
    _, _, size, rows, columns = keep.shape
    cut = columns // 2
    whole = lambda half: pl.BlockSpec(
        (None, None, size, rows, cut), lambda j, where: (where[1] // 2, where[1] % 2, 0, 0, half)
    )
    half_a = pl.BlockSpec((None, size, rows, cut), lambda j, where: (where[1] % 2, 0, 0, 0))
    half_b = pl.BlockSpec((None, size, rows, cut), lambda j, where: (where[1] // 2, 0, 0, 0))
    last = pl.BlockSpec((size, rows, cut), lambda j, where: (0, 0, 0))
    return pl.pallas_call(
        line_first_kernel,
        grid_spec=pltpu.PrefetchScalarGridSpec(
            num_scalar_prefetch=1,
            grid=(1,),
            in_specs=[whole(0), whole(0), half_a, last, whole(1), whole(1), half_b, last],
            out_specs=[once((size // 2, rows, columns))] * 2,
        ),
        out_shape=[shape_of((size // 2, rows, columns), bf16)] * 2,
        compiler_params=params(1),
        cost_estimate=cost(),
        name="line_first",
    )(where, keep, came, came_a, last_a, keep, came, came_b, last_b)


def swap_steps(send, mesh):
    core, _, _ = bit_groups(mesh)
    (came,) = yield [(send, partners(mesh.size, core)[0][1])]
    return came


def part_of(terms, axis, index, kind):
    total = None
    for term in terms:
        if term.shape[axis] != 1:
            term = pick(term, axis, index)
        total = term.astype(f32) if total is None else total + term.astype(f32)
    return total.astype(kind)


def plane_steps(keep, came, mesh):
    count = mesh.size
    _, outer, rest = bit_groups(mesh)
    spot = position(lax.axis_index(AXES), outer)
    size = 1 << len(outer)
    terms = [array.reshape((size, 1 << len(rest[0])) + keep.shape[1:]) for array in (keep, came)]
    sends = [part_of(terms, 0, spot ^ step, bf16)[0] for step in range(1, size)]
    came = yield [(array, pairs) for array, (_, pairs) in zip(sends, partners(count, outer))]
    return [pick(term, 0, spot)[0] for term in terms] + came


def line_steps(groups, mesh):
    count = mesh.size
    _, _, rest = bit_groups(mesh)
    spot = position(lax.axis_index(AXES), rest[0])
    side = lambda index, kind: jnp.concatenate([part_of(terms, 0, index, kind)[0] for terms in groups], -1)
    came = yield [(side(spot ^ step, bf16), pairs) for step, pairs in partners(count, rest[0])]
    return side(spot, f32) + sum(array.astype(f32) for array in came)


def fold_sum_steps(keep, send, where, mesh):
    count = mesh.size
    core, outer, rest = bit_groups(mesh)
    (came,) = yield [(send, partners(count, core)[0][1])]
    shape = (2, 2, 1 << len(rest[0]), keep.shape[0] * 2 // count, keep.shape[1])
    keep, came = keep.reshape(shape), came.reshape(shape)
    fast, slow = (partners(count, [bit])[0][1] for bit in outer)
    send_a, send_b = fold_first(where, keep, came)
    came_a, came_b = yield [(send_a, slow), (send_b, fast)]
    send_a, send_b = fold_second(where, keep, came, came_a, came_b)
    last_a, last_b = yield [(send_a, fast), (send_b, slow)]
    keep, send = line_first(where, keep, came, came_a, came_b, last_a, last_b)
    (came,) = yield [(send, partners(count, [rest[0][0]])[0][1])]
    me = lax.axis_index(AXES)
    spot = position(me, [rest[0][1]])
    both = [keep, came]
    (last,) = yield [(total(both, 0, spot ^ 1, bf16), partners(count, [rest[0][1]])[0][1])]
    done = (total(both, 0, spot, f32) + last.astype(f32)).reshape(2, shape[3] // 2, shape[4])
    spot = position(me, core)
    (came,) = yield [(pick(done, 0, spot ^ 1), partners(count, core)[0][1])]
    own, came = pick(done, 0, spot)[0], came[0]
    return jnp.where(spot == 0, own, came), jnp.where(spot == 0, came, own)


def small_sum_steps(parts, mesh):
    count = mesh.size
    core, outer, rest = bit_groups(mesh)
    groups = [core, outer, *reversed(rest)]
    order = [outer, *reversed(rest), core]
    me = lax.axis_index(AXES)
    columns = parts.shape[1]
    held = parts.reshape([1 << len(bits) for bits in order] + [columns])
    for bits in groups:
        axis = order.index(bits)
        spot = position(me, bits)
        swaps = partners(count, bits)
        came = yield [(pick(held, axis, spot ^ step), pairs) for step, pairs in swaps]
        held = pick(held, axis, spot) + sum(came)
    return held.reshape(columns)


def cut_by_core(mesh):
    _, outer, rest = bit_groups(mesh)
    return len(outer) == 2 and len(rest) == 1 and len(rest[0]) == 2


def store_cut(core, outs, lanes, value, rows):
    if len(outs) == 1:
        outs[0][:, lanes] = value.astype(bf16)
        return
    keep, send = outs
    for parity in range(2):
        @pl.when(core == parity)
        def _():
            for device in range(value.shape[0] // rows):
                out = keep if device % 2 == parity else send
                out[device // 2, :, lanes] = value[device * rows : (device + 1) * rows, :].astype(bf16)


def cut_shapes(width, columns, chunk, index, rows):
    if not rows:
        spec = pl.BlockSpec((width, chunk), lambda j, *_: (0, index(j)))
        return [spec], [shape_of((width, columns), bf16)]
    blocks = width // rows // 2
    spec = pl.BlockSpec((blocks, rows, chunk), lambda j, *_: (0, 0, index(j)))
    return [spec] * 2, [shape_of((blocks, rows, columns), bf16)] * 2


def normalize(values):
    center = values - jnp.mean(values, -1, keepdims=True)
    scale = lax.rsqrt(jnp.mean(center * center, -1, keepdims=True) + 1e-05)
    return center * scale, scale


def norm_back(grad, gain, unit, scale):
    inner = grad * gain
    return scale * (
        inner
        - jnp.mean(inner, -1, keepdims=True)
        - unit * jnp.mean(inner * unit, -1, keepdims=True)
    )


def gelu_parts(u):
    phi = 0.5 + 0.5 * lax.erf(u * 0.7071067811865476)
    slope = phi + u * (0.3989422804014327 * jnp.exp2((u * u) * (-0.5 * LOG2E)))
    return u * phi, slope


def column_sum(values):
    return jnp.sum(values, 0, keepdims=True)


def accumulate(ref, value, first):
    @pl.when(first)
    def _():
        ref[...] = value

    @pl.when(jnp.logical_not(first))
    def _():
        ref[...] += value


def two_heads(block, padded):
    seq = block.shape[0]
    first = lax.broadcasted_iota(jnp.int32, block.shape, 1) < 64
    zero = jnp.zeros_like(block)
    pad = jnp.zeros((padded - seq, 128), block.dtype)
    return jnp.concatenate(
        [jnp.where(first, block, zero), pad, jnp.where(first, zero, block), pad], 0
    )


def attend_kernel(valid, *refs, tile, padded, first, pairs):
    if first:
        tokens, gain, shift, weight, bias, normed, joined, mixed, raised_out, inverse = refs
    else:
        (
            normed, weight, bias, tokens, mixed_first, bias_out, gain, shift,
            joined, mixed, raised_out, inverse, middle, normed_two,
        ) = refs
    seq, span = joined.shape
    for start in range(0, seq, tile):
        rows = slice(start, start + tile)
        if first:
            unit, _ = normalize(tokens[rows, :].astype(f32))
            low = (unit * gain[...] + shift[...]).astype(bf16)
            normed[rows, :] = low
        else:
            low = normed[rows, :]
        joined[rows, :] = (dot(low, weight[:, :span], NN) + bias[...]).astype(bf16)

    column = lax.broadcasted_iota(jnp.int32, (1, padded), 1)
    mask = jnp.where(column < valid[pl.program_id(0)], 0.0, -1e30).astype(f32)
    places = [(pair, start) for pair in range(pairs) for start in range(0, seq, ATILE)]
    keys, values = {}, {}
    row = lax.broadcasted_iota(jnp.int32, (2 * padded, 128), 0)
    lane = lax.broadcasted_iota(jnp.int32, (2 * padded, 128), 1)
    ones = jnp.where((row < padded) == (lane < 64), 1.0, 0.0).astype(bf16)

    def scores_at(pair, start):
        if pair not in keys:
            at = pair * 384
            keys[pair] = two_heads(joined[:, at + 128 : at + 256], padded)
            values[pair] = jnp.concatenate([two_heads(joined[:, at + 256 : at + 384], padded), ones], 1)
        return dot(joined[start : start + ATILE, pair * 384 : pair * 384 + 128], keys[pair], NT)

    ahead = [scores_at(*place) for place in places[:AHEAD]]
    for index, (pair, start) in enumerate(places):
        rows = slice(start, start + ATILE)
        if index + AHEAD < len(places):
            ahead.append(scores_at(*places[index + AHEAD]))
        scores = ahead.pop(0)
        halves = []
        for head in range(2):
            part = scores[:, head * padded : (head + 1) * padded] * (0.125 * LOG2E) + mask
            halves.append(jnp.exp2(part - jnp.max(part, 1, keepdims=True)).astype(bf16))
        raised = jnp.concatenate(halves, 1)
        raised_out[pair, rows, :] = raised
        both = dot(raised, values[pair], NN)
        scale = 1.0 / both[:, 128:]
        inverse[rows, pair * 128 : (pair + 1) * 128] = scale
        mixed[rows, pair * 128 : (pair + 1) * 128] = (both[:, :128] * scale).astype(bf16)
    if first:
        return
    width = tokens.shape[1]
    for start in range(0, seq, tile):
        rows = slice(start, start + tile)
        value = tokens[rows, :].astype(f32) + bias_out[...]
        value = value + dot(mixed_first[rows, :], weight[: width // 2, -width:], NN)
        value = value + dot(mixed[rows, :], weight[width // 2 :, -width:], NN)
        middle[rows, :] = value
        unit, _ = normalize(value)
        normed_two[rows, :] = (unit * gain[...] + shift[...]).astype(bf16)


def attend(start, valid, weight, bias, seq, norm=None, after=None):
    rows, width = start.shape
    span = bias.shape[1]
    pairs = span // 384
    items = rows // seq
    padded = -(-seq // 128) * 128
    row = lambda w: pl.BlockSpec((seq, w), lambda i, *_: (i, 0))
    one = once((1, width))
    main = [once(weight.shape), once((1, span))]
    if norm:
        specs, arrays = [row(width), one, one, *main], [start, *norm, weight, bias]
    else:
        specs = [row(width), *main, row(width), row(width // 2), one, one, one]
        arrays = [start, weight, bias, *after]
    outs = [
        row(span),
        row(span // 3),
        pl.BlockSpec((None, pairs, seq, 2 * padded), lambda i, *_: (i, 0, 0, 0)),
        row(span // 3),
    ]
    shapes = [
        shape_of((rows, span), bf16),
        shape_of((rows, span // 3), bf16),
        shape_of((items, pairs, seq, 2 * padded), bf16),
        shape_of((rows, span // 3), f32),
    ]
    if norm:
        outs, shapes = [row(width)] + outs, [shape_of((rows, width), bf16)] + shapes
    else:
        outs += [row(width)] * 2
        shapes += [shape_of((rows, width), f32), shape_of((rows, width), bf16)]
    return pl.pallas_call(
        functools.partial(attend_kernel, tile=tile_of(seq), padded=padded, first=bool(norm), pairs=pairs),
        grid_spec=pltpu.PrefetchScalarGridSpec(
            num_scalar_prefetch=1, grid=(items,), in_specs=specs, out_specs=outs
        ),
        out_shape=shapes,
        compiler_params=params(1),
        cost_estimate=cost(),
        name="attend",
    )(valid, *arrays)


def attend_back_kernel(where, *refs, pairs, extra, spare, cut):
    lists = [refs[kind * pairs : (kind + 1) * pairs] for kind in range(5)]
    joined, mixed_grad, mixed, raised, inverse = lists
    normed, weight, *rest = refs[5 * pairs :]
    if extra:
        mixed_a, mixed_b, low_grad, *rest, total_out = rest
    joined_grad, column, gain_sum, shift_sum, *outs, held, scaled, total = rest
    item = pl.program_id(0)
    seq, span = joined_grad.shape
    padded = raised[0].shape[1] // 2
    tile = BTILE if seq % BTILE == 0 else seq
    first = lax.broadcasted_iota(jnp.int32, (tile, 128), 1) < 64
    places = [(pair, start) for pair in range(pairs) for start in range(0, seq, tile)]
    keys, values = {}, {}

    def prob_grad_at(pair, start):
        if pair not in keys:
            keys[pair] = two_heads(joined[pair][:, 128:256], padded)
            values[pair] = two_heads(joined[pair][:, 256:], padded)
        rows = slice(start, start + tile)
        grad = (mixed_grad[pair][rows, :].astype(f32) * inverse[pair][rows, :]).astype(bf16)
        scaled[pair, rows, :] = grad
        return grad, dot(grad, values[pair], NT)

    def own_half(both):
        return jnp.concatenate([both[:64, :padded], both[64:, padded:]], 0).T[:seq]

    ahead = [prob_grad_at(*place) for place in places[:BAHEAD]]
    for index, (pair, start) in enumerate(places):
        rows = slice(start, start + tile)
        at = pair * 384
        if index + BAHEAD < len(places):
            ahead.append(prob_grad_at(*places[index + BAHEAD]))
        grad, prob_grad = ahead.pop(0)
        product = grad.astype(f32) * mixed[pair][rows, :].astype(f32)
        zero = jnp.zeros_like(product)
        halves = []
        for head in range(2):
            own = jnp.where(first, product, zero) if head == 0 else jnp.where(first, zero, product)
            centre = jnp.sum(own, 1, keepdims=True)
            half = slice(head * padded, (head + 1) * padded)
            halves.append((raised[pair][rows, half].astype(f32) * (prob_grad[:, half] - centre)).astype(bf16))
        score_grad = jnp.concatenate(halves, 1)
        held[rows, :] = score_grad
        joined_grad[rows, at : at + 128] = (dot(score_grad, keys[pair], NN) * 0.125).astype(bf16)
        if start + tile == seq:
            joined_grad[:, at + 128 : at + 256] = (
                own_half(dot(joined[pair][:, :128].T, held[...], NN)) * 0.125
            ).astype(bf16)
            joined_grad[:, at + 256 : at + 384] = own_half(
                dot(scaled[pair].T, raised[pair][...], NN)
            ).astype(bf16)

    value = joined_grad[...]
    accumulate(total, dot(normed[...], value, TN), item == 0)
    accumulate(column, column_sum(value.astype(f32)), item == 0)
    if extra:
        both = [dot(mixed_a[...], low_grad[...], TN), dot(mixed_b[...], low_grad[...], TN)]
        accumulate(total_out, jnp.concatenate(both, 0), item == 0)

    @pl.when(item == pl.num_programs(0) - 1)
    def _():
        store_cut(where[0], outs, slice(0, span), total[...], cut)
        if spare:
            for out in outs:
                out[..., span:] = jnp.zeros(out.shape[:-1] + (spare,), bf16)
        wide = weight[...].astype(f32)
        for ref, product in ((gain_sum, wide * total[...]), (shift_sum, wide * column[...])):
            row = jnp.sum(product, 1, keepdims=True)
            ref[...] = jnp.broadcast_to(row, (row.shape[0], 128)).T[:1]
        if extra:
            store_cut(where[0], outs, slice(span, span + total_out.shape[1]), total_out[...], cut)


def attend_back(mixed_grad, where, joined, mixed, raised, inverse, normed, weight, seq, part, cut, others=(), spare=0):
    rows, width = normed.shape
    items, in_part, _, keys = raised.shape
    pairs = in_part
    chosen = range(pairs)
    span = 384 * pairs
    row = lambda w, off=0: pl.BlockSpec((seq, w), lambda i, *_: (i, off))
    each = lambda w, off=0: [row(w, off + pair) for pair in chosen]
    weights = [
        pl.BlockSpec((None, None, seq, keys), functools.partial(lambda at, i, *_: (i, at, 0, 0), pair))
        for pair in chosen
    ]
    columns = span + (width if others else 0) + spare
    one = pl.BlockSpec((1, width), lambda i, *_: (0, 0))
    specs, shapes = cut_shapes(width, columns, columns, lambda j: 0, cut)
    return pl.pallas_call(
        functools.partial(
            attend_back_kernel, pairs=pairs, extra=bool(others), spare=spare, cut=cut
        ),
        grid_spec=pltpu.PrefetchScalarGridSpec(
            num_scalar_prefetch=1,
            grid=(items,),
            in_specs=[
                *each(384), *each(128, part * in_part), *each(128), *weights, *each(128), row(width)
            ]
            + [once((width, span))]
            + [row(array.shape[1]) for array in others],
            out_specs=[row(span), pl.BlockSpec((1, span), lambda i, *_: (0, 0)), one, one] + specs,
            scratch_shapes=[
                pltpu.VMEM((seq, keys), bf16),
                pltpu.VMEM((pairs, seq, 128), bf16),
                pltpu.VMEM((width, span), f32),
            ]
            + ([pltpu.VMEM((width, width), f32)] if others else []),
        ),
        out_shape=[shape_of((rows, span), bf16), shape_of((1, span), f32)]
        + [shape_of((1, width), f32)] * 2
        + shapes,
        compiler_params=params(1),
        cost_estimate=cost(),
        name="attend_back",
    )(
        where, *[joined] * pairs, *[mixed_grad] * pairs, *[mixed] * pairs, *[raised] * pairs,
        *[inverse] * pairs, normed, weight, *others,
    )


def mlp_kernel(
    valid, where, normed, cotangent, up, down, bias_up,
    active, hidden_grad, up_sum, *rest, seq, tile, cut,
):
    *outs, grad = rest
    rows, width = normed.shape

    @pl.when(pl.program_id(0) == 0)
    def _():
        place = lax.broadcasted_iota(jnp.int32, (seq, 1), 0)
        for item in range(rows // seq):
            span = slice(item * seq, (item + 1) * seq)
            grad[span, :] = jnp.where(place < valid[item], cotangent[span, :].astype(f32), 0.0).astype(bf16)

    def ahead_of(start):
        span = slice(start, start + MTILE)
        return dot(normed[span, :], up[...], NN), dot(grad[span, :], down[...], NT)

    column = jnp.zeros(up_sum.shape, f32)
    starts = list(range(0, rows, MTILE))
    ahead = [ahead_of(start) for start in starts[:MAHEAD]]
    for index, start in enumerate(starts):
        span = slice(start, start + MTILE)
        if index + MAHEAD < len(starts):
            ahead.append(ahead_of(starts[index + MAHEAD]))
        hidden, wide = ahead.pop(0)
        value, slope = gelu_parts(hidden + bias_up[...])
        low = (slope * wide).astype(bf16)
        active[span, :] = value.astype(bf16)
        hidden_grad[span, :] = low
        column = column + column_sum(low.astype(f32))
    up_sum[...] = column
    first = dot(normed[...], hidden_grad[...], TN).astype(bf16)
    second = dot(active[...], grad[...], TN).astype(bf16)
    if cut:
        keep, send = outs
        for core in range(2):
            @pl.when(where[0] == core)
            def _():
                (keep, send)[core][...] = first
                (send, keep)[core][...] = second
    else:
        outs[0][:, :width] = first
        outs[0][:, width:] = second


def mlp(normed, valid, where, cotangent, both, bias_up, seq, cut):
    rows, width = normed.shape
    wide = both.shape[1] // 2
    chunks = wide // width
    whole = once((rows, width))
    square = lambda off: pl.BlockSpec((width, width), lambda j, *_: (0, j + off))
    row = pl.BlockSpec((rows, width), lambda j, *_: (0, j))
    one = pl.BlockSpec((1, width), lambda j, *_: (0, j))
    if cut:
        specs = [pl.BlockSpec((width, width), lambda j, *_: (0, j))] * 2
        shapes = [shape_of((width, wide), bf16)] * 2
    else:
        specs, shapes = cut_shapes(width, 2 * wide, 2 * width, lambda j: j, 0)
    return pl.pallas_call(
        functools.partial(mlp_kernel, seq=seq, tile=tile_of(seq), cut=cut),
        grid_spec=pltpu.PrefetchScalarGridSpec(
            num_scalar_prefetch=2,
            grid=(chunks,),
            in_specs=[whole, whole, square(0), square(chunks), one],
            out_specs=[row, row, one] + specs,
            scratch_shapes=[pltpu.VMEM((rows, width), bf16)],
        ),
        out_shape=[
            shape_of((rows, width * chunks), bf16),
            shape_of((rows, width * chunks), bf16),
            shape_of((1, width * chunks), f32),
        ]
        + shapes,
        compiler_params=params(1),
        cost_estimate=cost(),
        name="mlp",
    )(valid, where, normed, cotangent, both, both, bias_up)


def block_out_kernel(valid, active, downs, middle, bias_down, *rest, seq, begin):
    block_out = rest[-1]
    tile, width = middle.shape
    step = pl.program_id(0) + begin // tile
    place = lax.broadcasted_iota(jnp.int32, (tile, 1), 0) + lax.rem(step, seq // tile) * tile
    value = middle[...] + bias_down[...]
    for at in range(0, downs.shape[1], width):
        value = value + dot(active[:, at : at + width], downs[:, at : at + width], NN)
    block_out[...] = jnp.where(place < valid[step // (seq // tile)], value, 0.0).astype(bf16)


def half_of(both, second):
    width, columns = both.shape
    return pl.BlockSpec(
        (width, columns // 2), lambda j, *_: (0, second), pipeline_mode=pl.Buffered(buffer_count=1)
    )


def block_out_of(middle, valid, active, both, bias_down, seq, begin, end, before=None):
    rows, width = middle.shape
    tile = BOT if seq % BOT == 0 else seq
    skip = begin // tile
    row = lambda w: pl.BlockSpec((tile, w), lambda j, *_: (j + skip, 0))
    specs = [row(active.shape[1]), half_of(both, 1), row(width), once((1, width))]
    arrays = [active, both, middle, bias_down]
    aliases = {}
    if before is not None:
        aliases = {len(arrays) + 1: 0}
        specs.append(pl.BlockSpec(memory_space=pl.ANY))
        arrays.append(before)
    return pl.pallas_call(
        functools.partial(block_out_kernel, seq=seq, begin=begin),
        grid_spec=pltpu.PrefetchScalarGridSpec(
            num_scalar_prefetch=1,
            grid=((end - begin) // tile,),
            in_specs=specs,
            out_specs=row(width),
        ),
        out_shape=shape_of((rows, width), bf16),
        input_output_aliases=aliases,
        compiler_params=params(1),
        cost_estimate=cost(),
        name="block_out",
    )(valid, *arrays)


def middle_back_kernel(
    valid, hidden_grad, ups, middle, cotangent, gain, weight_a, weight_b,
    low_grad, mixed_grad, gain_sum, shift_sum, bias_sum, down_sum, *, seq, sub,
):
    step = pl.program_id(0)
    tile, width = middle.shape
    each = seq // tile
    starts = list(range(0, tile, sub))
    ahead = [dot(hidden_grad[:sub, :], ups[...], NT)]
    sums = [jnp.zeros((1, width), f32)] * 4
    for index, start in enumerate(starts):
        rows = slice(start, start + sub)
        if index + 1 < len(starts):
            ahead.append(dot(hidden_grad[start + sub : start + 2 * sub, :], ups[...], NT))
        grad = ahead.pop(0)
        unit, scale = normalize(middle[rows, :])
        place = lax.broadcasted_iota(jnp.int32, (sub, 1), 0) + (lax.rem(step, each) * tile + start)
        kept = jnp.where(place < valid[step // each], cotangent[rows, :].astype(f32), 0.0)
        low = (kept + norm_back(grad, gain[...], unit, scale)).astype(bf16)
        low_grad[rows, :] = low
        mixed_grad[rows, :] = (
            dot(low[:, : width // 2], weight_a[...], NT) + dot(low[:, width // 2 :], weight_b[...], NT)
        ).astype(bf16)
        terms = (grad * unit, grad, low.astype(f32), kept)
        sums = [before + column_sum(term) for before, term in zip(sums, terms)]
    for ref, value in zip((gain_sum, shift_sum, bias_sum, down_sum), sums):
        accumulate(ref, value, step == 0)


def middle_back(middle, valid, hidden_grad, both, cotangent, gain, weight, seq):
    rows, width = middle.shape
    tile = LTILE if seq % LTILE == 0 else seq
    sub = LSUB if tile % LSUB == 0 else tile
    row = lambda w: pl.BlockSpec((tile, w), lambda j, *_: (j, 0))
    one = pl.BlockSpec((1, width), lambda j, *_: (0, 0))
    half = width // 2
    at = weight.shape[1] // half - 2
    halves = [
        pl.BlockSpec((width, half), lambda j, *_: (0, at), pipeline_mode=pl.Buffered(buffer_count=1)),
        pl.BlockSpec((width, half), lambda j, *_: (0, at + 1), pipeline_mode=pl.Buffered(buffer_count=1)),
    ]
    return pl.pallas_call(
        functools.partial(middle_back_kernel, seq=seq, sub=sub),
        grid_spec=pltpu.PrefetchScalarGridSpec(
            num_scalar_prefetch=1,
            grid=(rows // tile,),
            in_specs=[
                row(hidden_grad.shape[1]), half_of(both, 0), row(width), row(width),
                once((1, width)), *halves,
            ],
            out_specs=[row(width), row(width)] + [one] * 4,
        ),
        out_shape=[shape_of((rows, width), bf16)] * 2 + [shape_of((1, width), f32)] * 4,
        compiler_params=params(1),
        cost_estimate=cost(),
        name="middle_back",
    )(valid, hidden_grad, both, middle, cotangent, gain, weight, weight)


def input_back_kernel(*refs, spans, sub):
    grads = refs[: len(spans)]
    weights = refs[len(spans) : len(spans) + 2]
    tokens, low_grad, gain, input_grad = refs[len(spans) + 2 :]
    tile, width = tokens.shape

    def ahead_of(start):
        rows = slice(start, start + sub)
        terms = [
            dot(grad[rows, :], weights[which][:, lanes], NT) for grad, (which, lanes) in zip(grads, spans)
        ]
        return sum(terms[1:], terms[0])

    starts = list(range(0, tile, sub))
    ahead = [ahead_of(0)]
    for index, start in enumerate(starts):
        rows = slice(start, start + sub)
        if index + 1 < len(starts):
            ahead.append(ahead_of(start + sub))
        grad = ahead.pop(0)
        unit, scale = normalize(tokens[rows, :].astype(f32))
        full = low_grad[rows, :].astype(f32) + norm_back(grad, gain[...], unit, scale)
        input_grad[rows, :] = full.astype(bf16)


def input_back(last, others, spans, weights, tokens, low_grad, gain, seq):
    rows, width = tokens.shape
    tile = LTILE if seq % LTILE == 0 else seq
    sub = LSUB if tile % LSUB == 0 else tile
    row = lambda w: pl.BlockSpec((tile, w), lambda i: (i, 0))
    grads = [*others, last]
    return pl.pallas_call(
        functools.partial(input_back_kernel, spans=spans, sub=sub),
        grid=(rows // tile,),
        in_specs=[row(grad.shape[1]) for grad in grads]
        + [once((width, spans[0][1].stop))] * 2
        + [row(width), row(width), once((1, width))],
        out_specs=row(width),
        out_shape=shape_of((rows, width), bf16),
        compiler_params=params(1),
        cost_estimate=cost(),
        name="input_back",
    )(*grads, *weights, tokens, low_grad, gain)


def local(mesh, tokens, cotangent, group, text_len, qkv_w, out_w, mlp_in, mlp_out, gains, biases):
    items, seq, width = tokens.shape
    rows = items * seq
    count = mesh.size
    share = width // count
    wide = mlp_in.shape[0] // share
    chunks = wide // width
    half = width // 2
    span = 3 * half
    valid = (PATCH_SMALL + (PATCH_LARGE - PATCH_SMALL) * group + text_len).astype(jnp.int32)
    flat = tokens.reshape(rows, width)
    cot = cotangent.reshape(rows, width)
    flights = Flights()
    me = lax.axis_index(AXES)
    core, outer, others = bit_groups(mesh)
    where = jnp.stack([position(me, core), position(me, outer), position(me, others[0])]).astype(jnp.int32)
    cut = share if cut_by_core(mesh) and share % 8 == 0 else 0

    def mlp_sums(arrays):
        if cut:
            return flights.add(fold_sum_steps(*arrays, where, mesh), [])
        return flights.add(sum_steps(arrays[0], mesh, bf16), [])

    def swap(arrays):
        return flights.add(swap_steps(arrays[1], mesh), []) if cut else None

    def by_pairs(matrix, part):
        rows = matrix.shape[0]
        cubes = matrix.reshape(rows, 3, 2, half // 128, 128)[:, :, part]
        return cubes.transpose(0, 2, 1, 3).reshape(rows, span)

    def by_kind(part_a, part_b):
        rows = part_a.shape[0]
        cubes = [piece[:, :span].reshape(rows, half // 128, 3, 128) for piece in (part_a, part_b)]
        return jnp.stack(cubes, 1).transpose(0, 3, 1, 2, 4).reshape(rows, 3 * width)

    own_up = mlp_in.reshape(share, count, chunks, share).transpose(0, 2, 1, 3).reshape(share, wide)
    own_down = mlp_out.reshape(chunks, share, width).transpose(1, 0, 2).reshape(share, wide)
    own_both = jnp.concatenate([own_up, own_down], 1)

    own_qkv = qkv_w.reshape(share, 3 * width)
    small = jnp.concatenate([gains, biases])
    small_rows = -(-small.shape[0] // 128)
    padded = jnp.pad(small, (0, small_rows * 128 - small.shape[0])).reshape(small_rows, 128)
    padded = jnp.pad(padded, ((0, share - small_rows), (0, 0)))
    both = lax.all_gather(own_both, AXES, axis=0, tiled=True)
    own_first = jnp.concatenate([by_pairs(own_qkv, 0), padded], 1)
    own_second = jnp.concatenate([by_pairs(own_qkv, 1), out_w.reshape(share, width)], 1)
    singles = [[bit] for group in reversed(others) for bit in reversed(group)]
    job = flights.add(gather_steps(own_first, mesh, [*others, outer, core]), [])
    second_job = flights.add(gather_steps(own_second, mesh, [*singles, outer, core]), [1] * len(singles) + [2])
    flights.finish(len(others) + 2)
    first = job["result"]
    small = first[:, span:].reshape(count, share, 128)[:, :small_rows]
    small = small.reshape(count, small_rows * 128).astype(f32)
    edge = gains.shape[0]
    gain = small[:, :edge].reshape(1, 2 * width)
    bias = small[:, edge : edge + biases.shape[0]].reshape(1, 6 * width + wide)
    gain_one, gain_two = gain[:, :width], gain[:, width:]
    bias_query, bias_value, bias_output, shift_one, shift_two, bias_down = (
        bias[:, p * width : (p + 1) * width] for p in range(6)
    )
    bias_up = bias[:, 6 * width :].reshape(count, chunks, share).transpose(1, 0, 2).reshape(1, wide)
    bias_joined = jnp.concatenate([bias_query, jnp.zeros_like(bias_query), bias_value], 1)
    bias_parts = [by_pairs(bias_joined, part) for part in range(2)]

    normed, joined_a, mixed_a, raised_a, inverse_a = flights.run(
        lambda x: attend(x, valid, first, bias_parts[0], seq, (gain_one, shift_one)), flat
    )
    flights.finish()
    second = second_job["result"]
    joined_b, mixed_b, raised_b, inverse_b, middle, normed_two = attend(
        normed, valid, second, bias_parts[1], seq,
        after=(flat, mixed_a, bias_output, gain_two, shift_two),
    )

    active, hidden_grad, up_sum, *mlp_grads = mlp(
        normed_two, valid, where, cot, both, bias_up, seq, cut
    )
    mlp_job = mlp_sums(mlp_grads)

    low_grad, mixed_grad, gain_two_sum, shift_two_sum, bias_out_sum, down_sum = flights.run(
        lambda x: middle_back(x, valid, hidden_grad, both, cot, gain_two, second, seq), middle
    )
    joined_grad_a, qkv_sum_a, gain_sum_a, shift_sum_a, *grads_a = flights.run(
        lambda x: attend_back(
            x, where, joined_a, mixed_a, raised_a, inverse_a, normed, first, seq, 0, cut,
            others=(mixed_a, mixed_b, low_grad),
        ),
        mixed_grad,
    )
    swap_a = swap(grads_a)
    joined_grad_b, qkv_sum_b, gain_sum_b, shift_sum_b, *grads_b = flights.run(
        lambda x: attend_back(
            x, where, joined_b, mixed_b, raised_b, inverse_b, normed, second, seq, 1, cut,
            spare=128 if cut else 0,
        ),
        mixed_grad,
    )
    shift_one_sum = shift_sum_a + shift_sum_b
    gain_one_sum = (gain_sum_a + gain_sum_b - shift_one * shift_one_sum) / gain_one
    joined_sums = by_kind(qkv_sum_a, qkv_sum_b)
    up_sum = up_sum.reshape(chunks, count, share).transpose(1, 0, 2).reshape(1, wide)
    gain_sums = jnp.concatenate([gain_one_sum, gain_two_sum], 1).reshape(count, edge)
    bias_sums = jnp.concatenate(
        [
            joined_sums[:, :width],
            joined_sums[:, 2 * width :],
            bias_out_sum,
            shift_one_sum,
            shift_two_sum,
            down_sum,
            up_sum,
        ],
        1,
    ).reshape(count, biases.shape[0])
    small = jnp.concatenate([gain_sums, bias_sums], 1)
    if cut:
        small = jnp.pad(small, ((0, 0), (0, small_rows * 128 - small.shape[1])))
        small = small.reshape(count // 2, 2, small_rows, 128)
        spot = position(me, core)
        grads_b = [
            lax.dynamic_update_slice(grads, pick(small, 1, place)[:, 0].astype(bf16), (0, 0, span))
            for grads, place in zip(grads_b, (spot, spot ^ 1))
        ]
        swap_b = swap(grads_b)
        plane_a = flights.add(plane_steps(grads_a[0], swap_a["result"], mesh), [])
    else:
        small_job = flights.add(small_sum_steps(small, mesh), [])
        sum_a, sum_b = (flights.add(sum_steps(grads, mesh, bf16), []) for (grads,) in (grads_a, grads_b))
    spans = ((0, slice(0, span)), (1, slice(0, span)))
    input_grad = flights.run(
        lambda x: input_back(x, [joined_grad_a], spans, [first, second], flat, low_grad, gain_one, seq),
        joined_grad_b,
    )
    if cut:
        plane_b = flights.add(plane_steps(grads_b[0], swap_b["result"], mesh), [])
    block_out = flights.run(
        lambda x: block_out_of(x, valid, active, both, bias_down, seq, 0, rows), middle
    )
    if cut:
        line = flights.add(line_steps([plane_a["result"], plane_b["result"]], mesh), [])
    flights.finish()
    if cut:
        edge_a = grads_a[0].shape[-1]
        total_a, total_b = line["result"][:, :edge_a], line["result"][:, edge_a:]
        small_total = total_b[:small_rows, span:].reshape(-1)
        small_total = small_total[: edge + biases.shape[0]]
    else:
        total_a, total_b = sum_a["result"], sum_b["result"]
        small_total = small_job["result"]
    if cut:
        up_total, down_total = mlp_job["result"]
    else:
        mlp_total = mlp_job["result"].reshape(share, chunks, 2, width)
        up_total, down_total = mlp_total[:, :, 0], mlp_total[:, :, 1]
    up_total = up_total.reshape(share, chunks, count, share).transpose(0, 2, 1, 3)
    down_total = down_total.reshape(share, chunks, width).transpose(1, 0, 2)
    return (
        block_out.reshape(tokens.shape),
        input_grad.reshape(tokens.shape),
        by_kind(total_a, total_b).reshape(-1),
        total_a[:, span:].reshape(-1),
        up_total.reshape(-1),
        down_total.reshape(-1),
        small_total[:edge],
        small_total[edge:],
    )


def solution(mesh):
    split = P(AXES)
    whole = P(AXES, None, None)
    return jax.shard_map(
        functools.partial(local, mesh),
        mesh=mesh,
        in_specs=(whole, whole) + (split,) * 8,
        out_specs=(whole, whole) + (split,) * 6,
        check_vma=False,
    )
```

```python
import functools
import math

import jax
import jax.numpy as jnp
from jax import lax
from jax.experimental import pallas as pl
from jax.experimental.pallas import tpu as pltpu
from jax.sharding import PartitionSpec as P

HEADS = 12
PATCH_SMALL = 196
PATCH_LARGE = 576
AXES = ("dp", "fsdp")
bf16 = jnp.bfloat16
f32 = jnp.float32
NN = (((1,), (0,)), ((), ()))
NT = (((1,), (1,)), ((), ()))
TN = (((0,), (0,)), ((), ()))
VMEM_LIMIT = 60 * 2**20
TILE = 304
ATILE = 304
AHEAD = 1
MTILE = 304
MAHEAD = 1
LTILE = 608
LSUB = 304
BOT = 304
BTILE = 304
BAHEAD = 1
LOG2E = 1.4426950408889634


def dot(a, b, dims):
    return lax.dot_general(a, b, dims, preferred_element_type=f32)


def params(n):
    return pltpu.CompilerParams(
        vmem_limit_bytes=VMEM_LIMIT, dimension_semantics=("arbitrary",) * n
    )


def cost(*_):
    return pl.CostEstimate(flops=1, bytes_accessed=1, transcendentals=0)


def tile_of(seq):
    return TILE if seq % TILE == 0 else seq


def once(shape):
    return pl.BlockSpec(
        shape, lambda *_: (0,) * len(shape), pipeline_mode=pl.Buffered(buffer_count=1)
    )


def shape_of(shape, dtype):
    return jax.ShapeDtypeStruct(shape, dtype)


class Flights:
    def __init__(self):
        self.waiting = []
        self.flying = []

    def add(self, steps, lengths):
        job = {"steps": steps, "lengths": list(lengths), "result": None}
        self.advance(job, None)
        return job

    def advance(self, job, came):
        try:
            sends = job["steps"].send(came) if came is not None else next(job["steps"])
        except StopIteration as stop:
            job["result"] = lax.optimization_barrier(stop.value)
            return
        length = job["lengths"].pop(0) if job["lengths"] else 1
        self.waiting.append((job, sends, length))

    def depart(self):
        for job, sends, length in self.waiting:
            came = [lax.ppermute(array, AXES, pairs) for array, pairs in sends]
            self.flying.append([job, came, length])
        self.waiting = []

    def run(self, kernel, operand, *others):
        arrays = [array for _, sends, _ in self.waiting for array, _ in sends]
        if arrays:
            operand, arrays = lax.optimization_barrier((operand, arrays))
            left = iter(arrays)
            self.waiting = [
                (job, [(next(left), pairs) for _, pairs in sends], length)
                for job, sends, length in self.waiting
            ]
        self.depart()
        out = kernel(operand, *others)
        for flight in self.flying:
            flight[2] -= 1
        landed = [flight for flight in self.flying if flight[2] <= 0]
        self.flying = [flight for flight in self.flying if flight[2] > 0]
        if landed:
            out, came = lax.optimization_barrier((out, [flight[1] for flight in landed]))
            for flight, got in zip(landed, came):
                self.advance(flight[0], got)
        return out

    def land(self, job):
        self.depart()
        for flight in [flight for flight in self.flying if flight[0] is job]:
            self.flying.remove(flight)
            self.advance(job, flight[1])

    def finish_after(self, values):
        cames, values = lax.optimization_barrier(([flight[1] for flight in self.flying], values))
        for flight, came in zip(self.flying, cames):
            flight[1] = came
        self.finish()
        return values

    def finish(self, turns=None):
        turn = 0
        while (self.waiting or self.flying) and turn != turns:
            turn += 1
            self.depart()
            for flight in self.flying:
                flight[2] -= 1
            landed = [flight for flight in self.flying if turns is None or flight[2] <= 0]
            self.flying = [flight for flight in self.flying if not (turns is None or flight[2] <= 0)]
            cames = [flight[1] for flight in landed]
            if turns is not None:
                cames = lax.optimization_barrier(cames)
            for flight, came in zip(landed, cames):
                self.advance(flight[0], came)


def bit_groups(mesh):
    inner = int(math.log2(mesh.shape["fsdp"]))
    outer = int(math.log2(mesh.shape["dp"]))
    rest = [list(range(b, min(b + 2, inner))) for b in range(1, inner, 2)]
    return [0], list(range(inner, inner + outer)), rest


def position(me, bits):
    spot = 0
    for place, bit in enumerate(bits):
        spot = spot + ((me >> bit) & 1) * (1 << place)
    return spot


def partners(count, bits):
    swaps = []
    for step in range(1, 1 << len(bits)):
        mask = 0
        for place, bit in enumerate(bits):
            if (step >> place) & 1:
                mask |= 1 << bit
        swaps.append((step, [(i, i ^ mask) for i in range(count)]))
    return swaps


def gather_steps(shard, mesh, groups):
    count = mesh.size
    me = lax.axis_index(AXES)
    bits = int(math.log2(count))
    rows, columns = shard.shape
    held = shard.reshape((1,) * bits + (rows, columns))
    for group in groups:
        swaps = partners(count, group)
        came = yield [(held, pairs) for _, pairs in swaps]
        shape = list(held.shape)
        for bit in group:
            shape[bits - 1 - bit] = 2
        whole = jnp.zeros(shape, shard.dtype)
        for (step, _), got in zip([(0, None)] + swaps, [held] + came):
            start = [0] * len(shape)
            for place, bit in enumerate(group):
                start[bits - 1 - bit] = ((me >> bit) & 1) ^ ((step >> place) & 1)
            whole = lax.dynamic_update_slice(whole, got, start)
        held = whole
    return held.reshape(count * rows, columns)


def pick(array, axis, index):
    return lax.dynamic_slice_in_dim(array, index, 1, axis)


def total(terms, axis, index, kind):
    return sum(pick(term, axis, index).astype(f32) for term in terms).astype(kind)


def sum_steps(parts, mesh, kind):
    count = mesh.size
    core, outer, rest = bit_groups(mesh)
    me = lax.axis_index(AXES)
    rows, columns = parts.shape[0] // count, parts.shape[1]
    rest_size = mesh.shape["fsdp"] // 2
    held = parts.reshape(mesh.shape["dp"], rest_size, 2, rows, columns)
    spot = position(me, core)
    (got,) = yield [(pick(held, 2, spot ^ 1).astype(kind), partners(count, core)[0][1])]
    terms = [pick(held, 2, spot), got]
    split = 2 if len(outer) == 2 and columns % 256 == 0 else 1
    width = columns // split
    shape = (2,) * len(outer) + (rest_size, 1, rows, width)
    pieces = []
    for piece in range(split):
        own = [term[..., piece * width : (piece + 1) * width].reshape(shape) for term in terms]
        order = list(range(len(outer)))
        pieces.append((own, order if piece == 0 else order[::-1]))
    for turn in range(len(outer)):
        sends = []
        for own, order in pieces:
            axis = order[turn]
            bit = outer[len(outer) - 1 - axis]
            mine = position(me, [bit])
            sends.append((total(own, axis, mine ^ 1, kind), partners(count, [bit])[0][1]))
        came = yield sends
        pieces = [
            ([pick(term, order[turn], position(me, [outer[len(outer) - 1 - order[turn]]])) for term in own] + [got], order)
            for (own, order), got in zip(pieces, came)
        ]
    left = rest_size
    pieces = [[term.reshape(rest_size, rows, width) for term in own] for own, _ in pieces]
    for bits in reversed(rest):
        size = 1 << len(bits)
        left //= size
        pieces = [[term.reshape(size, left, rows, width) for term in own] for own in pieces]
        spot = position(me, bits)
        swaps = partners(count, bits)
        sends = [
            (jnp.concatenate([total(own, 0, spot ^ step, kind) for own in pieces], -1), pairs)
            for step, pairs in swaps
        ]
        came = yield sends
        pieces = [
            [pick(term, 0, spot) for term in own]
            + [got[..., place * width : (place + 1) * width] for got in came]
            for place, own in enumerate(pieces)
        ]
    sums = [sum(term.astype(f32) for term in own).reshape(rows, width) for own in pieces]
    return jnp.concatenate(sums, -1)


def send_sum_kernel(where, *refs, sizes):
    at = 0
    for size, out in zip(sizes, refs[sum(sizes) :]):
        out[...] = sum(term[...].astype(f32) for term in refs[at : at + size]).astype(out.dtype)
        at += size


def fold_first(where, keep, came):
    _, _, left, rows, columns = keep.shape
    cut = columns // 2
    spec_a = pl.BlockSpec((None, 2, 2, rows, cut), lambda j, where: ((where[1] // 2) ^ 1, 0, j, 0, 0))
    spec_b = pl.BlockSpec((2, None, 2, rows, cut), lambda j, where: (0, (where[1] % 2) ^ 1, j, 0, 1))
    return pl.pallas_call(
        functools.partial(send_sum_kernel, sizes=[2, 2]),
        grid_spec=pltpu.PrefetchScalarGridSpec(
            num_scalar_prefetch=1,
            grid=(left // 2,),
            in_specs=[spec_a, spec_a, spec_b, spec_b],
            out_specs=[pl.BlockSpec((2, 2, rows, cut), lambda j, where: (0, j, 0, 0))] * 2,
        ),
        out_shape=[shape_of((2, left, rows, cut), bf16)] * 2,
        compiler_params=params(1),
        cost_estimate=cost(),
        name="fold_first",
    )(where, keep, came, keep, came)


def fold_second(where, keep, came, came_a, came_b):
    _, _, left, rows, columns = keep.shape
    cut = columns // 2
    spec_a = pl.BlockSpec(
        (None, None, 2, rows, cut), lambda j, where: (where[1] // 2, (where[1] % 2) ^ 1, j, 0, 0)
    )
    spec_b = pl.BlockSpec(
        (None, None, 2, rows, cut), lambda j, where: ((where[1] // 2) ^ 1, where[1] % 2, j, 0, 1)
    )
    half_a = pl.BlockSpec((None, 2, rows, cut), lambda j, where: ((where[1] % 2) ^ 1, j, 0, 0))
    half_b = pl.BlockSpec((None, 2, rows, cut), lambda j, where: ((where[1] // 2) ^ 1, j, 0, 0))
    return pl.pallas_call(
        functools.partial(send_sum_kernel, sizes=[3, 3]),
        grid_spec=pltpu.PrefetchScalarGridSpec(
            num_scalar_prefetch=1,
            grid=(left // 2,),
            in_specs=[spec_a, spec_a, half_a, spec_b, spec_b, half_b],
            out_specs=[pl.BlockSpec((2, rows, cut), lambda j, where: (j, 0, 0))] * 2,
        ),
        out_shape=[shape_of((left, rows, cut), bf16)] * 2,
        compiler_params=params(1),
        cost_estimate=cost(),
        name="fold_second",
    )(where, keep, came, came_a, keep, came, came_b)


def line_first_kernel(where, *refs):
    *terms, keep, send = refs
    fast = where[2] % 2
    cut = terms[0].shape[-1]
    for slow in range(2):
        for place, out in ((slow * 2 + fast, keep), (slow * 2 + (fast ^ 1), send)):
            for half in range(2):
                own = terms[4 * half : 4 * half + 4]
                lanes = slice(half * cut, (half + 1) * cut)
                out[slow, :, lanes] = sum(term[place].astype(f32) for term in own).astype(out.dtype)


def line_first(where, keep, came, came_a, came_b, last_a, last_b):
    _, _, size, rows, columns = keep.shape
    cut = columns // 2
    whole = lambda half: pl.BlockSpec(
        (None, None, size, rows, cut), lambda j, where: (where[1] // 2, where[1] % 2, 0, 0, half)
    )
    half_a = pl.BlockSpec((None, size, rows, cut), lambda j, where: (where[1] % 2, 0, 0, 0))
    half_b = pl.BlockSpec((None, size, rows, cut), lambda j, where: (where[1] // 2, 0, 0, 0))
    last = pl.BlockSpec((size, rows, cut), lambda j, where: (0, 0, 0))
    return pl.pallas_call(
        line_first_kernel,
        grid_spec=pltpu.PrefetchScalarGridSpec(
            num_scalar_prefetch=1,
            grid=(1,),
            in_specs=[whole(0), whole(0), half_a, last, whole(1), whole(1), half_b, last],
            out_specs=[once((size // 2, rows, columns))] * 2,
        ),
        out_shape=[shape_of((size // 2, rows, columns), bf16)] * 2,
        compiler_params=params(1),
        cost_estimate=cost(),
        name="line_first",
    )(where, keep, came, came_a, last_a, keep, came, came_b, last_b)


def swap_steps(send, mesh):
    core, _, _ = bit_groups(mesh)
    (came,) = yield [(send, partners(mesh.size, core)[0][1])]
    return came


def part_of(terms, axis, index, kind):
    total = None
    for term in terms:
        if term.shape[axis] != 1:
            term = pick(term, axis, index)
        total = term.astype(f32) if total is None else total + term.astype(f32)
    return total.astype(kind)


def plane_steps(keep, came, mesh):
    count = mesh.size
    _, outer, rest = bit_groups(mesh)
    spot = position(lax.axis_index(AXES), outer)
    size = 1 << len(outer)
    terms = [array.reshape((size, 1 << len(rest[0])) + keep.shape[1:]) for array in (keep, came)]
    sends = [part_of(terms, 0, spot ^ step, bf16)[0] for step in range(1, size)]
    came = yield [(array, pairs) for array, (_, pairs) in zip(sends, partners(count, outer))]
    return [pick(term, 0, spot)[0] for term in terms] + came


def line_steps(groups, mesh):
    count = mesh.size
    _, _, rest = bit_groups(mesh)
    spot = position(lax.axis_index(AXES), rest[0])
    side = lambda index, kind: jnp.concatenate([part_of(terms, 0, index, kind)[0] for terms in groups], -1)
    came = yield [(side(spot ^ step, bf16), pairs) for step, pairs in partners(count, rest[0])]
    return side(spot, f32) + sum(array.astype(f32) for array in came)


def fold_sum_steps(keep, send, where, mesh):
    count = mesh.size
    core, outer, rest = bit_groups(mesh)
    (came,) = yield [(send, partners(count, core)[0][1])]
    shape = (2, 2, 1 << len(rest[0]), keep.shape[0] * 2 // count, keep.shape[1])
    keep, came = keep.reshape(shape), came.reshape(shape)
    fast, slow = (partners(count, [bit])[0][1] for bit in outer)
    send_a, send_b = fold_first(where, keep, came)
    came_a, came_b = yield [(send_a, slow), (send_b, fast)]
    send_a, send_b = fold_second(where, keep, came, came_a, came_b)
    last_a, last_b = yield [(send_a, fast), (send_b, slow)]
    keep, send = line_first(where, keep, came, came_a, came_b, last_a, last_b)
    (came,) = yield [(send, partners(count, [rest[0][0]])[0][1])]
    me = lax.axis_index(AXES)
    spot = position(me, [rest[0][1]])
    both = [keep, came]
    (last,) = yield [(total(both, 0, spot ^ 1, bf16), partners(count, [rest[0][1]])[0][1])]
    done = (total(both, 0, spot, f32) + last.astype(f32)).reshape(2, shape[3] // 2, shape[4])
    spot = position(me, core)
    (came,) = yield [(pick(done, 0, spot ^ 1), partners(count, core)[0][1])]
    own, came = pick(done, 0, spot)[0], came[0]
    return jnp.where(spot == 0, own, came), jnp.where(spot == 0, came, own)


def small_sum_steps(parts, mesh):
    count = mesh.size
    core, outer, rest = bit_groups(mesh)
    groups = [core, outer, *reversed(rest)]
    order = [outer, *reversed(rest), core]
    me = lax.axis_index(AXES)
    columns = parts.shape[1]
    held = parts.reshape([1 << len(bits) for bits in order] + [columns])
    for bits in groups:
        axis = order.index(bits)
        spot = position(me, bits)
        swaps = partners(count, bits)
        came = yield [(pick(held, axis, spot ^ step), pairs) for step, pairs in swaps]
        held = pick(held, axis, spot) + sum(came)
    return held.reshape(columns)


def cut_by_core(mesh):
    _, outer, rest = bit_groups(mesh)
    return len(outer) == 2 and len(rest) == 1 and len(rest[0]) == 2


def store_cut(core, outs, lanes, value, rows):
    if len(outs) == 1:
        outs[0][:, lanes] = value.astype(bf16)
        return
    keep, send = outs
    for parity in range(2):
        @pl.when(core == parity)
        def _():
            for device in range(value.shape[0] // rows):
                out = keep if device % 2 == parity else send
                out[device // 2, :, lanes] = value[device * rows : (device + 1) * rows, :].astype(bf16)


def cut_shapes(width, columns, chunk, index, rows):
    if not rows:
        spec = pl.BlockSpec((width, chunk), lambda j, *_: (0, index(j)))
        return [spec], [shape_of((width, columns), bf16)]
    blocks = width // rows // 2
    spec = pl.BlockSpec((blocks, rows, chunk), lambda j, *_: (0, 0, index(j)))
    return [spec] * 2, [shape_of((blocks, rows, columns), bf16)] * 2


def normalize(values):
    center = values - jnp.mean(values, -1, keepdims=True)
    scale = lax.rsqrt(jnp.mean(center * center, -1, keepdims=True) + 1e-05)
    return center * scale, scale


def norm_back(grad, gain, unit, scale):
    inner = grad * gain
    return scale * (
        inner
        - jnp.mean(inner, -1, keepdims=True)
        - unit * jnp.mean(inner * unit, -1, keepdims=True)
    )


def gelu_parts(u):
    phi = 0.5 + 0.5 * lax.erf(u * 0.7071067811865476)
    slope = phi + u * (0.3989422804014327 * jnp.exp2((u * u) * (-0.5 * LOG2E)))
    return u * phi, slope


def column_sum(values):
    return jnp.sum(values, 0, keepdims=True)


def accumulate(ref, value, first):
    @pl.when(first)
    def _():
        ref[...] = value

    @pl.when(jnp.logical_not(first))
    def _():
        ref[...] += value


def two_heads(block, padded):
    seq = block.shape[0]
    first = lax.broadcasted_iota(jnp.int32, block.shape, 1) < 64
    zero = jnp.zeros_like(block)
    pad = jnp.zeros((padded - seq, 128), block.dtype)
    return jnp.concatenate(
        [jnp.where(first, block, zero), pad, jnp.where(first, zero, block), pad], 0
    )


def attend_kernel(valid, *refs, tile, padded, first, pairs):
    if first:
        tokens, gain, shift, weight, bias, normed, joined, mixed, raised_out, inverse = refs
    else:
        (
            normed, weight, bias, tokens, mixed_first, bias_out, gain, shift,
            joined, mixed, raised_out, inverse, middle, normed_two,
        ) = refs
    seq, span = joined.shape
    for start in range(0, seq, tile):
        rows = slice(start, start + tile)
        if first:
            unit, _ = normalize(tokens[rows, :].astype(f32))
            low = (unit * gain[...] + shift[...]).astype(bf16)
            normed[rows, :] = low
        else:
            low = normed[rows, :]
        joined[rows, :] = (dot(low, weight[:, :span], NN) + bias[...]).astype(bf16)

    column = lax.broadcasted_iota(jnp.int32, (1, padded), 1)
    mask = jnp.where(column < valid[pl.program_id(0)], 0.0, -1e30).astype(f32)
    places = [(pair, start) for pair in range(pairs) for start in range(0, seq, ATILE)]
    keys, values = {}, {}
    row = lax.broadcasted_iota(jnp.int32, (2 * padded, 128), 0)
    lane = lax.broadcasted_iota(jnp.int32, (2 * padded, 128), 1)
    ones = jnp.where((row < padded) == (lane < 64), 1.0, 0.0).astype(bf16)

    def scores_at(pair, start):
        if pair not in keys:
            at = pair * 384
            keys[pair] = two_heads(joined[:, at + 128 : at + 256], padded)
            values[pair] = jnp.concatenate([two_heads(joined[:, at + 256 : at + 384], padded), ones], 1)
        return dot(joined[start : start + ATILE, pair * 384 : pair * 384 + 128], keys[pair], NT)

    ahead = [scores_at(*place) for place in places[:AHEAD]]
    for index, (pair, start) in enumerate(places):
        rows = slice(start, start + ATILE)
        if index + AHEAD < len(places):
            ahead.append(scores_at(*places[index + AHEAD]))
        scores = ahead.pop(0)
        halves = []
        for head in range(2):
            part = scores[:, head * padded : (head + 1) * padded] * (0.125 * LOG2E) + mask
            halves.append(jnp.exp2(part - jnp.max(part, 1, keepdims=True)).astype(bf16))
        raised = jnp.concatenate(halves, 1)
        raised_out[pair, rows, :] = raised
        both = dot(raised, values[pair], NN)
        scale = 1.0 / both[:, 128:]
        inverse[rows, pair * 128 : (pair + 1) * 128] = scale
        mixed[rows, pair * 128 : (pair + 1) * 128] = (both[:, :128] * scale).astype(bf16)
    if first:
        return
    width = tokens.shape[1]
    for start in range(0, seq, tile):
        rows = slice(start, start + tile)
        value = tokens[rows, :].astype(f32) + bias_out[...]
        value = value + dot(mixed_first[rows, :], weight[: width // 2, -width:], NN)
        value = value + dot(mixed[rows, :], weight[width // 2 :, -width:], NN)
        middle[rows, :] = value
        unit, _ = normalize(value)
        normed_two[rows, :] = (unit * gain[...] + shift[...]).astype(bf16)


def attend(start, valid, weight, bias, seq, norm=None, after=None):
    rows, width = start.shape
    span = bias.shape[1]
    pairs = span // 384
    items = rows // seq
    padded = -(-seq // 128) * 128
    row = lambda w: pl.BlockSpec((seq, w), lambda i, *_: (i, 0))
    one = once((1, width))
    main = [once(weight.shape), once((1, span))]
    if norm:
        specs, arrays = [row(width), one, one, *main], [start, *norm, weight, bias]
    else:
        specs = [row(width), *main, row(width), row(width // 2), one, one, one]
        arrays = [start, weight, bias, *after]
    outs = [
        row(span),
        row(span // 3),
        pl.BlockSpec((None, pairs, seq, 2 * padded), lambda i, *_: (i, 0, 0, 0)),
        row(span // 3),
    ]
    shapes = [
        shape_of((rows, span), bf16),
        shape_of((rows, span // 3), bf16),
        shape_of((items, pairs, seq, 2 * padded), bf16),
        shape_of((rows, span // 3), f32),
    ]
    if norm:
        outs, shapes = [row(width)] + outs, [shape_of((rows, width), bf16)] + shapes
    else:
        outs += [row(width)] * 2
        shapes += [shape_of((rows, width), f32), shape_of((rows, width), bf16)]
    return pl.pallas_call(
        functools.partial(attend_kernel, tile=tile_of(seq), padded=padded, first=bool(norm), pairs=pairs),
        grid_spec=pltpu.PrefetchScalarGridSpec(
            num_scalar_prefetch=1, grid=(items,), in_specs=specs, out_specs=outs
        ),
        out_shape=shapes,
        compiler_params=params(1),
        cost_estimate=cost(),
        name="attend",
    )(valid, *arrays)


def attend_back_kernel(where, *refs, pairs, extra, spare, cut):
    lists = [refs[kind * pairs : (kind + 1) * pairs] for kind in range(5)]
    joined, mixed_grad, mixed, raised, inverse = lists
    normed, weight, *rest = refs[5 * pairs :]
    if extra:
        mixed_a, mixed_b, low_grad, *rest, total_out = rest
    joined_grad, column, gain_sum, shift_sum, *outs, held, scaled, total = rest
    item = pl.program_id(0)
    seq, span = joined_grad.shape
    padded = raised[0].shape[1] // 2
    tile = BTILE if seq % BTILE == 0 else seq
    first = lax.broadcasted_iota(jnp.int32, (tile, 128), 1) < 64
    places = [(pair, start) for pair in range(pairs) for start in range(0, seq, tile)]
    keys, values = {}, {}

    def prob_grad_at(pair, start):
        if pair not in keys:
            keys[pair] = two_heads(joined[pair][:, 128:256], padded)
            values[pair] = two_heads(joined[pair][:, 256:], padded)
        rows = slice(start, start + tile)
        grad = (mixed_grad[pair][rows, :].astype(f32) * inverse[pair][rows, :]).astype(bf16)
        scaled[pair, rows, :] = grad
        return grad, dot(grad, values[pair], NT)

    def own_half(both):
        return jnp.concatenate([both[:64, :padded], both[64:, padded:]], 0).T[:seq]

    ahead = [prob_grad_at(*place) for place in places[:BAHEAD]]
    for index, (pair, start) in enumerate(places):
        rows = slice(start, start + tile)
        at = pair * 384
        if index + BAHEAD < len(places):
            ahead.append(prob_grad_at(*places[index + BAHEAD]))
        grad, prob_grad = ahead.pop(0)
        product = grad.astype(f32) * mixed[pair][rows, :].astype(f32)
        zero = jnp.zeros_like(product)
        halves = []
        for head in range(2):
            own = jnp.where(first, product, zero) if head == 0 else jnp.where(first, zero, product)
            centre = jnp.sum(own, 1, keepdims=True)
            half = slice(head * padded, (head + 1) * padded)
            halves.append((raised[pair][rows, half].astype(f32) * (prob_grad[:, half] - centre)).astype(bf16))
        score_grad = jnp.concatenate(halves, 1)
        held[rows, :] = score_grad
        joined_grad[rows, at : at + 128] = (dot(score_grad, keys[pair], NN) * 0.125).astype(bf16)
        if start + tile == seq:
            joined_grad[:, at + 128 : at + 256] = (
                own_half(dot(joined[pair][:, :128].T, held[...], NN)) * 0.125
            ).astype(bf16)
            joined_grad[:, at + 256 : at + 384] = own_half(
                dot(scaled[pair].T, raised[pair][...], NN)
            ).astype(bf16)

    value = joined_grad[...]
    accumulate(total, dot(normed[...], value, TN), item == 0)
    accumulate(column, column_sum(value.astype(f32)), item == 0)
    if extra:
        both = [dot(mixed_a[...], low_grad[...], TN), dot(mixed_b[...], low_grad[...], TN)]
        accumulate(total_out, jnp.concatenate(both, 0), item == 0)

    @pl.when(item == pl.num_programs(0) - 1)
    def _():
        store_cut(where[0], outs, slice(0, span), total[...], cut)
        if spare:
            for out in outs:
                out[..., span:] = jnp.zeros(out.shape[:-1] + (spare,), bf16)
        wide = weight[...].astype(f32)
        for ref, product in ((gain_sum, wide * total[...]), (shift_sum, wide * column[...])):
            row = jnp.sum(product, 1, keepdims=True)
            ref[...] = jnp.broadcast_to(row, (row.shape[0], 128)).T[:1]
        if extra:
            store_cut(where[0], outs, slice(span, span + total_out.shape[1]), total_out[...], cut)


def attend_back(mixed_grad, where, joined, mixed, raised, inverse, normed, weight, seq, part, cut, others=(), spare=0):
    rows, width = normed.shape
    items, in_part, _, keys = raised.shape
    pairs = in_part
    chosen = range(pairs)
    span = 384 * pairs
    row = lambda w, off=0: pl.BlockSpec((seq, w), lambda i, *_: (i, off))
    each = lambda w, off=0: [row(w, off + pair) for pair in chosen]
    weights = [
        pl.BlockSpec((None, None, seq, keys), functools.partial(lambda at, i, *_: (i, at, 0, 0), pair))
        for pair in chosen
    ]
    columns = span + (width if others else 0) + spare
    one = pl.BlockSpec((1, width), lambda i, *_: (0, 0))
    specs, shapes = cut_shapes(width, columns, columns, lambda j: 0, cut)
    return pl.pallas_call(
        functools.partial(
            attend_back_kernel, pairs=pairs, extra=bool(others), spare=spare, cut=cut
        ),
        grid_spec=pltpu.PrefetchScalarGridSpec(
            num_scalar_prefetch=1,
            grid=(items,),
            in_specs=[
                *each(384), *each(128, part * in_part), *each(128), *weights, *each(128), row(width)
            ]
            + [once((width, span))]
            + [row(array.shape[1]) for array in others],
            out_specs=[row(span), pl.BlockSpec((1, span), lambda i, *_: (0, 0)), one, one] + specs,
            scratch_shapes=[
                pltpu.VMEM((seq, keys), bf16),
                pltpu.VMEM((pairs, seq, 128), bf16),
                pltpu.VMEM((width, span), f32),
            ]
            + ([pltpu.VMEM((width, width), f32)] if others else []),
        ),
        out_shape=[shape_of((rows, span), bf16), shape_of((1, span), f32)]
        + [shape_of((1, width), f32)] * 2
        + shapes,
        compiler_params=params(1),
        cost_estimate=cost(),
        name="attend_back",
    )(
        where, *[joined] * pairs, *[mixed_grad] * pairs, *[mixed] * pairs, *[raised] * pairs,
        *[inverse] * pairs, normed, weight, *others,
    )


def mlp_kernel(
    valid, where, normed, cotangent, up, down, bias_up,
    active, hidden_grad, up_sum, *rest, seq, tile, cut,
):
    *outs, grad = rest
    rows, width = normed.shape

    @pl.when(pl.program_id(0) == 0)
    def _():
        place = lax.broadcasted_iota(jnp.int32, (seq, 1), 0)
        for item in range(rows // seq):
            span = slice(item * seq, (item + 1) * seq)
            grad[span, :] = jnp.where(place < valid[item], cotangent[span, :].astype(f32), 0.0).astype(bf16)

    def ahead_of(start):
        span = slice(start, start + MTILE)
        return dot(normed[span, :], up[...], NN), dot(grad[span, :], down[...], NT)

    column = jnp.zeros(up_sum.shape, f32)
    starts = list(range(0, rows, MTILE))
    ahead = [ahead_of(start) for start in starts[:MAHEAD]]
    for index, start in enumerate(starts):
        span = slice(start, start + MTILE)
        if index + MAHEAD < len(starts):
            ahead.append(ahead_of(starts[index + MAHEAD]))
        hidden, wide = ahead.pop(0)
        value, slope = gelu_parts(hidden + bias_up[...])
        low = (slope * wide).astype(bf16)
        active[span, :] = value.astype(bf16)
        hidden_grad[span, :] = low
        column = column + column_sum(low.astype(f32))
    up_sum[...] = column
    first = dot(normed[...], hidden_grad[...], TN).astype(bf16)
    second = dot(active[...], grad[...], TN).astype(bf16)
    if cut:
        keep, send = outs
        for core in range(2):
            @pl.when(where[0] == core)
            def _():
                (keep, send)[core][...] = first
                (send, keep)[core][...] = second
    else:
        outs[0][:, :width] = first
        outs[0][:, width:] = second


def mlp(normed, valid, where, cotangent, both, bias_up, seq, cut):
    rows, width = normed.shape
    wide = both.shape[1] // 2
    chunks = wide // width
    whole = once((rows, width))
    square = lambda off: pl.BlockSpec((width, width), lambda j, *_: (0, j + off))
    row = pl.BlockSpec((rows, width), lambda j, *_: (0, j))
    one = pl.BlockSpec((1, width), lambda j, *_: (0, j))
    if cut:
        specs = [pl.BlockSpec((width, width), lambda j, *_: (0, j))] * 2
        shapes = [shape_of((width, wide), bf16)] * 2
    else:
        specs, shapes = cut_shapes(width, 2 * wide, 2 * width, lambda j: j, 0)
    return pl.pallas_call(
        functools.partial(mlp_kernel, seq=seq, tile=tile_of(seq), cut=cut),
        grid_spec=pltpu.PrefetchScalarGridSpec(
            num_scalar_prefetch=2,
            grid=(chunks,),
            in_specs=[whole, whole, square(0), square(chunks), one],
            out_specs=[row, row, one] + specs,
            scratch_shapes=[pltpu.VMEM((rows, width), bf16)],
        ),
        out_shape=[
            shape_of((rows, width * chunks), bf16),
            shape_of((rows, width * chunks), bf16),
            shape_of((1, width * chunks), f32),
        ]
        + shapes,
        compiler_params=params(1),
        cost_estimate=cost(),
        name="mlp",
    )(valid, where, normed, cotangent, both, both, bias_up)


def block_out_kernel(valid, active, downs, middle, bias_down, *rest, seq, begin):
    block_out = rest[-1]
    tile, width = middle.shape
    step = pl.program_id(0) + begin // tile
    place = lax.broadcasted_iota(jnp.int32, (tile, 1), 0) + lax.rem(step, seq // tile) * tile
    value = middle[...] + bias_down[...]
    for at in range(0, downs.shape[1], width):
        value = value + dot(active[:, at : at + width], downs[:, at : at + width], NN)
    block_out[...] = jnp.where(place < valid[step // (seq // tile)], value, 0.0).astype(bf16)


def half_of(both, second):
    width, columns = both.shape
    return pl.BlockSpec(
        (width, columns // 2), lambda j, *_: (0, second), pipeline_mode=pl.Buffered(buffer_count=1)
    )


def block_out_of(middle, valid, active, both, bias_down, seq, begin, end, before=None):
    rows, width = middle.shape
    tile = BOT if seq % BOT == 0 else seq
    skip = begin // tile
    row = lambda w: pl.BlockSpec((tile, w), lambda j, *_: (j + skip, 0))
    specs = [row(active.shape[1]), half_of(both, 1), row(width), once((1, width))]
    arrays = [active, both, middle, bias_down]
    aliases = {}
    if before is not None:
        aliases = {len(arrays) + 1: 0}
        specs.append(pl.BlockSpec(memory_space=pl.ANY))
        arrays.append(before)
    return pl.pallas_call(
        functools.partial(block_out_kernel, seq=seq, begin=begin),
        grid_spec=pltpu.PrefetchScalarGridSpec(
            num_scalar_prefetch=1,
            grid=((end - begin) // tile,),
            in_specs=specs,
            out_specs=row(width),
        ),
        out_shape=shape_of((rows, width), bf16),
        input_output_aliases=aliases,
        compiler_params=params(1),
        cost_estimate=cost(),
        name="block_out",
    )(valid, *arrays)


def middle_back_kernel(
    valid, hidden_grad, ups, middle, cotangent, gain, weight_a, weight_b,
    low_grad, mixed_grad, gain_sum, shift_sum, bias_sum, down_sum, *, seq, sub,
):
    step = pl.program_id(0)
    tile, width = middle.shape
    each = seq // tile
    starts = list(range(0, tile, sub))
    ahead = [dot(hidden_grad[:sub, :], ups[...], NT)]
    sums = [jnp.zeros((1, width), f32)] * 4
    for index, start in enumerate(starts):
        rows = slice(start, start + sub)
        if index + 1 < len(starts):
            ahead.append(dot(hidden_grad[start + sub : start + 2 * sub, :], ups[...], NT))
        grad = ahead.pop(0)
        unit, scale = normalize(middle[rows, :])
        place = lax.broadcasted_iota(jnp.int32, (sub, 1), 0) + (lax.rem(step, each) * tile + start)
        kept = jnp.where(place < valid[step // each], cotangent[rows, :].astype(f32), 0.0)
        low = (kept + norm_back(grad, gain[...], unit, scale)).astype(bf16)
        low_grad[rows, :] = low
        mixed_grad[rows, :] = (
            dot(low[:, : width // 2], weight_a[...], NT) + dot(low[:, width // 2 :], weight_b[...], NT)
        ).astype(bf16)
        terms = (grad * unit, grad, low.astype(f32), kept)
        sums = [before + column_sum(term) for before, term in zip(sums, terms)]
    for ref, value in zip((gain_sum, shift_sum, bias_sum, down_sum), sums):
        accumulate(ref, value, step == 0)


def middle_back(middle, valid, hidden_grad, both, cotangent, gain, weight, seq):
    rows, width = middle.shape
    tile = LTILE if seq % LTILE == 0 else seq
    sub = LSUB if tile % LSUB == 0 else tile
    row = lambda w: pl.BlockSpec((tile, w), lambda j, *_: (j, 0))
    one = pl.BlockSpec((1, width), lambda j, *_: (0, 0))
    half = width // 2
    at = weight.shape[1] // half - 2
    halves = [
        pl.BlockSpec((width, half), lambda j, *_: (0, at), pipeline_mode=pl.Buffered(buffer_count=1)),
        pl.BlockSpec((width, half), lambda j, *_: (0, at + 1), pipeline_mode=pl.Buffered(buffer_count=1)),
    ]
    return pl.pallas_call(
        functools.partial(middle_back_kernel, seq=seq, sub=sub),
        grid_spec=pltpu.PrefetchScalarGridSpec(
            num_scalar_prefetch=1,
            grid=(rows // tile,),
            in_specs=[
                row(hidden_grad.shape[1]), half_of(both, 0), row(width), row(width),
                once((1, width)), *halves,
            ],
            out_specs=[row(width), row(width)] + [one] * 4,
        ),
        out_shape=[shape_of((rows, width), bf16)] * 2 + [shape_of((1, width), f32)] * 4,
        compiler_params=params(1),
        cost_estimate=cost(),
        name="middle_back",
    )(valid, hidden_grad, both, middle, cotangent, gain, weight, weight)


def input_back_kernel(*refs, spans, sub):
    grads = refs[: len(spans)]
    weights = refs[len(spans) : len(spans) + 2]
    tokens, low_grad, gain, input_grad = refs[len(spans) + 2 :]
    tile, width = tokens.shape

    def ahead_of(start):
        rows = slice(start, start + sub)
        terms = [
            dot(grad[rows, :], weights[which][:, lanes], NT) for grad, (which, lanes) in zip(grads, spans)
        ]
        return sum(terms[1:], terms[0])

    starts = list(range(0, tile, sub))
    ahead = [ahead_of(0)]
    for index, start in enumerate(starts):
        rows = slice(start, start + sub)
        if index + 1 < len(starts):
            ahead.append(ahead_of(start + sub))
        grad = ahead.pop(0)
        unit, scale = normalize(tokens[rows, :].astype(f32))
        full = low_grad[rows, :].astype(f32) + norm_back(grad, gain[...], unit, scale)
        input_grad[rows, :] = full.astype(bf16)


def input_back(last, others, spans, weights, tokens, low_grad, gain, seq):
    rows, width = tokens.shape
    tile = LTILE if seq % LTILE == 0 else seq
    sub = LSUB if tile % LSUB == 0 else tile
    row = lambda w: pl.BlockSpec((tile, w), lambda i: (i, 0))
    grads = [*others, last]
    return pl.pallas_call(
        functools.partial(input_back_kernel, spans=spans, sub=sub),
        grid=(rows // tile,),
        in_specs=[row(grad.shape[1]) for grad in grads]
        + [once((width, spans[0][1].stop))] * 2
        + [row(width), row(width), once((1, width))],
        out_specs=row(width),
        out_shape=shape_of((rows, width), bf16),
        compiler_params=params(1),
        cost_estimate=cost(),
        name="input_back",
    )(*grads, *weights, tokens, low_grad, gain)


def local(mesh, tokens, cotangent, group, text_len, qkv_w, out_w, mlp_in, mlp_out, gains, biases):
    items, seq, width = tokens.shape
    rows = items * seq
    count = mesh.size
    share = width // count
    wide = mlp_in.shape[0] // share
    chunks = wide // width
    half = width // 2
    span = 3 * half
    valid = (PATCH_SMALL + (PATCH_LARGE - PATCH_SMALL) * group + text_len).astype(jnp.int32)
    flat = tokens.reshape(rows, width)
    cot = cotangent.reshape(rows, width)
    flights = Flights()
    me = lax.axis_index(AXES)
    core, outer, others = bit_groups(mesh)
    where = jnp.stack([position(me, core), position(me, outer), position(me, others[0])]).astype(jnp.int32)
    cut = share if cut_by_core(mesh) and share % 8 == 0 else 0

    def mlp_sums(arrays):
        if cut:
            return flights.add(fold_sum_steps(*arrays, where, mesh), [])
        return flights.add(sum_steps(arrays[0], mesh, bf16), [])

    def swap(arrays):
        return flights.add(swap_steps(arrays[1], mesh), []) if cut else None

    def by_pairs(matrix, part):
        rows = matrix.shape[0]
        cubes = matrix.reshape(rows, 3, 2, half // 128, 128)[:, :, part]
        return cubes.transpose(0, 2, 1, 3).reshape(rows, span)

    def by_kind(part_a, part_b):
        rows = part_a.shape[0]
        cubes = [piece[:, :span].reshape(rows, half // 128, 3, 128) for piece in (part_a, part_b)]
        return jnp.stack(cubes, 1).transpose(0, 3, 1, 2, 4).reshape(rows, 3 * width)

    own_up = mlp_in.reshape(share, count, chunks, share).transpose(0, 2, 1, 3).reshape(share, wide)
    own_down = mlp_out.reshape(chunks, share, width).transpose(1, 0, 2).reshape(share, wide)
    own_both = jnp.concatenate([own_up, own_down], 1)

    own_qkv = qkv_w.reshape(share, 3 * width)
    small = jnp.concatenate([gains, biases])
    small_rows = -(-small.shape[0] // 128)
    padded = jnp.pad(small, (0, small_rows * 128 - small.shape[0])).reshape(small_rows, 128)
    padded = jnp.pad(padded, ((0, share - small_rows), (0, 0)))
    both = lax.all_gather(own_both, AXES, axis=0, tiled=True)
    own_first = jnp.concatenate([by_pairs(own_qkv, 0), padded], 1)
    own_second = jnp.concatenate([by_pairs(own_qkv, 1), out_w.reshape(share, width)], 1)
    singles = [[bit] for group in reversed(others) for bit in reversed(group)]
    job = flights.add(gather_steps(own_first, mesh, [*others, outer, core]), [])
    second_job = flights.add(gather_steps(own_second, mesh, [*singles, outer, core]), [1] * len(singles) + [2])
    flights.finish(len(others) + 2)
    first = job["result"]
    small = first[:, span:].reshape(count, share, 128)[:, :small_rows]
    small = small.reshape(count, small_rows * 128).astype(f32)
    edge = gains.shape[0]
    gain = small[:, :edge].reshape(1, 2 * width)
    bias = small[:, edge : edge + biases.shape[0]].reshape(1, 6 * width + wide)
    gain_one, gain_two = gain[:, :width], gain[:, width:]
    bias_query, bias_value, bias_output, shift_one, shift_two, bias_down = (
        bias[:, p * width : (p + 1) * width] for p in range(6)
    )
    bias_up = bias[:, 6 * width :].reshape(count, chunks, share).transpose(1, 0, 2).reshape(1, wide)
    bias_joined = jnp.concatenate([bias_query, jnp.zeros_like(bias_query), bias_value], 1)
    bias_parts = [by_pairs(bias_joined, part) for part in range(2)]

    normed, joined_a, mixed_a, raised_a, inverse_a = flights.run(
        lambda x: attend(x, valid, first, bias_parts[0], seq, (gain_one, shift_one)), flat
    )
    flights.finish()
    second = second_job["result"]
    joined_b, mixed_b, raised_b, inverse_b, middle, normed_two = attend(
        normed, valid, second, bias_parts[1], seq,
        after=(flat, mixed_a, bias_output, gain_two, shift_two),
    )

    active, hidden_grad, up_sum, *mlp_grads = mlp(
        normed_two, valid, where, cot, both, bias_up, seq, cut
    )
    mlp_job = mlp_sums(mlp_grads)

    low_grad, mixed_grad, gain_two_sum, shift_two_sum, bias_out_sum, down_sum = flights.run(
        lambda x: middle_back(x, valid, hidden_grad, both, cot, gain_two, second, seq), middle
    )
    joined_grad_a, qkv_sum_a, gain_sum_a, shift_sum_a, *grads_a = flights.run(
        lambda x: attend_back(
            x, where, joined_a, mixed_a, raised_a, inverse_a, normed, first, seq, 0, cut,
            others=(mixed_a, mixed_b, low_grad),
        ),
        mixed_grad,
    )
    swap_a = swap(grads_a)
    joined_grad_b, qkv_sum_b, gain_sum_b, shift_sum_b, *grads_b = flights.run(
        lambda x: attend_back(
            x, where, joined_b, mixed_b, raised_b, inverse_b, normed, second, seq, 1, cut,
            spare=128 if cut else 0,
        ),
        mixed_grad,
    )
    shift_one_sum = shift_sum_a + shift_sum_b
    gain_one_sum = (gain_sum_a + gain_sum_b - shift_one * shift_one_sum) / gain_one
    joined_sums = by_kind(qkv_sum_a, qkv_sum_b)
    up_sum = up_sum.reshape(chunks, count, share).transpose(1, 0, 2).reshape(1, wide)
    gain_sums = jnp.concatenate([gain_one_sum, gain_two_sum], 1).reshape(count, edge)
    bias_sums = jnp.concatenate(
        [
            joined_sums[:, :width],
            joined_sums[:, 2 * width :],
            bias_out_sum,
            shift_one_sum,
            shift_two_sum,
            down_sum,
            up_sum,
        ],
        1,
    ).reshape(count, biases.shape[0])
    small = jnp.concatenate([gain_sums, bias_sums], 1)
    if cut:
        small = jnp.pad(small, ((0, 0), (0, small_rows * 128 - small.shape[1])))
        small = small.reshape(count // 2, 2, small_rows, 128)
        spot = position(me, core)
        grads_b = [
            lax.dynamic_update_slice(grads, pick(small, 1, place)[:, 0].astype(bf16), (0, 0, span))
            for grads, place in zip(grads_b, (spot, spot ^ 1))
        ]
        swap_b = swap(grads_b)
        plane_a = flights.add(plane_steps(grads_a[0], swap_a["result"], mesh), [])
    else:
        small_job = flights.add(small_sum_steps(small, mesh), [])
        sum_a, sum_b = (flights.add(sum_steps(grads, mesh, bf16), []) for (grads,) in (grads_a, grads_b))
    spans = ((0, slice(0, span)), (1, slice(0, span)))
    input_grad = flights.run(
        lambda x: input_back(x, [joined_grad_a], spans, [first, second], flat, low_grad, gain_one, seq),
        joined_grad_b,
    )
    if cut:
        plane_b = flights.add(plane_steps(grads_b[0], swap_b["result"], mesh), [])
    block_out = flights.run(
        lambda x: block_out_of(x, valid, active, both, bias_down, seq, 0, rows), middle
    )
    if cut:
        line = flights.add(line_steps([plane_a["result"], plane_b["result"]], mesh), [])
        flights.land(mlp_job)
        up_total, down_total = mlp_job["result"]
    else:
        flights.finish()
        mlp_total = mlp_job["result"].reshape(share, chunks, 2, width)
        up_total, down_total = mlp_total[:, :, 0], mlp_total[:, :, 1]
    up_total = up_total.reshape(share, chunks, count, share).transpose(0, 2, 1, 3).reshape(-1)
    down_total = down_total.reshape(share, chunks, width).transpose(1, 0, 2).reshape(-1)
    up_total, down_total = flights.finish_after((up_total, down_total))
    if cut:
        edge_a = grads_a[0].shape[-1]
        total_a, total_b = line["result"][:, :edge_a], line["result"][:, edge_a:]
        small_total = total_b[:small_rows, span:].reshape(-1)
        small_total = small_total[: edge + biases.shape[0]]
    else:
        total_a, total_b = sum_a["result"], sum_b["result"]
        small_total = small_job["result"]
    return (
        block_out.reshape(tokens.shape),
        input_grad.reshape(tokens.shape),
        by_kind(total_a, total_b).reshape(-1),
        total_a[:, span:].reshape(-1),
        up_total,
        down_total,
        small_total[:edge],
        small_total[edge:],
    )


def solution(mesh):
    split = P(AXES)
    whole = P(AXES, None, None)
    return jax.shard_map(
        functools.partial(local, mesh),
        mesh=mesh,
        in_specs=(whole, whole) + (split,) * 8,
        out_specs=(whole, whole) + (split,) * 6,
        check_vma=False,
    )
```

```python
import functools
import math

import jax
import jax.numpy as jnp
from jax import lax
from jax.experimental import pallas as pl
from jax.experimental.pallas import tpu as pltpu
from jax.sharding import PartitionSpec as P

HEADS = 12
PATCH_SMALL = 196
PATCH_LARGE = 576
AXES = ("dp", "fsdp")
bf16 = jnp.bfloat16
f32 = jnp.float32
NN = (((1,), (0,)), ((), ()))
NT = (((1,), (1,)), ((), ()))
TN = (((0,), (0,)), ((), ()))
VMEM_LIMIT = 60 * 2**20
TILE = 304
ATILE = 304
AHEAD = 1
MTILE = 304
MAHEAD = 1
LTILE = 608
LSUB = 304
BOT = 304
BTILE = 304
BAHEAD = 1
LOG2E = 1.4426950408889634


def dot(a, b, dims):
    return lax.dot_general(a, b, dims, preferred_element_type=f32)


def params(n):
    return pltpu.CompilerParams(
        vmem_limit_bytes=VMEM_LIMIT, dimension_semantics=("arbitrary",) * n
    )


def cost(*_):
    return pl.CostEstimate(flops=1, bytes_accessed=1, transcendentals=0)


def tile_of(seq):
    return TILE if seq % TILE == 0 else seq


def once(shape):
    return pl.BlockSpec(
        shape, lambda *_: (0,) * len(shape), pipeline_mode=pl.Buffered(buffer_count=1)
    )


def shape_of(shape, dtype):
    return jax.ShapeDtypeStruct(shape, dtype)


class Flights:
    def __init__(self):
        self.waiting = []
        self.flying = []

    def add(self, steps, lengths):
        job = {"steps": steps, "lengths": list(lengths), "result": None}
        self.advance(job, None)
        return job

    def advance(self, job, came):
        try:
            sends = job["steps"].send(came) if came is not None else next(job["steps"])
        except StopIteration as stop:
            job["result"] = lax.optimization_barrier(stop.value)
            return
        length = job["lengths"].pop(0) if job["lengths"] else 1
        self.waiting.append((job, sends, length))

    def depart(self):
        for job, sends, length in self.waiting:
            came = [lax.ppermute(array, AXES, pairs) for array, pairs in sends]
            self.flying.append([job, came, length])
        self.waiting = []

    def run(self, kernel, operand, *others):
        arrays = [array for _, sends, _ in self.waiting for array, _ in sends]
        if arrays:
            operand, arrays = lax.optimization_barrier((operand, arrays))
            left = iter(arrays)
            self.waiting = [
                (job, [(next(left), pairs) for _, pairs in sends], length)
                for job, sends, length in self.waiting
            ]
        self.depart()
        out = kernel(operand, *others)
        for flight in self.flying:
            flight[2] -= 1
        landed = [flight for flight in self.flying if flight[2] <= 0]
        self.flying = [flight for flight in self.flying if flight[2] > 0]
        if landed:
            out, came = lax.optimization_barrier((out, [flight[1] for flight in landed]))
            for flight, got in zip(landed, came):
                self.advance(flight[0], got)
        return out

    def land(self, job):
        self.depart()
        for flight in [flight for flight in self.flying if flight[0] is job]:
            self.flying.remove(flight)
            self.advance(job, flight[1])

    def finish_after(self, values):
        cames, values = lax.optimization_barrier(([flight[1] for flight in self.flying], values))
        for flight, came in zip(self.flying, cames):
            flight[1] = came
        self.finish()
        return values

    def finish(self, turns=None):
        turn = 0
        while (self.waiting or self.flying) and turn != turns:
            turn += 1
            self.depart()
            for flight in self.flying:
                flight[2] -= 1
            landed = [flight for flight in self.flying if turns is None or flight[2] <= 0]
            self.flying = [flight for flight in self.flying if not (turns is None or flight[2] <= 0)]
            cames = [flight[1] for flight in landed]
            if turns is not None:
                cames = lax.optimization_barrier(cames)
            for flight, came in zip(landed, cames):
                self.advance(flight[0], came)


def bit_groups(mesh):
    inner = int(math.log2(mesh.shape["fsdp"]))
    outer = int(math.log2(mesh.shape["dp"]))
    rest = [list(range(b, min(b + 2, inner))) for b in range(1, inner, 2)]
    return [0], list(range(inner, inner + outer)), rest


def position(me, bits):
    spot = 0
    for place, bit in enumerate(bits):
        spot = spot + ((me >> bit) & 1) * (1 << place)
    return spot


def partners(count, bits):
    swaps = []
    for step in range(1, 1 << len(bits)):
        mask = 0
        for place, bit in enumerate(bits):
            if (step >> place) & 1:
                mask |= 1 << bit
        swaps.append((step, [(i, i ^ mask) for i in range(count)]))
    return swaps


def gather_steps(shard, mesh, groups):
    count = mesh.size
    me = lax.axis_index(AXES)
    bits = int(math.log2(count))
    rows, columns = shard.shape
    held = shard.reshape((1,) * bits + (rows, columns))
    for group in groups:
        swaps = partners(count, group)
        came = yield [(held, pairs) for _, pairs in swaps]
        shape = list(held.shape)
        for bit in group:
            shape[bits - 1 - bit] = 2
        whole = jnp.zeros(shape, shard.dtype)
        for (step, _), got in zip([(0, None)] + swaps, [held] + came):
            start = [0] * len(shape)
            for place, bit in enumerate(group):
                start[bits - 1 - bit] = ((me >> bit) & 1) ^ ((step >> place) & 1)
            whole = lax.dynamic_update_slice(whole, got, start)
        held = whole
    return held.reshape(count * rows, columns)


def pick(array, axis, index):
    return lax.dynamic_slice_in_dim(array, index, 1, axis)


def total(terms, axis, index, kind):
    return sum(pick(term, axis, index).astype(f32) for term in terms).astype(kind)


def sum_steps(parts, mesh, kind):
    count = mesh.size
    core, outer, rest = bit_groups(mesh)
    me = lax.axis_index(AXES)
    rows, columns = parts.shape[0] // count, parts.shape[1]
    rest_size = mesh.shape["fsdp"] // 2
    held = parts.reshape(mesh.shape["dp"], rest_size, 2, rows, columns)
    spot = position(me, core)
    (got,) = yield [(pick(held, 2, spot ^ 1).astype(kind), partners(count, core)[0][1])]
    terms = [pick(held, 2, spot), got]
    split = 2 if len(outer) == 2 and columns % 256 == 0 else 1
    width = columns // split
    shape = (2,) * len(outer) + (rest_size, 1, rows, width)
    pieces = []
    for piece in range(split):
        own = [term[..., piece * width : (piece + 1) * width].reshape(shape) for term in terms]
        order = list(range(len(outer)))
        pieces.append((own, order if piece == 0 else order[::-1]))
    for turn in range(len(outer)):
        sends = []
        for own, order in pieces:
            axis = order[turn]
            bit = outer[len(outer) - 1 - axis]
            mine = position(me, [bit])
            sends.append((total(own, axis, mine ^ 1, kind), partners(count, [bit])[0][1]))
        came = yield sends
        pieces = [
            ([pick(term, order[turn], position(me, [outer[len(outer) - 1 - order[turn]]])) for term in own] + [got], order)
            for (own, order), got in zip(pieces, came)
        ]
    left = rest_size
    pieces = [[term.reshape(rest_size, rows, width) for term in own] for own, _ in pieces]
    for bits in reversed(rest):
        size = 1 << len(bits)
        left //= size
        pieces = [[term.reshape(size, left, rows, width) for term in own] for own in pieces]
        spot = position(me, bits)
        swaps = partners(count, bits)
        sends = [
            (jnp.concatenate([total(own, 0, spot ^ step, kind) for own in pieces], -1), pairs)
            for step, pairs in swaps
        ]
        came = yield sends
        pieces = [
            [pick(term, 0, spot) for term in own]
            + [got[..., place * width : (place + 1) * width] for got in came]
            for place, own in enumerate(pieces)
        ]
    sums = [sum(term.astype(f32) for term in own).reshape(rows, width) for own in pieces]
    return jnp.concatenate(sums, -1)


def send_sum_kernel(where, *refs, sizes):
    at = 0
    for size, out in zip(sizes, refs[sum(sizes) :]):
        out[...] = sum(term[...].astype(f32) for term in refs[at : at + size]).astype(out.dtype)
        at += size


def fold_first(where, keep, came):
    _, _, left, rows, columns = keep.shape
    cut = columns // 2
    spec_a = pl.BlockSpec((None, 2, 2, rows, cut), lambda j, where: ((where[1] // 2) ^ 1, 0, j, 0, 0))
    spec_b = pl.BlockSpec((2, None, 2, rows, cut), lambda j, where: (0, (where[1] % 2) ^ 1, j, 0, 1))
    return pl.pallas_call(
        functools.partial(send_sum_kernel, sizes=[2, 2]),
        grid_spec=pltpu.PrefetchScalarGridSpec(
            num_scalar_prefetch=1,
            grid=(left // 2,),
            in_specs=[spec_a, spec_a, spec_b, spec_b],
            out_specs=[pl.BlockSpec((2, 2, rows, cut), lambda j, where: (0, j, 0, 0))] * 2,
        ),
        out_shape=[shape_of((2, left, rows, cut), bf16)] * 2,
        compiler_params=params(1),
        cost_estimate=cost(),
        name="fold_first",
    )(where, keep, came, keep, came)


def fold_second(where, keep, came, came_a, came_b):
    _, _, left, rows, columns = keep.shape
    cut = columns // 2
    spec_a = pl.BlockSpec(
        (None, None, 2, rows, cut), lambda j, where: (where[1] // 2, (where[1] % 2) ^ 1, j, 0, 0)
    )
    spec_b = pl.BlockSpec(
        (None, None, 2, rows, cut), lambda j, where: ((where[1] // 2) ^ 1, where[1] % 2, j, 0, 1)
    )
    half_a = pl.BlockSpec((None, 2, rows, cut), lambda j, where: ((where[1] % 2) ^ 1, j, 0, 0))
    half_b = pl.BlockSpec((None, 2, rows, cut), lambda j, where: ((where[1] // 2) ^ 1, j, 0, 0))
    return pl.pallas_call(
        functools.partial(send_sum_kernel, sizes=[3, 3]),
        grid_spec=pltpu.PrefetchScalarGridSpec(
            num_scalar_prefetch=1,
            grid=(left // 2,),
            in_specs=[spec_a, spec_a, half_a, spec_b, spec_b, half_b],
            out_specs=[pl.BlockSpec((2, rows, cut), lambda j, where: (j, 0, 0))] * 2,
        ),
        out_shape=[shape_of((left, rows, cut), bf16)] * 2,
        compiler_params=params(1),
        cost_estimate=cost(),
        name="fold_second",
    )(where, keep, came, came_a, keep, came, came_b)


def line_first_kernel(where, *refs):
    *terms, keep, send = refs
    fast = where[2] % 2
    cut = terms[0].shape[-1]
    for place, out in ((fast, keep), (fast ^ 1, send)):
        for half in range(2):
            own = terms[4 * half : 4 * half + 4]
            lanes = slice(half * cut, (half + 1) * cut)
            out[:, lanes] = sum(term[place].astype(f32) for term in own).astype(out.dtype)


def line_first(where, keep, came, came_a, came_b, last_a, last_b):
    _, _, size, rows, columns = keep.shape
    cut = columns // 2
    whole = lambda half: pl.BlockSpec(
        (None, None, 2, rows, cut), lambda j, where: (where[1] // 2, where[1] % 2, j, 0, half)
    )
    half_a = pl.BlockSpec((None, 2, rows, cut), lambda j, where: (where[1] % 2, j, 0, 0))
    half_b = pl.BlockSpec((None, 2, rows, cut), lambda j, where: (where[1] // 2, j, 0, 0))
    last = pl.BlockSpec((2, rows, cut), lambda j, where: (j, 0, 0))
    return pl.pallas_call(
        line_first_kernel,
        grid_spec=pltpu.PrefetchScalarGridSpec(
            num_scalar_prefetch=1,
            grid=(size // 2,),
            in_specs=[whole(0), whole(0), half_a, last, whole(1), whole(1), half_b, last],
            out_specs=[pl.BlockSpec((None, rows, columns), lambda j, where: (j, 0, 0))] * 2,
        ),
        out_shape=[shape_of((size // 2, rows, columns), bf16)] * 2,
        compiler_params=params(1),
        cost_estimate=cost(),
        name="line_first",
    )(where, keep, came, came_a, last_a, keep, came, came_b, last_b)


def swap_steps(send, mesh):
    core, _, _ = bit_groups(mesh)
    (came,) = yield [(send, partners(mesh.size, core)[0][1])]
    return came


def part_of(terms, axis, index, kind):
    total = None
    for term in terms:
        if term.shape[axis] != 1:
            term = pick(term, axis, index)
        total = term.astype(f32) if total is None else total + term.astype(f32)
    return total.astype(kind)


def plane_steps(keep, came, mesh):
    count = mesh.size
    _, outer, rest = bit_groups(mesh)
    spot = position(lax.axis_index(AXES), outer)
    size = 1 << len(outer)
    terms = [array.reshape((size, 1 << len(rest[0])) + keep.shape[1:]) for array in (keep, came)]
    sends = [part_of(terms, 0, spot ^ step, bf16)[0] for step in range(1, size)]
    came = yield [(array, pairs) for array, (_, pairs) in zip(sends, partners(count, outer))]
    return [pick(term, 0, spot)[0] for term in terms] + came


def line_steps(terms, mesh):
    count = mesh.size
    _, _, rest = bit_groups(mesh)
    spot = position(lax.axis_index(AXES), rest[0])
    came = yield [
        (part_of(terms, 0, spot ^ step, bf16)[0], pairs) for step, pairs in partners(count, rest[0])
    ]
    return part_of(terms, 0, spot, f32)[0] + sum(array.astype(f32) for array in came)


def line_fold_steps(terms, mesh):
    count = mesh.size
    _, _, rest = bit_groups(mesh)
    me = lax.axis_index(AXES)
    terms = [term.reshape((2, 2) + term.shape[1:]) for term in terms]
    for axis, bit in ((1, rest[0][0]), (0, rest[0][1])):
        spot = position(me, [bit])
        came = yield [(part_of(terms, axis, spot ^ 1, bf16), partners(count, [bit])[0][1])]
        terms = [pick(term, axis, spot) for term in terms] + came
    return sum(term.astype(f32) for term in terms)[0, 0]


def fold_sum_steps(keep, send, where, mesh):
    count = mesh.size
    core, outer, rest = bit_groups(mesh)
    (came,) = yield [(send, partners(count, core)[0][1])]
    shape = (2, 2, 1 << len(rest[0]), keep.shape[0] * 2 // count, keep.shape[1])
    keep, came = keep.reshape(shape), came.reshape(shape)
    fast, slow = (partners(count, [bit])[0][1] for bit in outer)
    send_a, send_b = fold_first(where, keep, came)
    came_a, came_b = yield [(send_a, slow), (send_b, fast)]
    send_a, send_b = fold_second(where, keep, came, came_a, came_b)
    last_a, last_b = yield [(send_a, fast), (send_b, slow)]
    keep, send = line_first(where, keep, came, came_a, came_b, last_a, last_b)
    (came,) = yield [(send, partners(count, [rest[0][0]])[0][1])]
    me = lax.axis_index(AXES)
    spot = position(me, [rest[0][1]])
    both = [keep, came]
    (last,) = yield [(total(both, 0, spot ^ 1, bf16), partners(count, [rest[0][1]])[0][1])]
    done = (total(both, 0, spot, f32) + last.astype(f32)).reshape(2, shape[3] // 2, shape[4])
    spot = position(me, core)
    (came,) = yield [(pick(done, 0, spot ^ 1), partners(count, core)[0][1])]
    own, came = pick(done, 0, spot)[0], came[0]
    return jnp.where(spot == 0, own, came), jnp.where(spot == 0, came, own)


def small_sum_steps(parts, mesh):
    count = mesh.size
    core, outer, rest = bit_groups(mesh)
    groups = [core, outer, *reversed(rest)]
    order = [outer, *reversed(rest), core]
    me = lax.axis_index(AXES)
    columns = parts.shape[1]
    held = parts.reshape([1 << len(bits) for bits in order] + [columns])
    for bits in groups:
        axis = order.index(bits)
        spot = position(me, bits)
        swaps = partners(count, bits)
        came = yield [(pick(held, axis, spot ^ step), pairs) for step, pairs in swaps]
        held = pick(held, axis, spot) + sum(came)
    return held.reshape(columns)


def cut_by_core(mesh):
    _, outer, rest = bit_groups(mesh)
    return len(outer) == 2 and len(rest) == 1 and len(rest[0]) == 2


def store_cut(core, outs, lanes, value, rows):
    if len(outs) == 1:
        outs[0][:, lanes] = value.astype(bf16)
        return
    keep, send = outs
    for parity in range(2):
        @pl.when(core == parity)
        def _():
            for device in range(value.shape[0] // rows):
                out = keep if device % 2 == parity else send
                out[device // 2, :, lanes] = value[device * rows : (device + 1) * rows, :].astype(bf16)


def cut_shapes(width, columns, chunk, index, rows):
    if not rows:
        spec = pl.BlockSpec((width, chunk), lambda j, *_: (0, index(j)))
        return [spec], [shape_of((width, columns), bf16)]
    blocks = width // rows // 2
    spec = pl.BlockSpec((blocks, rows, chunk), lambda j, *_: (0, 0, index(j)))
    return [spec] * 2, [shape_of((blocks, rows, columns), bf16)] * 2


def normalize(values):
    center = values - jnp.mean(values, -1, keepdims=True)
    scale = lax.rsqrt(jnp.mean(center * center, -1, keepdims=True) + 1e-05)
    return center * scale, scale


def norm_back(grad, gain, unit, scale):
    inner = grad * gain
    return scale * (
        inner
        - jnp.mean(inner, -1, keepdims=True)
        - unit * jnp.mean(inner * unit, -1, keepdims=True)
    )


def gelu_parts(u):
    phi = 0.5 + 0.5 * lax.erf(u * 0.7071067811865476)
    slope = phi + u * (0.3989422804014327 * jnp.exp2((u * u) * (-0.5 * LOG2E)))
    return u * phi, slope


def column_sum(values):
    return jnp.sum(values, 0, keepdims=True)


def accumulate(ref, value, first):
    @pl.when(first)
    def _():
        ref[...] = value

    @pl.when(jnp.logical_not(first))
    def _():
        ref[...] += value


def two_heads(block, padded):
    seq = block.shape[0]
    first = lax.broadcasted_iota(jnp.int32, block.shape, 1) < 64
    zero = jnp.zeros_like(block)
    pad = jnp.zeros((padded - seq, 128), block.dtype)
    return jnp.concatenate(
        [jnp.where(first, block, zero), pad, jnp.where(first, zero, block), pad], 0
    )


def attend_kernel(valid, *refs, tile, padded, first, pairs):
    if first:
        tokens, gain, shift, weight, bias, normed, joined, mixed, raised_out, inverse = refs
    else:
        (
            normed, weight, bias, tokens, mixed_first, bias_out, gain, shift,
            joined, mixed, raised_out, inverse, middle, normed_two,
        ) = refs
    seq, span = joined.shape
    for start in range(0, seq, tile):
        rows = slice(start, start + tile)
        if first:
            unit, _ = normalize(tokens[rows, :].astype(f32))
            low = (unit * gain[...] + shift[...]).astype(bf16)
            normed[rows, :] = low
        else:
            low = normed[rows, :]
        joined[rows, :] = (dot(low, weight[:, :span], NN) + bias[...]).astype(bf16)

    column = lax.broadcasted_iota(jnp.int32, (1, padded), 1)
    mask = jnp.where(column < valid[pl.program_id(0)], 0.0, -1e30).astype(f32)
    places = [(pair, start) for pair in range(pairs) for start in range(0, seq, ATILE)]
    keys, values = {}, {}
    row = lax.broadcasted_iota(jnp.int32, (2 * padded, 128), 0)
    lane = lax.broadcasted_iota(jnp.int32, (2 * padded, 128), 1)
    ones = jnp.where((row < padded) == (lane < 64), 1.0, 0.0).astype(bf16)

    def scores_at(pair, start):
        if pair not in keys:
            at = pair * 384
            keys[pair] = two_heads(joined[:, at + 128 : at + 256], padded)
            values[pair] = jnp.concatenate([two_heads(joined[:, at + 256 : at + 384], padded), ones], 1)
        return dot(joined[start : start + ATILE, pair * 384 : pair * 384 + 128], keys[pair], NT)

    ahead = [scores_at(*place) for place in places[:AHEAD]]
    for index, (pair, start) in enumerate(places):
        rows = slice(start, start + ATILE)
        if index + AHEAD < len(places):
            ahead.append(scores_at(*places[index + AHEAD]))
        scores = ahead.pop(0)
        halves = []
        for head in range(2):
            part = scores[:, head * padded : (head + 1) * padded] * (0.125 * LOG2E) + mask
            halves.append(jnp.exp2(part - jnp.max(part, 1, keepdims=True)).astype(bf16))
        raised = jnp.concatenate(halves, 1)
        raised_out[pair, rows, :] = raised
        both = dot(raised, values[pair], NN)
        scale = 1.0 / both[:, 128:]
        inverse[rows, pair * 128 : (pair + 1) * 128] = scale
        mixed[rows, pair * 128 : (pair + 1) * 128] = (both[:, :128] * scale).astype(bf16)
    if first:
        return
    width = tokens.shape[1]
    for start in range(0, seq, tile):
        rows = slice(start, start + tile)
        value = tokens[rows, :].astype(f32) + bias_out[...]
        value = value + dot(mixed_first[rows, :], weight[: width // 2, -width:], NN)
        value = value + dot(mixed[rows, :], weight[width // 2 :, -width:], NN)
        middle[rows, :] = value
        unit, _ = normalize(value)
        normed_two[rows, :] = (unit * gain[...] + shift[...]).astype(bf16)


def attend(start, valid, weight, bias, seq, norm=None, after=None):
    rows, width = start.shape
    span = bias.shape[1]
    pairs = span // 384
    items = rows // seq
    padded = -(-seq // 128) * 128
    row = lambda w: pl.BlockSpec((seq, w), lambda i, *_: (i, 0))
    one = once((1, width))
    main = [once(weight.shape), once((1, span))]
    if norm:
        specs, arrays = [row(width), one, one, *main], [start, *norm, weight, bias]
    else:
        specs = [row(width), *main, row(width), row(width // 2), one, one, one]
        arrays = [start, weight, bias, *after]
    outs = [
        row(span),
        row(span // 3),
        pl.BlockSpec((None, pairs, seq, 2 * padded), lambda i, *_: (i, 0, 0, 0)),
        row(span // 3),
    ]
    shapes = [
        shape_of((rows, span), bf16),
        shape_of((rows, span // 3), bf16),
        shape_of((items, pairs, seq, 2 * padded), bf16),
        shape_of((rows, span // 3), f32),
    ]
    if norm:
        outs, shapes = [row(width)] + outs, [shape_of((rows, width), bf16)] + shapes
    else:
        outs += [row(width)] * 2
        shapes += [shape_of((rows, width), f32), shape_of((rows, width), bf16)]
    return pl.pallas_call(
        functools.partial(attend_kernel, tile=tile_of(seq), padded=padded, first=bool(norm), pairs=pairs),
        grid_spec=pltpu.PrefetchScalarGridSpec(
            num_scalar_prefetch=1, grid=(items,), in_specs=specs, out_specs=outs
        ),
        out_shape=shapes,
        compiler_params=params(1),
        cost_estimate=cost(),
        name="attend",
    )(valid, *arrays)


def attend_back_kernel(where, *refs, pairs, extra, spare, cut):
    lists = [refs[kind * pairs : (kind + 1) * pairs] for kind in range(5)]
    joined, mixed_grad, mixed, raised, inverse = lists
    normed, weight, *rest = refs[5 * pairs :]
    if extra:
        mixed_a, mixed_b, low_grad, *rest, total_out = rest
    joined_grad, column, gain_sum, shift_sum, *outs, held, scaled, total = rest
    item = pl.program_id(0)
    seq, span = joined_grad.shape
    padded = raised[0].shape[1] // 2
    tile = BTILE if seq % BTILE == 0 else seq
    first = lax.broadcasted_iota(jnp.int32, (tile, 128), 1) < 64
    places = [(pair, start) for pair in range(pairs) for start in range(0, seq, tile)]
    keys, values = {}, {}

    def prob_grad_at(pair, start):
        if pair not in keys:
            keys[pair] = two_heads(joined[pair][:, 128:256], padded)
            values[pair] = two_heads(joined[pair][:, 256:], padded)
        rows = slice(start, start + tile)
        grad = (mixed_grad[pair][rows, :].astype(f32) * inverse[pair][rows, :]).astype(bf16)
        scaled[pair, rows, :] = grad
        return grad, dot(grad, values[pair], NT)

    def own_half(both):
        return jnp.concatenate([both[:64, :padded], both[64:, padded:]], 0).T[:seq]

    ahead = [prob_grad_at(*place) for place in places[:BAHEAD]]
    for index, (pair, start) in enumerate(places):
        rows = slice(start, start + tile)
        at = pair * 384
        if index + BAHEAD < len(places):
            ahead.append(prob_grad_at(*places[index + BAHEAD]))
        grad, prob_grad = ahead.pop(0)
        product = grad.astype(f32) * mixed[pair][rows, :].astype(f32)
        zero = jnp.zeros_like(product)
        halves = []
        for head in range(2):
            own = jnp.where(first, product, zero) if head == 0 else jnp.where(first, zero, product)
            centre = jnp.sum(own, 1, keepdims=True)
            half = slice(head * padded, (head + 1) * padded)
            halves.append((raised[pair][rows, half].astype(f32) * (prob_grad[:, half] - centre)).astype(bf16))
        score_grad = jnp.concatenate(halves, 1)
        held[rows, :] = score_grad
        joined_grad[rows, at : at + 128] = (dot(score_grad, keys[pair], NN) * 0.125).astype(bf16)
        if start + tile == seq:
            joined_grad[:, at + 128 : at + 256] = (
                own_half(dot(joined[pair][:, :128].T, held[...], NN)) * 0.125
            ).astype(bf16)
            joined_grad[:, at + 256 : at + 384] = own_half(
                dot(scaled[pair].T, raised[pair][...], NN)
            ).astype(bf16)

    value = joined_grad[...]
    accumulate(total, dot(normed[...], value, TN), item == 0)
    accumulate(column, column_sum(value.astype(f32)), item == 0)
    if extra:
        both = [dot(mixed_a[...], low_grad[...], TN), dot(mixed_b[...], low_grad[...], TN)]
        accumulate(total_out, jnp.concatenate(both, 0), item == 0)

    @pl.when(item == pl.num_programs(0) - 1)
    def _():
        store_cut(where[0], outs, slice(0, span), total[...], cut)
        if spare:
            for out in outs:
                out[..., span:] = jnp.zeros(out.shape[:-1] + (spare,), bf16)
        wide = weight[...].astype(f32)
        for ref, product in ((gain_sum, wide * total[...]), (shift_sum, wide * column[...])):
            row = jnp.sum(product, 1, keepdims=True)
            ref[...] = jnp.broadcast_to(row, (row.shape[0], 128)).T[:1]
        if extra:
            store_cut(where[0], outs, slice(span, span + total_out.shape[1]), total_out[...], cut)


def attend_back(mixed_grad, where, joined, mixed, raised, inverse, normed, weight, seq, part, cut, others=(), spare=0):
    rows, width = normed.shape
    items, in_part, _, keys = raised.shape
    pairs = in_part
    chosen = range(pairs)
    span = 384 * pairs
    row = lambda w, off=0: pl.BlockSpec((seq, w), lambda i, *_: (i, off))
    each = lambda w, off=0: [row(w, off + pair) for pair in chosen]
    weights = [
        pl.BlockSpec((None, None, seq, keys), functools.partial(lambda at, i, *_: (i, at, 0, 0), pair))
        for pair in chosen
    ]
    columns = span + (width if others else 0) + spare
    one = pl.BlockSpec((1, width), lambda i, *_: (0, 0))
    specs, shapes = cut_shapes(width, columns, columns, lambda j: 0, cut)
    return pl.pallas_call(
        functools.partial(
            attend_back_kernel, pairs=pairs, extra=bool(others), spare=spare, cut=cut
        ),
        grid_spec=pltpu.PrefetchScalarGridSpec(
            num_scalar_prefetch=1,
            grid=(items,),
            in_specs=[
                *each(384), *each(128, part * in_part), *each(128), *weights, *each(128), row(width)
            ]
            + [once((width, span))]
            + [row(array.shape[1]) for array in others],
            out_specs=[row(span), pl.BlockSpec((1, span), lambda i, *_: (0, 0)), one, one] + specs,
            scratch_shapes=[
                pltpu.VMEM((seq, keys), bf16),
                pltpu.VMEM((pairs, seq, 128), bf16),
                pltpu.VMEM((width, span), f32),
            ]
            + ([pltpu.VMEM((width, width), f32)] if others else []),
        ),
        out_shape=[shape_of((rows, span), bf16), shape_of((1, span), f32)]
        + [shape_of((1, width), f32)] * 2
        + shapes,
        compiler_params=params(1),
        cost_estimate=cost(),
        name="attend_back",
    )(
        where, *[joined] * pairs, *[mixed_grad] * pairs, *[mixed] * pairs, *[raised] * pairs,
        *[inverse] * pairs, normed, weight, *others,
    )


def mlp_kernel(
    valid, where, normed, cotangent, up, down, bias_up,
    active, hidden_grad, up_sum, *rest, seq, tile, cut,
):
    *outs, grad = rest
    rows, width = normed.shape

    @pl.when(pl.program_id(0) == 0)
    def _():
        place = lax.broadcasted_iota(jnp.int32, (seq, 1), 0)
        for item in range(rows // seq):
            span = slice(item * seq, (item + 1) * seq)
            grad[span, :] = jnp.where(place < valid[item], cotangent[span, :].astype(f32), 0.0).astype(bf16)

    def ahead_of(start):
        span = slice(start, start + MTILE)
        return dot(normed[span, :], up[...], NN), dot(grad[span, :], down[...], NT)

    column = jnp.zeros(up_sum.shape, f32)
    starts = list(range(0, rows, MTILE))
    ahead = [ahead_of(start) for start in starts[:MAHEAD]]
    for index, start in enumerate(starts):
        span = slice(start, start + MTILE)
        if index + MAHEAD < len(starts):
            ahead.append(ahead_of(starts[index + MAHEAD]))
        hidden, wide = ahead.pop(0)
        value, slope = gelu_parts(hidden + bias_up[...])
        low = (slope * wide).astype(bf16)
        active[span, :] = value.astype(bf16)
        hidden_grad[span, :] = low
        column = column + column_sum(low.astype(f32))
    up_sum[...] = column
    first = dot(normed[...], hidden_grad[...], TN).astype(bf16)
    second = dot(active[...], grad[...], TN).astype(bf16)
    if cut:
        keep, send = outs
        for core in range(2):
            @pl.when(where[0] == core)
            def _():
                (keep, send)[core][...] = first
                (send, keep)[core][...] = second
    else:
        outs[0][:, :width] = first
        outs[0][:, width:] = second


def mlp(normed, valid, where, cotangent, both, bias_up, seq, cut):
    rows, width = normed.shape
    wide = both.shape[1] // 2
    chunks = wide // width
    whole = once((rows, width))
    square = lambda off: pl.BlockSpec((width, width), lambda j, *_: (0, j + off))
    row = pl.BlockSpec((rows, width), lambda j, *_: (0, j))
    one = pl.BlockSpec((1, width), lambda j, *_: (0, j))
    if cut:
        specs = [pl.BlockSpec((width, width), lambda j, *_: (0, j))] * 2
        shapes = [shape_of((width, wide), bf16)] * 2
    else:
        specs, shapes = cut_shapes(width, 2 * wide, 2 * width, lambda j: j, 0)
    return pl.pallas_call(
        functools.partial(mlp_kernel, seq=seq, tile=tile_of(seq), cut=cut),
        grid_spec=pltpu.PrefetchScalarGridSpec(
            num_scalar_prefetch=2,
            grid=(chunks,),
            in_specs=[whole, whole, square(0), square(chunks), one],
            out_specs=[row, row, one] + specs,
            scratch_shapes=[pltpu.VMEM((rows, width), bf16)],
        ),
        out_shape=[
            shape_of((rows, width * chunks), bf16),
            shape_of((rows, width * chunks), bf16),
            shape_of((1, width * chunks), f32),
        ]
        + shapes,
        compiler_params=params(1),
        cost_estimate=cost(),
        name="mlp",
    )(valid, where, normed, cotangent, both, both, bias_up)


def block_out_kernel(valid, active, downs, middle, bias_down, *rest, seq, begin):
    block_out = rest[-1]
    tile, width = middle.shape
    step = pl.program_id(0) + begin // tile
    place = lax.broadcasted_iota(jnp.int32, (tile, 1), 0) + lax.rem(step, seq // tile) * tile
    value = middle[...] + bias_down[...]
    for at in range(0, downs.shape[1], width):
        value = value + dot(active[:, at : at + width], downs[:, at : at + width], NN)
    block_out[...] = jnp.where(place < valid[step // (seq // tile)], value, 0.0).astype(bf16)


def half_of(both, second):
    width, columns = both.shape
    return pl.BlockSpec(
        (width, columns // 2), lambda j, *_: (0, second), pipeline_mode=pl.Buffered(buffer_count=1)
    )


def block_out_of(middle, valid, active, both, bias_down, seq, begin, end, before=None):
    rows, width = middle.shape
    tile = BOT if seq % BOT == 0 else seq
    skip = begin // tile
    row = lambda w: pl.BlockSpec((tile, w), lambda j, *_: (j + skip, 0))
    specs = [row(active.shape[1]), half_of(both, 1), row(width), once((1, width))]
    arrays = [active, both, middle, bias_down]
    aliases = {}
    if before is not None:
        aliases = {len(arrays) + 1: 0}
        specs.append(pl.BlockSpec(memory_space=pl.ANY))
        arrays.append(before)
    return pl.pallas_call(
        functools.partial(block_out_kernel, seq=seq, begin=begin),
        grid_spec=pltpu.PrefetchScalarGridSpec(
            num_scalar_prefetch=1,
            grid=((end - begin) // tile,),
            in_specs=specs,
            out_specs=row(width),
        ),
        out_shape=shape_of((rows, width), bf16),
        input_output_aliases=aliases,
        compiler_params=params(1),
        cost_estimate=cost(),
        name="block_out",
    )(valid, *arrays)


def middle_back_kernel(
    valid, hidden_grad, ups, middle, cotangent, gain, weight_a, weight_b,
    low_grad, mixed_grad, gain_sum, shift_sum, bias_sum, down_sum, *, seq, sub,
):
    step = pl.program_id(0)
    tile, width = middle.shape
    each = seq // tile
    starts = list(range(0, tile, sub))
    ahead = [dot(hidden_grad[:sub, :], ups[...], NT)]
    sums = [jnp.zeros((1, width), f32)] * 4
    for index, start in enumerate(starts):
        rows = slice(start, start + sub)
        if index + 1 < len(starts):
            ahead.append(dot(hidden_grad[start + sub : start + 2 * sub, :], ups[...], NT))
        grad = ahead.pop(0)
        unit, scale = normalize(middle[rows, :])
        place = lax.broadcasted_iota(jnp.int32, (sub, 1), 0) + (lax.rem(step, each) * tile + start)
        kept = jnp.where(place < valid[step // each], cotangent[rows, :].astype(f32), 0.0)
        low = (kept + norm_back(grad, gain[...], unit, scale)).astype(bf16)
        low_grad[rows, :] = low
        mixed_grad[rows, :] = (
            dot(low[:, : width // 2], weight_a[...], NT) + dot(low[:, width // 2 :], weight_b[...], NT)
        ).astype(bf16)
        terms = (grad * unit, grad, low.astype(f32), kept)
        sums = [before + column_sum(term) for before, term in zip(sums, terms)]
    for ref, value in zip((gain_sum, shift_sum, bias_sum, down_sum), sums):
        accumulate(ref, value, step == 0)


def middle_back(middle, valid, hidden_grad, both, cotangent, gain, weight, seq):
    rows, width = middle.shape
    tile = LTILE if seq % LTILE == 0 else seq
    sub = LSUB if tile % LSUB == 0 else tile
    row = lambda w: pl.BlockSpec((tile, w), lambda j, *_: (j, 0))
    one = pl.BlockSpec((1, width), lambda j, *_: (0, 0))
    half = width // 2
    at = weight.shape[1] // half - 2
    halves = [
        pl.BlockSpec((width, half), lambda j, *_: (0, at), pipeline_mode=pl.Buffered(buffer_count=1)),
        pl.BlockSpec((width, half), lambda j, *_: (0, at + 1), pipeline_mode=pl.Buffered(buffer_count=1)),
    ]
    return pl.pallas_call(
        functools.partial(middle_back_kernel, seq=seq, sub=sub),
        grid_spec=pltpu.PrefetchScalarGridSpec(
            num_scalar_prefetch=1,
            grid=(rows // tile,),
            in_specs=[
                row(hidden_grad.shape[1]), half_of(both, 0), row(width), row(width),
                once((1, width)), *halves,
            ],
            out_specs=[row(width), row(width)] + [one] * 4,
        ),
        out_shape=[shape_of((rows, width), bf16)] * 2 + [shape_of((1, width), f32)] * 4,
        compiler_params=params(1),
        cost_estimate=cost(),
        name="middle_back",
    )(valid, hidden_grad, both, middle, cotangent, gain, weight, weight)


def input_back_kernel(*refs, spans, sub):
    grads = refs[: len(spans)]
    weights = refs[len(spans) : len(spans) + 2]
    tokens, low_grad, gain, input_grad = refs[len(spans) + 2 :]
    tile, width = tokens.shape

    def ahead_of(start):
        rows = slice(start, start + sub)
        terms = [
            dot(grad[rows, :], weights[which][:, lanes], NT) for grad, (which, lanes) in zip(grads, spans)
        ]
        return sum(terms[1:], terms[0])

    starts = list(range(0, tile, sub))
    ahead = [ahead_of(0)]
    for index, start in enumerate(starts):
        rows = slice(start, start + sub)
        if index + 1 < len(starts):
            ahead.append(ahead_of(start + sub))
        grad = ahead.pop(0)
        unit, scale = normalize(tokens[rows, :].astype(f32))
        full = low_grad[rows, :].astype(f32) + norm_back(grad, gain[...], unit, scale)
        input_grad[rows, :] = full.astype(bf16)


def input_back(last, others, spans, weights, tokens, low_grad, gain, seq):
    rows, width = tokens.shape
    tile = LTILE if seq % LTILE == 0 else seq
    sub = LSUB if tile % LSUB == 0 else tile
    row = lambda w: pl.BlockSpec((tile, w), lambda i: (i, 0))
    grads = [*others, last]
    return pl.pallas_call(
        functools.partial(input_back_kernel, spans=spans, sub=sub),
        grid=(rows // tile,),
        in_specs=[row(grad.shape[1]) for grad in grads]
        + [once((width, spans[0][1].stop))] * 2
        + [row(width), row(width), once((1, width))],
        out_specs=row(width),
        out_shape=shape_of((rows, width), bf16),
        compiler_params=params(1),
        cost_estimate=cost(),
        name="input_back",
    )(*grads, *weights, tokens, low_grad, gain)


def local(mesh, tokens, cotangent, group, text_len, qkv_w, out_w, mlp_in, mlp_out, gains, biases):
    items, seq, width = tokens.shape
    rows = items * seq
    count = mesh.size
    share = width // count
    wide = mlp_in.shape[0] // share
    chunks = wide // width
    half = width // 2
    span = 3 * half
    valid = (PATCH_SMALL + (PATCH_LARGE - PATCH_SMALL) * group + text_len).astype(jnp.int32)
    flat = tokens.reshape(rows, width)
    cot = cotangent.reshape(rows, width)
    flights = Flights()
    me = lax.axis_index(AXES)
    core, outer, others = bit_groups(mesh)
    where = jnp.stack([position(me, core), position(me, outer), position(me, others[0])]).astype(jnp.int32)
    cut = share if cut_by_core(mesh) and share % 8 == 0 else 0

    def mlp_sums(arrays):
        if cut:
            return flights.add(fold_sum_steps(*arrays, where, mesh), [])
        return flights.add(sum_steps(arrays[0], mesh, bf16), [])

    def swap(arrays):
        return flights.add(swap_steps(arrays[1], mesh), []) if cut else None

    def by_pairs(matrix, part):
        rows = matrix.shape[0]
        cubes = matrix.reshape(rows, 3, 2, half // 128, 128)[:, :, part]
        return cubes.transpose(0, 2, 1, 3).reshape(rows, span)

    def by_kind(part_a, part_b):
        rows = part_a.shape[0]
        cubes = [piece[:, :span].reshape(rows, half // 128, 3, 128) for piece in (part_a, part_b)]
        return jnp.stack(cubes, 1).transpose(0, 3, 1, 2, 4).reshape(rows, 3 * width)

    own_up = mlp_in.reshape(share, count, chunks, share).transpose(0, 2, 1, 3).reshape(share, wide)
    own_down = mlp_out.reshape(chunks, share, width).transpose(1, 0, 2).reshape(share, wide)
    own_both = jnp.concatenate([own_up, own_down], 1)

    own_qkv = qkv_w.reshape(share, 3 * width)
    small = jnp.concatenate([gains, biases])
    small_rows = -(-small.shape[0] // 128)
    padded = jnp.pad(small, (0, small_rows * 128 - small.shape[0])).reshape(small_rows, 128)
    padded = jnp.pad(padded, ((0, share - small_rows), (0, 0)))
    both = lax.all_gather(own_both, AXES, axis=0, tiled=True)
    own_first = jnp.concatenate([by_pairs(own_qkv, 0), padded], 1)
    own_second = jnp.concatenate([by_pairs(own_qkv, 1), out_w.reshape(share, width)], 1)
    singles = [[bit] for group in reversed(others) for bit in reversed(group)]
    job = flights.add(gather_steps(own_first, mesh, [*others, outer, core]), [])
    second_job = flights.add(gather_steps(own_second, mesh, [*singles, outer, core]), [1] * len(singles) + [2])
    flights.finish(len(others) + 2)
    first = job["result"]
    small = first[:, span:].reshape(count, share, 128)[:, :small_rows]
    small = small.reshape(count, small_rows * 128).astype(f32)
    edge = gains.shape[0]
    gain = small[:, :edge].reshape(1, 2 * width)
    bias = small[:, edge : edge + biases.shape[0]].reshape(1, 6 * width + wide)
    gain_one, gain_two = gain[:, :width], gain[:, width:]
    bias_query, bias_value, bias_output, shift_one, shift_two, bias_down = (
        bias[:, p * width : (p + 1) * width] for p in range(6)
    )
    bias_up = bias[:, 6 * width :].reshape(count, chunks, share).transpose(1, 0, 2).reshape(1, wide)
    bias_joined = jnp.concatenate([bias_query, jnp.zeros_like(bias_query), bias_value], 1)
    bias_parts = [by_pairs(bias_joined, part) for part in range(2)]

    normed, joined_a, mixed_a, raised_a, inverse_a = flights.run(
        lambda x: attend(x, valid, first, bias_parts[0], seq, (gain_one, shift_one)), flat
    )
    flights.finish()
    second = second_job["result"]
    joined_b, mixed_b, raised_b, inverse_b, middle, normed_two = attend(
        normed, valid, second, bias_parts[1], seq,
        after=(flat, mixed_a, bias_output, gain_two, shift_two),
    )

    active, hidden_grad, up_sum, *mlp_grads = mlp(
        normed_two, valid, where, cot, both, bias_up, seq, cut
    )
    mlp_job = mlp_sums(mlp_grads)

    low_grad, mixed_grad, gain_two_sum, shift_two_sum, bias_out_sum, down_sum = flights.run(
        lambda x: middle_back(x, valid, hidden_grad, both, cot, gain_two, second, seq), middle
    )
    joined_grad_a, qkv_sum_a, gain_sum_a, shift_sum_a, *grads_a = flights.run(
        lambda x: attend_back(
            x, where, joined_a, mixed_a, raised_a, inverse_a, normed, first, seq, 0, cut,
            others=(mixed_a, mixed_b, low_grad),
        ),
        mixed_grad,
    )
    swap_a = swap(grads_a)
    joined_grad_b, qkv_sum_b, gain_sum_b, shift_sum_b, *grads_b = flights.run(
        lambda x: attend_back(
            x, where, joined_b, mixed_b, raised_b, inverse_b, normed, second, seq, 1, cut,
            spare=128 if cut else 0,
        ),
        mixed_grad,
    )
    shift_one_sum = shift_sum_a + shift_sum_b
    gain_one_sum = (gain_sum_a + gain_sum_b - shift_one * shift_one_sum) / gain_one
    joined_sums = by_kind(qkv_sum_a, qkv_sum_b)
    up_sum = up_sum.reshape(chunks, count, share).transpose(1, 0, 2).reshape(1, wide)
    gain_sums = jnp.concatenate([gain_one_sum, gain_two_sum], 1).reshape(count, edge)
    bias_sums = jnp.concatenate(
        [
            joined_sums[:, :width],
            joined_sums[:, 2 * width :],
            bias_out_sum,
            shift_one_sum,
            shift_two_sum,
            down_sum,
            up_sum,
        ],
        1,
    ).reshape(count, biases.shape[0])
    small = jnp.concatenate([gain_sums, bias_sums], 1)
    if cut:
        small = jnp.pad(small, ((0, 0), (0, small_rows * 128 - small.shape[1])))
        small = small.reshape(count // 2, 2, small_rows, 128)
        spot = position(me, core)
        grads_b = [
            lax.dynamic_update_slice(grads, pick(small, 1, place)[:, 0].astype(bf16), (0, 0, span))
            for grads, place in zip(grads_b, (spot, spot ^ 1))
        ]
        swap_b = swap(grads_b)
        plane_a = flights.add(plane_steps(grads_a[0], swap_a["result"], mesh), [])
    else:
        small_job = flights.add(small_sum_steps(small, mesh), [])
        sum_a, sum_b = (flights.add(sum_steps(grads, mesh, bf16), []) for (grads,) in (grads_a, grads_b))
    spans = ((0, slice(0, span)), (1, slice(0, span)))
    input_grad = flights.run(
        lambda x: input_back(x, [joined_grad_a], spans, [first, second], flat, low_grad, gain_one, seq),
        joined_grad_b,
    )
    if cut:
        plane_b = flights.add(plane_steps(grads_b[0], swap_b["result"], mesh), [])
        line_a = flights.add(line_fold_steps(plane_a["result"], mesh), [])
    block_out = flights.run(
        lambda x: block_out_of(x, valid, active, both, bias_down, seq, 0, rows), middle
    )
    if cut:
        line_b = flights.add(line_steps(plane_b["result"], mesh), [])
        flights.land(mlp_job)
        up_total, down_total = mlp_job["result"]
    else:
        flights.finish()
        mlp_total = mlp_job["result"].reshape(share, chunks, 2, width)
        up_total, down_total = mlp_total[:, :, 0], mlp_total[:, :, 1]
    up_total = up_total.reshape(share, chunks, count, share).transpose(0, 2, 1, 3).reshape(-1)
    down_total = down_total.reshape(share, chunks, width).transpose(1, 0, 2).reshape(-1)
    up_total, down_total = flights.finish_after((up_total, down_total))
    if cut:
        total_a, total_b = line_a["result"], line_b["result"]
        small_total = total_b[:small_rows, span:].reshape(-1)
        small_total = small_total[: edge + biases.shape[0]]
    else:
        total_a, total_b = sum_a["result"], sum_b["result"]
        small_total = small_job["result"]
    return (
        block_out.reshape(tokens.shape),
        input_grad.reshape(tokens.shape),
        by_kind(total_a, total_b).reshape(-1),
        total_a[:, span:].reshape(-1),
        up_total,
        down_total,
        small_total[:edge],
        small_total[edge:],
    )


def solution(mesh):
    split = P(AXES)
    whole = P(AXES, None, None)
    return jax.shard_map(
        functools.partial(local, mesh),
        mesh=mesh,
        in_specs=(whole, whole) + (split,) * 8,
        out_specs=(whole, whole) + (split,) * 6,
        check_vma=False,
    )
```

```python
import functools
import math

import jax
import jax.numpy as jnp
from jax import lax
from jax.experimental import pallas as pl
from jax.experimental.pallas import tpu as pltpu
from jax.sharding import PartitionSpec as P

HEADS = 12
PATCH_SMALL = 196
PATCH_LARGE = 576
AXES = ("dp", "fsdp")
bf16 = jnp.bfloat16
f32 = jnp.float32
NN = (((1,), (0,)), ((), ()))
NT = (((1,), (1,)), ((), ()))
TN = (((0,), (0,)), ((), ()))
VMEM_LIMIT = 63 * 2**20
TILE = 304
ATILE = 304
AHEAD = 1
MTILE = 304
MAHEAD = 1
LTILE = 608
LSUB = 304
BOT = 304
BTILE = 304
BAHEAD = 1
LOG2E = 1.4426950408889634


def dot(a, b, dims):
    return lax.dot_general(a, b, dims, preferred_element_type=f32)


def params(n):
    return pltpu.CompilerParams(
        vmem_limit_bytes=VMEM_LIMIT, dimension_semantics=("arbitrary",) * n
    )


def cost(*_):
    return pl.CostEstimate(flops=1, bytes_accessed=1, transcendentals=0)


def tile_of(seq):
    return TILE if seq % TILE == 0 else seq


def once(shape):
    return pl.BlockSpec(
        shape, lambda *_: (0,) * len(shape), pipeline_mode=pl.Buffered(buffer_count=1)
    )


def shape_of(shape, dtype):
    return jax.ShapeDtypeStruct(shape, dtype)


class Flights:
    def __init__(self):
        self.waiting = []
        self.flying = []

    def add(self, steps, lengths):
        job = {"steps": steps, "lengths": list(lengths), "result": None}
        self.advance(job, None)
        return job

    def advance(self, job, came):
        try:
            sends = job["steps"].send(came) if came is not None else next(job["steps"])
        except StopIteration as stop:
            job["result"] = lax.optimization_barrier(stop.value)
            return
        length = job["lengths"].pop(0) if job["lengths"] else 1
        self.waiting.append((job, sends, length))

    def depart(self):
        for job, sends, length in self.waiting:
            came = [lax.ppermute(array, AXES, pairs) for array, pairs in sends]
            self.flying.append([job, came, length])
        self.waiting = []

    def run(self, kernel, operand, *others):
        arrays = [array for _, sends, _ in self.waiting for array, _ in sends]
        if arrays:
            operand, arrays = lax.optimization_barrier((operand, arrays))
            left = iter(arrays)
            self.waiting = [
                (job, [(next(left), pairs) for _, pairs in sends], length)
                for job, sends, length in self.waiting
            ]
        self.depart()
        out = kernel(operand, *others)
        for flight in self.flying:
            flight[2] -= 1
        landed = [flight for flight in self.flying if flight[2] <= 0]
        self.flying = [flight for flight in self.flying if flight[2] > 0]
        if landed:
            out, came = lax.optimization_barrier((out, [flight[1] for flight in landed]))
            for flight, got in zip(landed, came):
                self.advance(flight[0], got)
        return out

    def land(self, job):
        self.depart()
        for flight in [flight for flight in self.flying if flight[0] is job]:
            self.flying.remove(flight)
            self.advance(job, flight[1])

    def finish_after(self, values):
        cames, values = lax.optimization_barrier(([flight[1] for flight in self.flying], values))
        for flight, came in zip(self.flying, cames):
            flight[1] = came
        self.finish()
        return values

    def finish(self, turns=None):
        turn = 0
        while (self.waiting or self.flying) and turn != turns:
            turn += 1
            self.depart()
            for flight in self.flying:
                flight[2] -= 1
            landed = [flight for flight in self.flying if turns is None or flight[2] <= 0]
            self.flying = [flight for flight in self.flying if not (turns is None or flight[2] <= 0)]
            cames = [flight[1] for flight in landed]
            if turns is not None:
                cames = lax.optimization_barrier(cames)
            for flight, came in zip(landed, cames):
                self.advance(flight[0], came)


def bit_groups(mesh):
    inner = int(math.log2(mesh.shape["fsdp"]))
    outer = int(math.log2(mesh.shape["dp"]))
    rest = [list(range(b, min(b + 2, inner))) for b in range(1, inner, 2)]
    return [0], list(range(inner, inner + outer)), rest


def position(me, bits):
    spot = 0
    for place, bit in enumerate(bits):
        spot = spot + ((me >> bit) & 1) * (1 << place)
    return spot


def partners(count, bits):
    swaps = []
    for step in range(1, 1 << len(bits)):
        mask = 0
        for place, bit in enumerate(bits):
            if (step >> place) & 1:
                mask |= 1 << bit
        swaps.append((step, [(i, i ^ mask) for i in range(count)]))
    return swaps


def gather_steps(shard, mesh, groups):
    count = mesh.size
    me = lax.axis_index(AXES)
    bits = int(math.log2(count))
    rows, columns = shard.shape
    held = shard.reshape((1,) * bits + (rows, columns))
    for group in groups:
        swaps = partners(count, group)
        came = yield [(held, pairs) for _, pairs in swaps]
        shape = list(held.shape)
        for bit in group:
            shape[bits - 1 - bit] = 2
        whole = jnp.zeros(shape, shard.dtype)
        for (step, _), got in zip([(0, None)] + swaps, [held] + came):
            start = [0] * len(shape)
            for place, bit in enumerate(group):
                start[bits - 1 - bit] = ((me >> bit) & 1) ^ ((step >> place) & 1)
            whole = lax.dynamic_update_slice(whole, got, start)
        held = whole
    return held.reshape(count * rows, columns)


def pick(array, axis, index):
    return lax.dynamic_slice_in_dim(array, index, 1, axis)


def total(terms, axis, index, kind):
    return sum(pick(term, axis, index).astype(f32) for term in terms).astype(kind)


def sum_steps(parts, mesh, kind):
    count = mesh.size
    core, outer, rest = bit_groups(mesh)
    me = lax.axis_index(AXES)
    rows, columns = parts.shape[0] // count, parts.shape[1]
    rest_size = mesh.shape["fsdp"] // 2
    held = parts.reshape(mesh.shape["dp"], rest_size, 2, rows, columns)
    spot = position(me, core)
    (got,) = yield [(pick(held, 2, spot ^ 1).astype(kind), partners(count, core)[0][1])]
    terms = [pick(held, 2, spot), got]
    split = 2 if len(outer) == 2 and columns % 256 == 0 else 1
    width = columns // split
    shape = (2,) * len(outer) + (rest_size, 1, rows, width)
    pieces = []
    for piece in range(split):
        own = [term[..., piece * width : (piece + 1) * width].reshape(shape) for term in terms]
        order = list(range(len(outer)))
        pieces.append((own, order if piece == 0 else order[::-1]))
    for turn in range(len(outer)):
        sends = []
        for own, order in pieces:
            axis = order[turn]
            bit = outer[len(outer) - 1 - axis]
            mine = position(me, [bit])
            sends.append((total(own, axis, mine ^ 1, kind), partners(count, [bit])[0][1]))
        came = yield sends
        pieces = [
            ([pick(term, order[turn], position(me, [outer[len(outer) - 1 - order[turn]]])) for term in own] + [got], order)
            for (own, order), got in zip(pieces, came)
        ]
    left = rest_size
    pieces = [[term.reshape(rest_size, rows, width) for term in own] for own, _ in pieces]
    for bits in reversed(rest):
        size = 1 << len(bits)
        left //= size
        pieces = [[term.reshape(size, left, rows, width) for term in own] for own in pieces]
        spot = position(me, bits)
        swaps = partners(count, bits)
        sends = [
            (jnp.concatenate([total(own, 0, spot ^ step, kind) for own in pieces], -1), pairs)
            for step, pairs in swaps
        ]
        came = yield sends
        pieces = [
            [pick(term, 0, spot) for term in own]
            + [got[..., place * width : (place + 1) * width] for got in came]
            for place, own in enumerate(pieces)
        ]
    sums = [sum(term.astype(f32) for term in own).reshape(rows, width) for own in pieces]
    return jnp.concatenate(sums, -1)


def send_sum_kernel(where, *refs, sizes):
    at = 0
    for size, out in zip(sizes, refs[sum(sizes) :]):
        out[...] = sum(term[...].astype(f32) for term in refs[at : at + size]).astype(out.dtype)
        at += size


def fold_first(where, keep, came):
    _, _, left, rows, columns = keep.shape
    cut = columns // 2
    spec_a = pl.BlockSpec((None, 2, 2, rows, cut), lambda j, where: ((where[1] // 2) ^ 1, 0, j, 0, 0))
    spec_b = pl.BlockSpec((2, None, 2, rows, cut), lambda j, where: (0, (where[1] % 2) ^ 1, j, 0, 1))
    return pl.pallas_call(
        functools.partial(send_sum_kernel, sizes=[2, 2]),
        grid_spec=pltpu.PrefetchScalarGridSpec(
            num_scalar_prefetch=1,
            grid=(left // 2,),
            in_specs=[spec_a, spec_a, spec_b, spec_b],
            out_specs=[pl.BlockSpec((2, 2, rows, cut), lambda j, where: (0, j, 0, 0))] * 2,
        ),
        out_shape=[shape_of((2, left, rows, cut), bf16)] * 2,
        compiler_params=params(1),
        cost_estimate=cost(),
        name="fold_first",
    )(where, keep, came, keep, came)


def fold_second(where, keep, came, came_a, came_b):
    _, _, left, rows, columns = keep.shape
    cut = columns // 2
    spec_a = pl.BlockSpec(
        (None, None, 2, rows, cut), lambda j, where: (where[1] // 2, (where[1] % 2) ^ 1, j, 0, 0)
    )
    spec_b = pl.BlockSpec(
        (None, None, 2, rows, cut), lambda j, where: ((where[1] // 2) ^ 1, where[1] % 2, j, 0, 1)
    )
    half_a = pl.BlockSpec((None, 2, rows, cut), lambda j, where: ((where[1] % 2) ^ 1, j, 0, 0))
    half_b = pl.BlockSpec((None, 2, rows, cut), lambda j, where: ((where[1] // 2) ^ 1, j, 0, 0))
    return pl.pallas_call(
        functools.partial(send_sum_kernel, sizes=[3, 3]),
        grid_spec=pltpu.PrefetchScalarGridSpec(
            num_scalar_prefetch=1,
            grid=(left // 2,),
            in_specs=[spec_a, spec_a, half_a, spec_b, spec_b, half_b],
            out_specs=[pl.BlockSpec((2, rows, cut), lambda j, where: (j, 0, 0))] * 2,
        ),
        out_shape=[shape_of((left, rows, cut), bf16)] * 2,
        compiler_params=params(1),
        cost_estimate=cost(),
        name="fold_second",
    )(where, keep, came, came_a, keep, came, came_b)


def line_first_kernel(where, *refs):
    *terms, keep, send = refs
    fast = where[2] % 2
    cut = terms[0].shape[-1]
    for place, out in ((fast, keep), (fast ^ 1, send)):
        for half in range(2):
            own = terms[4 * half : 4 * half + 4]
            lanes = slice(half * cut, (half + 1) * cut)
            out[:, lanes] = sum(term[place].astype(f32) for term in own).astype(out.dtype)


def line_first(where, keep, came, came_a, came_b, last_a, last_b):
    _, _, size, rows, columns = keep.shape
    cut = columns // 2
    whole = lambda half: pl.BlockSpec(
        (None, None, 2, rows, cut), lambda j, where: (where[1] // 2, where[1] % 2, j, 0, half)
    )
    half_a = pl.BlockSpec((None, 2, rows, cut), lambda j, where: (where[1] % 2, j, 0, 0))
    half_b = pl.BlockSpec((None, 2, rows, cut), lambda j, where: (where[1] // 2, j, 0, 0))
    last = pl.BlockSpec((2, rows, cut), lambda j, where: (j, 0, 0))
    return pl.pallas_call(
        line_first_kernel,
        grid_spec=pltpu.PrefetchScalarGridSpec(
            num_scalar_prefetch=1,
            grid=(size // 2,),
            in_specs=[whole(0), whole(0), half_a, last, whole(1), whole(1), half_b, last],
            out_specs=[pl.BlockSpec((None, rows, columns), lambda j, where: (j, 0, 0))] * 2,
        ),
        out_shape=[shape_of((size // 2, rows, columns), bf16)] * 2,
        compiler_params=params(1),
        cost_estimate=cost(),
        name="line_first",
    )(where, keep, came, came_a, last_a, keep, came, came_b, last_b)


def swap_steps(send, mesh):
    core, _, _ = bit_groups(mesh)
    (came,) = yield [(send, partners(mesh.size, core)[0][1])]
    return came


def part_of(terms, axis, index, kind):
    total = None
    for term in terms:
        if term.shape[axis] != 1:
            term = pick(term, axis, index)
        total = term.astype(f32) if total is None else total + term.astype(f32)
    return total.astype(kind)


def plane_steps(keep, came, mesh):
    count = mesh.size
    _, outer, rest = bit_groups(mesh)
    spot = position(lax.axis_index(AXES), outer)
    size = 1 << len(outer)
    terms = [array.reshape((size, 1 << len(rest[0])) + keep.shape[1:]) for array in (keep, came)]
    sends = [part_of(terms, 0, spot ^ step, bf16)[0] for step in range(1, size)]
    came = yield [(array, pairs) for array, (_, pairs) in zip(sends, partners(count, outer))]
    return [pick(term, 0, spot)[0] for term in terms] + came


def line_steps(terms, mesh):
    count = mesh.size
    _, _, rest = bit_groups(mesh)
    spot = position(lax.axis_index(AXES), rest[0])
    came = yield [
        (part_of(terms, 0, spot ^ step, bf16)[0], pairs) for step, pairs in partners(count, rest[0])
    ]
    return part_of(terms, 0, spot, f32)[0] + sum(array.astype(f32) for array in came)


def line_fold_steps(terms, mesh):
    count = mesh.size
    _, _, rest = bit_groups(mesh)
    me = lax.axis_index(AXES)
    terms = [term.reshape((2, 2) + term.shape[1:]) for term in terms]
    for axis, bit in ((1, rest[0][0]), (0, rest[0][1])):
        spot = position(me, [bit])
        came = yield [(part_of(terms, axis, spot ^ 1, bf16), partners(count, [bit])[0][1])]
        terms = [pick(term, axis, spot) for term in terms] + came
    return sum(term.astype(f32) for term in terms)[0, 0]


def fold_sum_steps(keep, send, where, mesh):
    count = mesh.size
    core, outer, rest = bit_groups(mesh)
    (came,) = yield [(send, partners(count, core)[0][1])]
    shape = (2, 2, 1 << len(rest[0]), keep.shape[0] * 2 // count, keep.shape[1])
    keep, came = keep.reshape(shape), came.reshape(shape)
    fast, slow = (partners(count, [bit])[0][1] for bit in outer)
    send_a, send_b = fold_first(where, keep, came)
    came_a, came_b = yield [(send_a, slow), (send_b, fast)]
    send_a, send_b = fold_second(where, keep, came, came_a, came_b)
    last_a, last_b = yield [(send_a, fast), (send_b, slow)]
    keep, send = line_first(where, keep, came, came_a, came_b, last_a, last_b)
    (came,) = yield [(send, partners(count, [rest[0][0]])[0][1])]
    me = lax.axis_index(AXES)
    spot = position(me, [rest[0][1]])
    both = [keep, came]
    (last,) = yield [(total(both, 0, spot ^ 1, bf16), partners(count, [rest[0][1]])[0][1])]
    done = (total(both, 0, spot, f32) + last.astype(f32)).reshape(2, shape[3] // 2, shape[4])
    spot = position(me, core)
    (came,) = yield [(pick(done, 0, spot ^ 1), partners(count, core)[0][1])]
    own, came = pick(done, 0, spot)[0], came[0]
    return jnp.where(spot == 0, own, came), jnp.where(spot == 0, came, own)


def small_sum_steps(parts, mesh):
    count = mesh.size
    core, outer, rest = bit_groups(mesh)
    groups = [core, outer, *reversed(rest)]
    order = [outer, *reversed(rest), core]
    me = lax.axis_index(AXES)
    columns = parts.shape[1]
    held = parts.reshape([1 << len(bits) for bits in order] + [columns])
    for bits in groups:
        axis = order.index(bits)
        spot = position(me, bits)
        swaps = partners(count, bits)
        came = yield [(pick(held, axis, spot ^ step), pairs) for step, pairs in swaps]
        held = pick(held, axis, spot) + sum(came)
    return held.reshape(columns)


def cut_by_core(mesh):
    _, outer, rest = bit_groups(mesh)
    return len(outer) == 2 and len(rest) == 1 and len(rest[0]) == 2


def store_cut(core, outs, lanes, value, rows):
    if len(outs) == 1:
        outs[0][:, lanes] = value.astype(bf16)
        return
    keep, send = outs
    for parity in range(2):
        @pl.when(core == parity)
        def _():
            for device in range(value.shape[0] // rows):
                out = keep if device % 2 == parity else send
                out[device // 2, :, lanes] = value[device * rows : (device + 1) * rows, :].astype(bf16)


def cut_shapes(width, columns, chunk, index, rows):
    if not rows:
        spec = pl.BlockSpec((width, chunk), lambda j, *_: (0, index(j)))
        return [spec], [shape_of((width, columns), bf16)]
    blocks = width // rows // 2
    spec = pl.BlockSpec((blocks, rows, chunk), lambda j, *_: (0, 0, index(j)))
    return [spec] * 2, [shape_of((blocks, rows, columns), bf16)] * 2


def normalize(values):
    center = values - jnp.mean(values, -1, keepdims=True)
    scale = lax.rsqrt(jnp.mean(center * center, -1, keepdims=True) + 1e-05)
    return center * scale, scale


def norm_back(grad, gain, unit, scale):
    inner = grad * gain
    return scale * (
        inner
        - jnp.mean(inner, -1, keepdims=True)
        - unit * jnp.mean(inner * unit, -1, keepdims=True)
    )


def gelu_parts(u):
    phi = 0.5 + 0.5 * lax.erf(u * 0.7071067811865476)
    slope = phi + u * (0.3989422804014327 * jnp.exp2((u * u) * (-0.5 * LOG2E)))
    return u * phi, slope


def column_sum(values):
    return jnp.sum(values, 0, keepdims=True)


def accumulate(ref, value, first):
    @pl.when(first)
    def _():
        ref[...] = value

    @pl.when(jnp.logical_not(first))
    def _():
        ref[...] += value


def two_heads(block, padded):
    seq = block.shape[0]
    first = lax.broadcasted_iota(jnp.int32, block.shape, 1) < 64
    zero = jnp.zeros_like(block)
    pad = jnp.zeros((padded - seq, 128), block.dtype)
    return jnp.concatenate(
        [jnp.where(first, block, zero), pad, jnp.where(first, zero, block), pad], 0
    )


def attend_kernel(valid, *refs, tile, padded, first, pairs):
    if first:
        tokens, gain, shift, weight, bias, normed, joined, mixed, raised_out, inverse = refs
    else:
        (
            normed, weight, bias, tokens, mixed_first, bias_out, gain, shift,
            joined, mixed, raised_out, inverse, middle, normed_two,
        ) = refs
    seq, span = joined.shape
    for start in range(0, seq, tile):
        rows = slice(start, start + tile)
        if first:
            unit, _ = normalize(tokens[rows, :].astype(f32))
            low = (unit * gain[...] + shift[...]).astype(bf16)
            normed[rows, :] = low
        else:
            low = normed[rows, :]
        joined[rows, :] = (dot(low, weight[:, :span], NN) + bias[...]).astype(bf16)

    column = lax.broadcasted_iota(jnp.int32, (1, padded), 1)
    mask = jnp.where(column < valid[pl.program_id(0)], 0.0, -1e30).astype(f32)
    places = [(pair, start) for pair in range(pairs) for start in range(0, seq, ATILE)]
    keys, values = {}, {}
    row = lax.broadcasted_iota(jnp.int32, (2 * padded, 128), 0)
    lane = lax.broadcasted_iota(jnp.int32, (2 * padded, 128), 1)
    ones = jnp.where((row < padded) == (lane < 64), 1.0, 0.0).astype(bf16)

    def scores_at(pair, start):
        if pair not in keys:
            at = pair * 384
            keys[pair] = two_heads(joined[:, at + 128 : at + 256], padded)
            values[pair] = jnp.concatenate([two_heads(joined[:, at + 256 : at + 384], padded), ones], 1)
        return dot(joined[start : start + ATILE, pair * 384 : pair * 384 + 128], keys[pair], NT)

    ahead = [scores_at(*place) for place in places[:AHEAD]]
    for index, (pair, start) in enumerate(places):
        rows = slice(start, start + ATILE)
        if index + AHEAD < len(places):
            ahead.append(scores_at(*places[index + AHEAD]))
        scores = ahead.pop(0)
        halves = []
        for head in range(2):
            part = scores[:, head * padded : (head + 1) * padded] * (0.125 * LOG2E) + mask
            halves.append(jnp.exp2(part - jnp.max(part, 1, keepdims=True)).astype(bf16))
        raised = jnp.concatenate(halves, 1)
        raised_out[pair, rows, :] = raised
        both = dot(raised, values[pair], NN)
        scale = 1.0 / both[:, 128:]
        inverse[rows, pair * 128 : (pair + 1) * 128] = scale
        mixed[rows, pair * 128 : (pair + 1) * 128] = (both[:, :128] * scale).astype(bf16)
    if first:
        return
    width = tokens.shape[1]
    for start in range(0, seq, tile):
        rows = slice(start, start + tile)
        value = tokens[rows, :].astype(f32) + bias_out[...]
        value = value + dot(mixed_first[rows, :], weight[: width // 2, -width:], NN)
        value = value + dot(mixed[rows, :], weight[width // 2 :, -width:], NN)
        middle[rows, :] = value
        unit, _ = normalize(value)
        normed_two[rows, :] = (unit * gain[...] + shift[...]).astype(bf16)


def attend(start, valid, weight, bias, seq, norm=None, after=None):
    rows, width = start.shape
    span = bias.shape[1]
    pairs = span // 384
    items = rows // seq
    padded = -(-seq // 128) * 128
    row = lambda w: pl.BlockSpec((seq, w), lambda i, *_: (i, 0))
    one = once((1, width))
    main = [once(weight.shape), once((1, span))]
    if norm:
        specs, arrays = [row(width), one, one, *main], [start, *norm, weight, bias]
    else:
        specs = [row(width), *main, row(width), row(width // 2), one, one, one]
        arrays = [start, weight, bias, *after]
    outs = [
        row(span),
        row(span // 3),
        pl.BlockSpec((None, pairs, seq, 2 * padded), lambda i, *_: (i, 0, 0, 0)),
        row(span // 3),
    ]
    shapes = [
        shape_of((rows, span), bf16),
        shape_of((rows, span // 3), bf16),
        shape_of((items, pairs, seq, 2 * padded), bf16),
        shape_of((rows, span // 3), f32),
    ]
    if norm:
        outs, shapes = [row(width)] + outs, [shape_of((rows, width), bf16)] + shapes
    else:
        outs += [row(width)] * 2
        shapes += [shape_of((rows, width), f32), shape_of((rows, width), bf16)]
    return pl.pallas_call(
        functools.partial(attend_kernel, tile=tile_of(seq), padded=padded, first=bool(norm), pairs=pairs),
        grid_spec=pltpu.PrefetchScalarGridSpec(
            num_scalar_prefetch=1, grid=(items,), in_specs=specs, out_specs=outs
        ),
        out_shape=shapes,
        compiler_params=params(1),
        cost_estimate=cost(),
        name="attend",
    )(valid, *arrays)


def attend_back_kernel(where, *refs, pairs, extra, spare, cut):
    lists = [refs[kind * pairs : (kind + 1) * pairs] for kind in range(5)]
    joined, mixed_grad, mixed, raised, inverse = lists
    normed, weight, *rest = refs[5 * pairs :]
    if extra:
        mixed_a, mixed_b, low_grad, *rest, total_out = rest
    joined_grad, column, gain_sum, shift_sum, *outs, held, scaled, total = rest
    item = pl.program_id(0)
    seq, span = joined_grad.shape
    padded = raised[0].shape[1] // 2
    tile = BTILE if seq % BTILE == 0 else seq
    first = lax.broadcasted_iota(jnp.int32, (tile, 128), 1) < 64
    places = [(pair, start) for pair in range(pairs) for start in range(0, seq, tile)]
    keys, values = {}, {}

    def prob_grad_at(pair, start):
        if pair not in keys:
            keys[pair] = two_heads(joined[pair][:, 128:256], padded)
            values[pair] = two_heads(joined[pair][:, 256:], padded)
        rows = slice(start, start + tile)
        grad = (mixed_grad[pair][rows, :].astype(f32) * inverse[pair][rows, :]).astype(bf16)
        scaled[pair, rows, :] = grad
        return grad, dot(grad, values[pair], NT)

    def own_half(both):
        return jnp.concatenate([both[:64, :padded], both[64:, padded:]], 0).T[:seq]

    ahead = [prob_grad_at(*place) for place in places[:BAHEAD]]
    for index, (pair, start) in enumerate(places):
        rows = slice(start, start + tile)
        at = pair * 384
        if index + BAHEAD < len(places):
            ahead.append(prob_grad_at(*places[index + BAHEAD]))
        grad, prob_grad = ahead.pop(0)
        product = grad.astype(f32) * mixed[pair][rows, :].astype(f32)
        zero = jnp.zeros_like(product)
        halves = []
        for head in range(2):
            own = jnp.where(first, product, zero) if head == 0 else jnp.where(first, zero, product)
            centre = jnp.sum(own, 1, keepdims=True)
            half = slice(head * padded, (head + 1) * padded)
            halves.append((raised[pair][rows, half].astype(f32) * (prob_grad[:, half] - centre)).astype(bf16))
        score_grad = jnp.concatenate(halves, 1)
        held[rows, :] = score_grad
        joined_grad[rows, at : at + 128] = (dot(score_grad, keys[pair], NN) * 0.125).astype(bf16)
        if start + tile == seq:
            joined_grad[:, at + 128 : at + 256] = (
                own_half(dot(joined[pair][:, :128].T, held[...], NN)) * 0.125
            ).astype(bf16)
            joined_grad[:, at + 256 : at + 384] = own_half(
                dot(scaled[pair].T, raised[pair][...], NN)
            ).astype(bf16)

    value = joined_grad[...]
    accumulate(total, dot(normed[...], value, TN), item == 0)
    accumulate(column, column_sum(value.astype(f32)), item == 0)
    if extra:
        both = [dot(mixed_a[...], low_grad[...], TN), dot(mixed_b[...], low_grad[...], TN)]
        accumulate(total_out, jnp.concatenate(both, 0), item == 0)

    @pl.when(item == pl.num_programs(0) - 1)
    def _():
        store_cut(where[0], outs, slice(0, span), total[...], cut)
        if spare:
            for out in outs:
                out[..., span:] = jnp.zeros(out.shape[:-1] + (spare,), bf16)
        wide = weight[...].astype(f32)
        for ref, product in ((gain_sum, wide * total[...]), (shift_sum, wide * column[...])):
            row = jnp.sum(product, 1, keepdims=True)
            ref[...] = jnp.broadcast_to(row, (row.shape[0], 128)).T[:1]
        if extra:
            store_cut(where[0], outs, slice(span, span + total_out.shape[1]), total_out[...], cut)


def attend_back(mixed_grad, where, joined, mixed, raised, inverse, normed, weight, seq, part, cut, others=(), spare=0):
    rows, width = normed.shape
    items, in_part, _, keys = raised.shape
    pairs = in_part
    chosen = range(pairs)
    span = 384 * pairs
    row = lambda w, off=0: pl.BlockSpec((seq, w), lambda i, *_: (i, off))
    each = lambda w, off=0: [row(w, off + pair) for pair in chosen]
    weights = [
        pl.BlockSpec((None, None, seq, keys), functools.partial(lambda at, i, *_: (i, at, 0, 0), pair))
        for pair in chosen
    ]
    columns = span + (width if others else 0) + spare
    one = pl.BlockSpec((1, width), lambda i, *_: (0, 0))
    specs, shapes = cut_shapes(width, columns, columns, lambda j: 0, cut)
    return pl.pallas_call(
        functools.partial(
            attend_back_kernel, pairs=pairs, extra=bool(others), spare=spare, cut=cut
        ),
        grid_spec=pltpu.PrefetchScalarGridSpec(
            num_scalar_prefetch=1,
            grid=(items,),
            in_specs=[
                *each(384), *each(128, part * in_part), *each(128), *weights, *each(128), row(width)
            ]
            + [once((width, span))]
            + [row(array.shape[1]) for array in others],
            out_specs=[row(span), pl.BlockSpec((1, span), lambda i, *_: (0, 0)), one, one] + specs,
            scratch_shapes=[
                pltpu.VMEM((seq, keys), bf16),
                pltpu.VMEM((pairs, seq, 128), bf16),
                pltpu.VMEM((width, span), f32),
            ]
            + ([pltpu.VMEM((width, width), f32)] if others else []),
        ),
        out_shape=[shape_of((rows, span), bf16), shape_of((1, span), f32)]
        + [shape_of((1, width), f32)] * 2
        + shapes,
        compiler_params=params(1),
        cost_estimate=cost(),
        name="attend_back",
    )(
        where, *[joined] * pairs, *[mixed_grad] * pairs, *[mixed] * pairs, *[raised] * pairs,
        *[inverse] * pairs, normed, weight, *others,
    )


def mlp_kernel(
    valid, where, normed, cotangent, up, down, bias_up,
    active, hidden_grad, up_sum, *rest, seq, tile, cut,
):
    *outs, grad = rest
    rows, width = normed.shape

    @pl.when(pl.program_id(0) == 0)
    def _():
        place = lax.broadcasted_iota(jnp.int32, (seq, 1), 0)
        for item in range(rows // seq):
            span = slice(item * seq, (item + 1) * seq)
            grad[span, :] = jnp.where(place < valid[item], cotangent[span, :].astype(f32), 0.0).astype(bf16)

    def ahead_of(start):
        span = slice(start, start + MTILE)
        return dot(normed[span, :], up[...], NN), dot(grad[span, :], down[...], NT)

    column = jnp.zeros(up_sum.shape, f32)
    starts = list(range(0, rows, MTILE))
    ahead = [ahead_of(start) for start in starts[:MAHEAD]]
    for index, start in enumerate(starts):
        span = slice(start, start + MTILE)
        if index + MAHEAD < len(starts):
            ahead.append(ahead_of(starts[index + MAHEAD]))
        hidden, wide = ahead.pop(0)
        value, slope = gelu_parts(hidden + bias_up[...])
        low = (slope * wide).astype(bf16)
        active[span, :] = value.astype(bf16)
        hidden_grad[span, :] = low
        column = column + column_sum(low.astype(f32))
    up_sum[...] = column
    first = dot(normed[...], hidden_grad[...], TN).astype(bf16)
    second = dot(active[...], grad[...], TN).astype(bf16)
    if cut:
        keep, send = outs
        for core in range(2):
            @pl.when(where[0] == core)
            def _():
                (keep, send)[core][...] = first
                (send, keep)[core][...] = second
    else:
        outs[0][:, :width] = first
        outs[0][:, width:] = second


def mlp(normed, valid, where, cotangent, both, bias_up, seq, cut):
    rows, width = normed.shape
    wide = both.shape[1] // 2
    chunks = wide // width
    whole = once((rows, width))
    square = lambda off: pl.BlockSpec((width, width), lambda j, *_: (0, j + off))
    row = pl.BlockSpec((rows, width), lambda j, *_: (0, j))
    one = pl.BlockSpec((1, width), lambda j, *_: (0, j))
    if cut:
        specs = [pl.BlockSpec((width, width), lambda j, *_: (0, j))] * 2
        shapes = [shape_of((width, wide), bf16)] * 2
    else:
        specs, shapes = cut_shapes(width, 2 * wide, 2 * width, lambda j: j, 0)
    return pl.pallas_call(
        functools.partial(mlp_kernel, seq=seq, tile=tile_of(seq), cut=cut),
        grid_spec=pltpu.PrefetchScalarGridSpec(
            num_scalar_prefetch=2,
            grid=(chunks,),
            in_specs=[whole, whole, square(0), square(chunks), one],
            out_specs=[row, row, one] + specs,
            scratch_shapes=[pltpu.VMEM((rows, width), bf16)],
        ),
        out_shape=[
            shape_of((rows, width * chunks), bf16),
            shape_of((rows, width * chunks), bf16),
            shape_of((1, width * chunks), f32),
        ]
        + shapes,
        compiler_params=params(1),
        cost_estimate=cost(),
        name="mlp",
    )(valid, where, normed, cotangent, both, both, bias_up)


def block_out_kernel(valid, active, downs, middle, bias_down, *rest, seq, begin):
    block_out = rest[-1]
    tile, width = middle.shape
    step = pl.program_id(0) + begin // tile
    place = lax.broadcasted_iota(jnp.int32, (tile, 1), 0) + lax.rem(step, seq // tile) * tile
    value = middle[...] + bias_down[...]
    for at in range(0, downs.shape[1], width):
        value = value + dot(active[:, at : at + width], downs[:, at : at + width], NN)
    block_out[...] = jnp.where(place < valid[step // (seq // tile)], value, 0.0).astype(bf16)


def half_of(both, second):
    width, columns = both.shape
    return pl.BlockSpec(
        (width, columns // 2), lambda j, *_: (0, second), pipeline_mode=pl.Buffered(buffer_count=1)
    )


def block_out_of(middle, valid, active, both, bias_down, seq, begin, end, before=None):
    rows, width = middle.shape
    tile = BOT if seq % BOT == 0 else seq
    skip = begin // tile
    row = lambda w: pl.BlockSpec((tile, w), lambda j, *_: (j + skip, 0))
    specs = [row(active.shape[1]), half_of(both, 1), row(width), once((1, width))]
    arrays = [active, both, middle, bias_down]
    aliases = {}
    if before is not None:
        aliases = {len(arrays) + 1: 0}
        specs.append(pl.BlockSpec(memory_space=pl.ANY))
        arrays.append(before)
    return pl.pallas_call(
        functools.partial(block_out_kernel, seq=seq, begin=begin),
        grid_spec=pltpu.PrefetchScalarGridSpec(
            num_scalar_prefetch=1,
            grid=((end - begin) // tile,),
            in_specs=specs,
            out_specs=row(width),
        ),
        out_shape=shape_of((rows, width), bf16),
        input_output_aliases=aliases,
        compiler_params=params(1),
        cost_estimate=cost(),
        name="block_out",
    )(valid, *arrays)


def middle_back_kernel(
    valid, hidden_grad, ups, middle, cotangent, gain, weight_a, weight_b,
    low_grad, mixed_grad, gain_sum, shift_sum, bias_sum, down_sum, *, seq, sub,
):
    step = pl.program_id(0)
    tile, width = middle.shape
    each = seq // tile
    starts = list(range(0, tile, sub))
    ahead = [dot(hidden_grad[:sub, :], ups[...], NT)]
    sums = [jnp.zeros((1, width), f32)] * 4
    for index, start in enumerate(starts):
        rows = slice(start, start + sub)
        if index + 1 < len(starts):
            ahead.append(dot(hidden_grad[start + sub : start + 2 * sub, :], ups[...], NT))
        grad = ahead.pop(0)
        unit, scale = normalize(middle[rows, :])
        place = lax.broadcasted_iota(jnp.int32, (sub, 1), 0) + (lax.rem(step, each) * tile + start)
        kept = jnp.where(place < valid[step // each], cotangent[rows, :].astype(f32), 0.0)
        low = (kept + norm_back(grad, gain[...], unit, scale)).astype(bf16)
        low_grad[rows, :] = low
        mixed_grad[rows, :] = (
            dot(low[:, : width // 2], weight_a[...], NT) + dot(low[:, width // 2 :], weight_b[...], NT)
        ).astype(bf16)
        terms = (grad * unit, grad, low.astype(f32), kept)
        sums = [before + column_sum(term) for before, term in zip(sums, terms)]
    for ref, value in zip((gain_sum, shift_sum, bias_sum, down_sum), sums):
        accumulate(ref, value, step == 0)


def middle_back(middle, valid, hidden_grad, both, cotangent, gain, weight, seq):
    rows, width = middle.shape
    tile = LTILE if seq % LTILE == 0 else seq
    sub = LSUB if tile % LSUB == 0 else tile
    row = lambda w: pl.BlockSpec((tile, w), lambda j, *_: (j, 0))
    one = pl.BlockSpec((1, width), lambda j, *_: (0, 0))
    half = width // 2
    at = weight.shape[1] // half - 2
    halves = [
        pl.BlockSpec((width, half), lambda j, *_: (0, at), pipeline_mode=pl.Buffered(buffer_count=1)),
        pl.BlockSpec((width, half), lambda j, *_: (0, at + 1), pipeline_mode=pl.Buffered(buffer_count=1)),
    ]
    return pl.pallas_call(
        functools.partial(middle_back_kernel, seq=seq, sub=sub),
        grid_spec=pltpu.PrefetchScalarGridSpec(
            num_scalar_prefetch=1,
            grid=(rows // tile,),
            in_specs=[
                row(hidden_grad.shape[1]), half_of(both, 0), row(width), row(width),
                once((1, width)), *halves,
            ],
            out_specs=[row(width), row(width)] + [one] * 4,
        ),
        out_shape=[shape_of((rows, width), bf16)] * 2 + [shape_of((1, width), f32)] * 4,
        compiler_params=params(1),
        cost_estimate=cost(),
        name="middle_back",
    )(valid, hidden_grad, both, middle, cotangent, gain, weight, weight)


def input_back_kernel(*refs, spans, sub):
    grads = refs[: len(spans)]
    weights = refs[len(spans) : len(spans) + 2]
    tokens, low_grad, gain, input_grad = refs[len(spans) + 2 :]
    tile, width = tokens.shape

    def ahead_of(start):
        rows = slice(start, start + sub)
        terms = [
            dot(grad[rows, :], weights[which][:, lanes], NT) for grad, (which, lanes) in zip(grads, spans)
        ]
        return sum(terms[1:], terms[0])

    starts = list(range(0, tile, sub))
    ahead = [ahead_of(0)]
    for index, start in enumerate(starts):
        rows = slice(start, start + sub)
        if index + 1 < len(starts):
            ahead.append(ahead_of(start + sub))
        grad = ahead.pop(0)
        unit, scale = normalize(tokens[rows, :].astype(f32))
        full = low_grad[rows, :].astype(f32) + norm_back(grad, gain[...], unit, scale)
        input_grad[rows, :] = full.astype(bf16)


def input_back(last, others, spans, weights, tokens, low_grad, gain, seq):
    rows, width = tokens.shape
    tile = LTILE if seq % LTILE == 0 else seq
    sub = LSUB if tile % LSUB == 0 else tile
    row = lambda w: pl.BlockSpec((tile, w), lambda i: (i, 0))
    grads = [*others, last]
    return pl.pallas_call(
        functools.partial(input_back_kernel, spans=spans, sub=sub),
        grid=(rows // tile,),
        in_specs=[row(grad.shape[1]) for grad in grads]
        + [once((width, spans[0][1].stop))] * 2
        + [row(width), row(width), once((1, width))],
        out_specs=row(width),
        out_shape=shape_of((rows, width), bf16),
        compiler_params=params(1),
        cost_estimate=cost(),
        name="input_back",
    )(*grads, *weights, tokens, low_grad, gain)


def local(mesh, tokens, cotangent, group, text_len, qkv_w, out_w, mlp_in, mlp_out, gains, biases):
    items, seq, width = tokens.shape
    rows = items * seq
    count = mesh.size
    share = width // count
    wide = mlp_in.shape[0] // share
    chunks = wide // width
    half = width // 2
    span = 3 * half
    valid = (PATCH_SMALL + (PATCH_LARGE - PATCH_SMALL) * group + text_len).astype(jnp.int32)
    flat = tokens.reshape(rows, width)
    cot = cotangent.reshape(rows, width)
    flights = Flights()
    me = lax.axis_index(AXES)
    core, outer, others = bit_groups(mesh)
    where = jnp.stack([position(me, core), position(me, outer), position(me, others[0])]).astype(jnp.int32)
    cut = share if cut_by_core(mesh) and share % 8 == 0 else 0

    def mlp_sums(arrays):
        if cut:
            return flights.add(fold_sum_steps(*arrays, where, mesh), [])
        return flights.add(sum_steps(arrays[0], mesh, bf16), [])

    def swap(arrays):
        return flights.add(swap_steps(arrays[1], mesh), []) if cut else None

    def by_pairs(matrix, part):
        rows = matrix.shape[0]
        cubes = matrix.reshape(rows, 3, 2, half // 128, 128)[:, :, part]
        return cubes.transpose(0, 2, 1, 3).reshape(rows, span)

    def by_kind(part_a, part_b):
        rows = part_a.shape[0]
        cubes = [piece[:, :span].reshape(rows, half // 128, 3, 128) for piece in (part_a, part_b)]
        return jnp.stack(cubes, 1).transpose(0, 3, 1, 2, 4).reshape(rows, 3 * width)

    own_up = mlp_in.reshape(share, count, chunks, share).transpose(0, 2, 1, 3).reshape(share, wide)
    own_down = mlp_out.reshape(chunks, share, width).transpose(1, 0, 2).reshape(share, wide)
    own_both = jnp.concatenate([own_up, own_down], 1)

    own_qkv = qkv_w.reshape(share, 3 * width)
    small = jnp.concatenate([gains, biases])
    small_rows = -(-small.shape[0] // 128)
    padded = jnp.pad(small, (0, small_rows * 128 - small.shape[0])).reshape(small_rows, 128)
    padded = jnp.pad(padded, ((0, share - small_rows), (0, 0)))
    both = lax.all_gather(own_both, AXES, axis=0, tiled=True)
    own_first = jnp.concatenate([by_pairs(own_qkv, 0), padded], 1)
    own_second = jnp.concatenate([by_pairs(own_qkv, 1), out_w.reshape(share, width)], 1)
    singles = [[bit] for group in reversed(others) for bit in reversed(group)]
    job = flights.add(gather_steps(own_first, mesh, [*others, outer, core]), [])
    second_job = flights.add(gather_steps(own_second, mesh, [*singles, outer, core]), [1] * len(singles) + [2])
    flights.finish(len(others) + 2)
    first = job["result"]
    small = first[:, span:].reshape(count, share, 128)[:, :small_rows]
    small = small.reshape(count, small_rows * 128).astype(f32)
    edge = gains.shape[0]
    gain = small[:, :edge].reshape(1, 2 * width)
    bias = small[:, edge : edge + biases.shape[0]].reshape(1, 6 * width + wide)
    gain_one, gain_two = gain[:, :width], gain[:, width:]
    bias_query, bias_value, bias_output, shift_one, shift_two, bias_down = (
        bias[:, p * width : (p + 1) * width] for p in range(6)
    )
    bias_up = bias[:, 6 * width :].reshape(count, chunks, share).transpose(1, 0, 2).reshape(1, wide)
    bias_joined = jnp.concatenate([bias_query, jnp.zeros_like(bias_query), bias_value], 1)
    bias_parts = [by_pairs(bias_joined, part) for part in range(2)]

    normed, joined_a, mixed_a, raised_a, inverse_a = flights.run(
        lambda x: attend(x, valid, first, bias_parts[0], seq, (gain_one, shift_one)), flat
    )
    flights.finish()
    second = second_job["result"]
    joined_b, mixed_b, raised_b, inverse_b, middle, normed_two = attend(
        normed, valid, second, bias_parts[1], seq,
        after=(flat, mixed_a, bias_output, gain_two, shift_two),
    )

    active, hidden_grad, up_sum, *mlp_grads = mlp(
        normed_two, valid, where, cot, both, bias_up, seq, cut
    )
    mlp_job = mlp_sums(mlp_grads)

    low_grad, mixed_grad, gain_two_sum, shift_two_sum, bias_out_sum, down_sum = flights.run(
        lambda x: middle_back(x, valid, hidden_grad, both, cot, gain_two, second, seq), middle
    )
    joined_grad_a, qkv_sum_a, gain_sum_a, shift_sum_a, *grads_a = flights.run(
        lambda x: attend_back(
            x, where, joined_a, mixed_a, raised_a, inverse_a, normed, first, seq, 0, cut,
            others=(mixed_a, mixed_b, low_grad),
        ),
        mixed_grad,
    )
    swap_a = swap(grads_a)
    joined_grad_b, qkv_sum_b, gain_sum_b, shift_sum_b, *grads_b = flights.run(
        lambda x: attend_back(
            x, where, joined_b, mixed_b, raised_b, inverse_b, normed, second, seq, 1, cut,
            spare=128 if cut else 0,
        ),
        mixed_grad,
    )
    shift_one_sum = shift_sum_a + shift_sum_b
    gain_one_sum = (gain_sum_a + gain_sum_b - shift_one * shift_one_sum) / gain_one
    joined_sums = by_kind(qkv_sum_a, qkv_sum_b)
    up_sum = up_sum.reshape(chunks, count, share).transpose(1, 0, 2).reshape(1, wide)
    gain_sums = jnp.concatenate([gain_one_sum, gain_two_sum], 1).reshape(count, edge)
    bias_sums = jnp.concatenate(
        [
            joined_sums[:, :width],
            joined_sums[:, 2 * width :],
            bias_out_sum,
            shift_one_sum,
            shift_two_sum,
            down_sum,
            up_sum,
        ],
        1,
    ).reshape(count, biases.shape[0])
    small = jnp.concatenate([gain_sums, bias_sums], 1)
    if cut:
        small = jnp.pad(small, ((0, 0), (0, small_rows * 128 - small.shape[1])))
        small = small.reshape(count // 2, 2, small_rows, 128)
        spot = position(me, core)
        grads_b = [
            lax.dynamic_update_slice(grads, pick(small, 1, place)[:, 0].astype(bf16), (0, 0, span))
            for grads, place in zip(grads_b, (spot, spot ^ 1))
        ]
        swap_b = swap(grads_b)
        plane_a = flights.add(plane_steps(grads_a[0], swap_a["result"], mesh), [])
    else:
        small_job = flights.add(small_sum_steps(small, mesh), [])
        sum_a, sum_b = (flights.add(sum_steps(grads, mesh, bf16), []) for (grads,) in (grads_a, grads_b))
    spans = ((0, slice(0, span)), (1, slice(0, span)))
    input_grad = flights.run(
        lambda x: input_back(x, [joined_grad_a], spans, [first, second], flat, low_grad, gain_one, seq),
        joined_grad_b,
    )
    if cut:
        plane_b = flights.add(plane_steps(grads_b[0], swap_b["result"], mesh), [])
        line_a = flights.add(line_fold_steps(plane_a["result"], mesh), [])
    block_out = flights.run(
        lambda x: block_out_of(x, valid, active, both, bias_down, seq, 0, rows), middle
    )
    if cut:
        line_b = flights.add(line_steps(plane_b["result"], mesh), [])
        flights.land(mlp_job)
        up_total, down_total = mlp_job["result"]
    else:
        flights.finish()
        mlp_total = mlp_job["result"].reshape(share, chunks, 2, width)
        up_total, down_total = mlp_total[:, :, 0], mlp_total[:, :, 1]
    up_total = up_total.reshape(share, chunks, count, share).transpose(0, 2, 1, 3).reshape(-1)
    down_total = down_total.reshape(share, chunks, width).transpose(1, 0, 2).reshape(-1)
    up_total, down_total = flights.finish_after((up_total, down_total))
    if cut:
        total_a, total_b = line_a["result"], line_b["result"]
        small_total = total_b[:small_rows, span:].reshape(-1)
        small_total = small_total[: edge + biases.shape[0]]
    else:
        total_a, total_b = sum_a["result"], sum_b["result"]
        small_total = small_job["result"]
    return (
        block_out.reshape(tokens.shape),
        input_grad.reshape(tokens.shape),
        by_kind(total_a, total_b).reshape(-1),
        total_a[:, span:].reshape(-1),
        up_total,
        down_total,
        small_total[:edge],
        small_total[edge:],
    )


def solution(mesh):
    split = P(AXES)
    whole = P(AXES, None, None)
    return jax.shard_map(
        functools.partial(local, mesh),
        mesh=mesh,
        in_specs=(whole, whole) + (split,) * 8,
        out_specs=(whole, whole) + (split,) * 6,
        check_vma=False,
    )
```
